128 devices in a mesh: seq: 2 (over y_hi), fsdp: 64 (over y_lo, x, z, core).
Axes of the slice: x: 4, y: 4 (y_hi: 2, y_lo: 2; y = y_hi * 2 + y_lo), z: 4, core: 2. Of those that a mesh axis runs over, the one named last changes fastest.
Arguments:
- tokens: bfloat16 [64, 256, 1024], P('fsdp', 'seq'), may hold values from -6 to 6
- positions: int32 [64, 256], P('fsdp', 'seq'), may hold values from 0 to 765, as said below
- routes: int32 [64, 256, 8], P('fsdp', 'seq'), may hold values from 0 to 31, all different within a row; in each aligned block of 128 rows (0 to 127, 128 to 255, ..., all dimensions but the last counted through in order) at most 44 rows name the same one
- cotangent: bfloat16 [64, 256, 1024], P('fsdp', 'seq'), may hold values from -6 to 6
- first_gain: bfloat16 [1024], P('fsdp'), may hold values from 0.099609375 to 1.8984375
- w_query: bfloat16 [1024, 1024], P('fsdp'), may hold values from -0.1875 to 0.1875
- w_key: bfloat16 [1024, 512], P('fsdp'), may hold values from -0.1875 to 0.1875
- w_value: bfloat16 [1024, 512], P('fsdp'), may hold values from -0.1875 to 0.1875
- w_out: bfloat16 [1024, 1024], P('fsdp'), may hold values from -0.75 to 0.75
- second_gain: bfloat16 [1024], P('fsdp'), may hold values from 0.099609375 to 1.8984375
- w_router: bfloat16 [1024, 32], P('fsdp'), may hold values from -0.09375 to 0.09375
- w_gate: bfloat16 [64, 512, 512], P('fsdp'), may hold values from -0.1875 to 0.1875
- w_up: bfloat16 [64, 512, 512], P('fsdp'), may hold values from -0.1875 to 0.1875
- w_down: bfloat16 [64, 256, 1024], P('fsdp'), may hold values from -0.75 to 0.75
Outputs:
- layer_out: bfloat16 [64, 256, 1024], P('fsdp', 'seq')
- grad_tokens: float32 [64, 256, 1024], P('fsdp', 'seq')
- grad_first_gain: float32 [1024], P('fsdp')
- grad_query: float32 [1024, 1024], P('fsdp')
- grad_key: float32 [1024, 512], P('fsdp')
- grad_value: float32 [1024, 512], P('fsdp')
- grad_out: float32 [1024, 1024], P('fsdp')
- grad_second_gain: float32 [1024], P('fsdp')
- grad_router: float32 [1024, 32], P('fsdp')
- grad_gate: float32 [64, 512, 512], P('fsdp')
- grad_up: float32 [64, 512, 512], P('fsdp')
- grad_down: float32 [64, 256, 1024], P('fsdp')
The draws below stay inside these ranges and needn't reach their ends.
Inputs may be any that keep to these rules, and one draw needn't show every extreme that they name: `positions`: each sequence starts at position 0; each next token's position is 1 to 3 larger, except that the last token of every sequence stands at position 765. `routes`: A row names 8 different experts. Among the 128 rows of one device (aligned blocks of a sequence), no expert is named by more than 44 rows, a bound that some block reaches.
All inputs are finite; a program needn't handle non-finite values.
Results may differ from the reference program's by a relative error of at most 0.017.
Values may be sent and summed in bfloat16 or wider, within the bound.
A program may use at most 128 MiB of HBM per device.

```python
import math
import jax
import jax.numpy as jnp
import numpy as np
from jax import lax

D = 1024
HEADS = 16
KV = 8
HD = 64
FF = 512
TOP = 8
SEQ_LEN = 256
EXPERTS = 32
HALF_D = 512
HALF_FF = 256
SLICES = 64
SEQS = 64
TOK_DEV = 128
CAP = 44


def draw_positions(key, part):
    key = jax.random.fold_in(key, 7)
    strides = jax.random.randint(key, (SEQS, SEQ_LEN), 1, 4, dtype=jnp.int32)
    rising = jnp.cumsum(strides, axis=1, dtype=jnp.int32) - strides[:, :1]
    last_place = jnp.arange(SEQ_LEN, dtype=jnp.int32)[None, :] == SEQ_LEN - 1
    return jnp.where(last_place, jnp.int32(3 * (SEQ_LEN - 1)), rising).astype(jnp.int32)


def block_scale(rng, shape, cuts, smallest, high):
    def one(position, shards_of):
        draws = jax.random.uniform(jax.random.fold_in(jax.random.fold_in(rng, 6), position), (shards_of,), jnp.float32, smallest / len(cuts), high / len(cuts))
        return jnp.repeat(jnp.exp(draws), shape[position] // shards_of).reshape((-1,) + (1,) * (len(shape) - position - 1))

    level = one(*cuts[0])
    for cut in cuts[1:]:
        level = level * one(*cut)
    return level


def shared_out(rng, own, number, rows, count, top, reach, skew):
    order = jax.random.permutation(rng, count)
    crowded, usual = load_shares(count, rows * top, reach, skew, True), load_shares(count, rows * top, reach, skew, False)
    places = jnp.arange(count)

    def named(sizes, offset_by):
        used = int((sizes > 0).sum())
        fixed = max(1, used // 4)
        passed = fixed + (places - fixed + offset_by * (used - fixed)) % max(1, count - fixed)
        return jnp.zeros((count,), jnp.int32).at[order[jnp.where(places < fixed, places, passed)]].set(jnp.asarray(sizes, jnp.int32))

    sizes = jnp.where(number % 4 == 0, named(crowded, number // 4), named(usual, number - number // 4 - 1))
    mixed = jax.random.permutation(jax.random.fold_in(own, 3), count)
    donor, taker = mixed[0:count // 2 * 2:2], mixed[1:count // 2 * 2:2]
    room = jnp.minimum(sizes[donor] - 1, reach - sizes[taker]) // 2
    room = jnp.where((donor == order[0]) | (taker == order[0]) | (sizes[taker] == 0), 0, jnp.maximum(room, 0))
    passed = jax.random.randint(jax.random.fold_in(own, 4), (count // 2,), 0, 1 << 20) % (room + 1)
    sizes = sizes.at[donor].add(-passed).at[taker].add(passed)
    members = jnp.searchsorted(jnp.cumsum(sizes), jnp.arange(rows * top), side="right").astype(jnp.int32)
    table = members.reshape(top, rows).T
    table = table[jax.random.permutation(jax.random.fold_in(own, 1), rows)]
    offset_by = jax.random.randint(jax.random.fold_in(own, 2), (rows, 1), 0, top)
    return jnp.take_along_axis(table, (jnp.arange(top)[None, :] + offset_by) % top, axis=1)


def load_shares(number_of, total, reach, lean, full):
    weights = [(1 << 20) // math.isqrt(grade ** lean) + 1 for grade in range(1, number_of + 1)]
    largest = reach if full else min(reach, max(-(-total // number_of), total * weights[0] // sum(weights)))
    least = 1 if total - largest >= number_of - 1 else 0
    holding, surplus = [largest] + [least] * (number_of - 1), total - largest - least * (number_of - 1)
    while surplus > 0:
        movable = [i for i in range(1, number_of) if holding[i] < largest] or [i for i in range(1, number_of) if holding[i] < reach]
        whole, left = sum([weights[i] for i in movable]), surplus
        for i in movable:
            addition = min(reach - holding[i], max(1, left * weights[i] // whole), surplus)
            holding[i] = holding[i] + addition
            surplus = surplus - addition
    return np.array(holding)


def centred(stream_key, shape, scale, most, shards=(), kind=jnp.bfloat16):
    level = block_scale(stream_key, shape, shards, -0.22, 0.18) if shards else 1.0
    array = jax.random.normal(stream_key, shape, jnp.float32) * scale * level
    return jnp.minimum(jnp.maximum(array, -most), most).astype(kind)


def setup_inputs(seed: int = 0) -> dict:
    arg_keys = jax.random.split(jax.random.key(seed), 15)
    tokens = centred(arg_keys[0], (SEQS, SEQ_LEN, D), 1.0, 6.0, ((0, 64), (1, 2)))
    positions = draw_positions(jax.random.fold_in(arg_keys[14], 71), 0)
    routes_keys = jax.random.split(jax.random.fold_in(arg_keys[2], 1), SEQS * SEQ_LEN // TOK_DEV)
    routes_turns = jax.random.permutation(jax.random.fold_in(arg_keys[2], 3), SEQS * SEQ_LEN // TOK_DEV)
    routes = jax.vmap(lambda own, number: shared_out(jax.random.fold_in(arg_keys[2], 2), own, number, TOK_DEV, EXPERTS, TOP, CAP, 1))(routes_keys, routes_turns).reshape((SEQS, SEQ_LEN, TOP))
    cotangent = centred(arg_keys[3], (SEQS, SEQ_LEN, D), 1.0, 6.0, ((0, 64), (1, 2)))
    first_gain = jnp.clip(1.0 + 0.18 * jax.random.normal(arg_keys[4], (D,), jnp.float32), 0.099609375, 1.8984375).astype(jnp.bfloat16)
    w_query = centred(arg_keys[5], (D, HEADS * HD), D ** -0.5, 0.1875, ((0, 64),))
    w_key = centred(arg_keys[6], (D, KV * HD), D ** -0.5, 0.1875, ((0, 64),))
    w_value = centred(arg_keys[7], (D, KV * HD), D ** -0.5, 0.1875, ((0, 64),))
    w_out = centred(arg_keys[8], (HEADS * HD, D), (HEADS * HD // 16) ** -0.5, 0.75, ((0, 64),))
    second_gain = jnp.clip(1.0 + 0.18 * jax.random.normal(arg_keys[9], (D,), jnp.float32), 0.099609375, 1.8984375).astype(jnp.bfloat16)
    w_router = centred(arg_keys[10], (D, EXPERTS), (4 * D) ** -0.5, 0.09375, ((0, 64),))
    w_gate = centred(arg_keys[11], (SLICES, HALF_D, FF), D ** -0.5, 0.1875, ((0, 64),))
    w_up = centred(arg_keys[12], (SLICES, HALF_D, FF), D ** -0.5, 0.1875, ((0, 64),))
    w_down = centred(arg_keys[13], (SLICES, HALF_FF, D), (FF // 8) ** -0.5, 0.75, ((0, 64),))
    return {"tokens": tokens, "positions": positions, "routes": routes, "cotangent": cotangent, "first_gain": first_gain, "w_query": w_query, "w_key": w_key, "w_value": w_value, "w_out": w_out, "second_gain": second_gain, "w_router": w_router, "w_gate": w_gate, "w_up": w_up, "w_down": w_down}


@jax.custom_vjp
def low(v):
    return lax.optimization_barrier(v.astype(jnp.bfloat16)).astype(jnp.float32)

@jax.custom_vjp
def low_back(v):
    return v

def low_keep(v):
    return (low(v), None)

def low_pass(kept, grad):
    return (grad,)

def back_keep(v):
    return (v, None)

def back_low(kept, grad):
    return (low(grad),)
low.defvjp(low_keep, low_pass)
low_back.defvjp(back_keep, back_low)
epsilon = 1e-06
rope_base = 10000.0
masked_score = -1e+30
highest = lax.Precision.HIGHEST

def product(left, right):
    return jnp.dot(left, right, precision=highest)

def rms_scale(values, gain):
    return values * lax.rsqrt(lax.optimization_barrier(jnp.mean(values * values, axis=-1, keepdims=True)) + epsilon) * gain

def rotate(values, cosine, sine_table):
    middle = values.shape[-1] // 2
    first_half = values[..., :middle]
    second_half = values[..., middle:]
    return jnp.concatenate([first_half * cosine - second_half * sine_table, second_half * cosine + first_half * sine_table], axis=-1)

def slot_index(chosen):
    flat_ids = chosen.reshape(-1).astype(jnp.int32)
    onehot = (flat_ids[:, None] == jnp.arange(EXPERTS, dtype=jnp.int32)[None, :]).astype(jnp.int32)
    blocked = onehot.reshape(-1, TOK_DEV * TOP, EXPERTS)
    ranked = jnp.cumsum(blocked, axis=1) - blocked
    places = lax.optimization_barrier(jnp.sum(ranked * blocked, axis=2)).reshape(-1)
    block_ids = jnp.arange(flat_ids.shape[0], dtype=jnp.int32) // (TOK_DEV * TOP)
    return ((block_ids * EXPERTS + flat_ids) * CAP + places).astype(jnp.int32)

def layer(inputs, cosine, sine_table, slot_ids, choose, params):
    first_gain, w_query, w_key, w_value, w_out, second_gain, w_router, w_gate, w_up, w_down = params
    seq_count = inputs.shape[0]
    token_rows = seq_count * SEQ_LEN
    flat_in = inputs.reshape(token_rows, D)
    normed = low(rms_scale(flat_in, first_gain))
    query_rows = low_back(product(normed, w_query)).reshape(seq_count, SEQ_LEN, HEADS, HD)
    key_rows = low_back(product(normed, w_key)).reshape(seq_count, SEQ_LEN, KV, HD)
    value_rows = low(low_back(product(normed, w_value))).reshape(seq_count, SEQ_LEN, KV, HD)
    query_rows = low(low_back(rotate(query_rows, cosine, sine_table) * HD ** (-0.5)))
    key_rows = low(low_back(rotate(key_rows, cosine, sine_table)))
    grouped = query_rows.reshape(seq_count, SEQ_LEN, KV, HEADS // KV, HD)
    scores = jnp.einsum('sqkgd,spkd->skgqp', grouped, key_rows, precision=highest)
    causal = jnp.arange(SEQ_LEN, dtype=jnp.int32)[:, None] >= jnp.arange(SEQ_LEN, dtype=jnp.int32)[None, :]
    scores = low_back(jnp.where(causal, scores, masked_score))
    attn_probs = low(jax.nn.softmax(scores, axis=-1))
    mixture = jnp.einsum('skgqp,spkd->sqkgd', attn_probs, value_rows, precision=highest)
    attended = low(low_back(mixture.reshape(token_rows, HEADS * HD)))
    middle = flat_in + low_back(product(attended, w_out))
    second = low(rms_scale(middle, second_gain))
    logits = low_back(product(second, w_router))
    picked = lax.optimization_barrier(jnp.sum(logits[:, None, :] * choose, axis=-1))
    gate_weights = jax.nn.softmax(picked, axis=-1)
    blocks = token_rows // TOK_DEV
    routed = jnp.repeat(second, TOP, axis=0)
    buffer = jnp.zeros((blocks * EXPERTS * CAP, D), jnp.float32).at[slot_ids].set(routed).reshape(blocks, EXPERTS, CAP, D)
    gate_all = w_gate.reshape(EXPERTS, D, FF)
    up_all = w_up.reshape(EXPERTS, D, FF)
    down_all = w_down.reshape(EXPERTS, FF, D)
    taken_rows = low_back(buffer)
    gate_pre = low_back(jnp.einsum('becd,edf->becf', taken_rows, gate_all, precision=highest))
    up_pre = low_back(jnp.einsum('becd,edf->becf', taken_rows, up_all, precision=highest))
    hidden = low(jax.nn.silu(gate_pre) * up_pre)
    combined = jnp.einsum('becf,efd->becd', hidden, down_all, precision=highest)
    combined = low(low_back(combined))
    returned = combined.reshape(-1, D)[slot_ids].reshape(token_rows, TOP, D)
    output = middle + lax.optimization_barrier(jnp.sum(gate_weights[:, :, None] * returned, axis=1))
    return output.reshape(seq_count, SEQ_LEN, D)

def reference(tokens, positions, routes, cotangent, first_gain, w_query, w_key, w_value, w_out, second_gain, w_router, w_gate, w_up, w_down):
    params = tuple((weight.astype(jnp.float32) for weight in (first_gain, w_query, w_key, w_value, w_out, second_gain, w_router, w_gate, w_up, w_down)))
    group = math.gcd(SEQS, max(1, 4096 // SEQ_LEN))
    rounds = SEQS // group
    inverse = rope_base ** (-(2.0 * jnp.arange(HD // 2, dtype=jnp.float32)) / HD)

    def one_group(totals, pieces):
        block_tokens, block_positions, block_routes, block_cotangent = pieces
        angle = block_positions.astype(jnp.float32)[..., None] * inverse
        cosine = jnp.cos(angle)[:, :, None, :]
        sine_table = jnp.sin(angle)[:, :, None, :]
        chosen = block_routes.reshape(-1, TOP).astype(jnp.int32)
        slot_ids = slot_index(chosen)
        choose = (chosen[:, :, None] == jnp.arange(EXPERTS, dtype=jnp.int32)[None, None, :]).astype(jnp.float32)

        def forward(inputs, weight_set):
            return layer(inputs, cosine, sine_table, slot_ids, choose, weight_set)
        output, pullback = jax.vjp(forward, block_tokens.astype(jnp.float32), params)
        grad_inputs, grad_params = pullback(block_cotangent.astype(jnp.float32))
        totals = tuple((running + increment for running, increment in zip(totals, grad_params)))
        return (totals, (output.astype(jnp.bfloat16), grad_inputs))
    sectioned = (tokens.reshape(rounds, group, SEQ_LEN, D), positions.reshape(rounds, group, SEQ_LEN), routes.reshape(rounds, group, SEQ_LEN, TOP), cotangent.reshape(rounds, group, SEQ_LEN, D))
    initial = tuple((jnp.zeros_like(weight) for weight in params))
    totals, (outputs, grad_all) = lax.scan(one_group, initial, sectioned)
    return (outputs.reshape(SEQS, SEQ_LEN, D), grad_all.reshape(SEQS, SEQ_LEN, D), totals[0], totals[1], totals[2], totals[3], totals[4], totals[5], totals[6], totals[7], totals[8], totals[9])
```

```python
import functools

import jax
import jax.numpy as jnp
from jax import lax
from jax.experimental import pallas as pl
from jax.experimental.pallas import tpu as pltpu
from jax.sharding import PartitionSpec as P

HD = 64
CORES = 2
SMALL = 128

epsilon = 1e-06
rope_base = 10000.0
masked_score = -1e30
MESH = pl.DeviceIdType.MESH
ANY = pl.BlockSpec(memory_space=pl.ANY)
VMEM = pl.BlockSpec(memory_space=pltpu.VMEM)


def from_partner(array, axis, apart):
    return lax.ppermute(array, axis, [(i, i ^ 1 << apart) for i in range(lax.axis_size(axis))])


def dot_plain(left, right):
    return jnp.dot(left, right, preferred_element_type=jnp.float32)


def dot_left(left, right):
    return lax.dot_general(
        left, right, (((0,), (0,)), ((), ())), preferred_element_type=jnp.float32
    )


def dot_right(left, right):
    return lax.dot_general(
        left, right, (((1,), (1,)), ((), ())), preferred_element_type=jnp.float32
    )


def rms_scale(values, gain):
    return values * lax.rsqrt(jnp.mean(values * values, axis=-1, keepdims=True) + epsilon) * gain


def rotate(values, cosine, sine_table):
    middle = values.shape[-1] // 2
    first_half = values[..., :middle]
    second_half = values[..., middle:]
    return jnp.concatenate(
        [
            first_half * cosine - second_half * sine_table,
            second_half * cosine + first_half * sine_table,
        ],
        axis=-1,
    )


def join_halves(own, other, parity):
    return jnp.where(
        parity == 0, jnp.concatenate([own, other], axis=0), jnp.concatenate([other, own], axis=0)
    )


def gather_kernel(chips, shard, full, send, recv, core_send, core_recv, local):
    seq, me = lax.axis_index("seq"), lax.axis_index("fsdp")
    chip, core = me // CORES, me % CORES
    partner = chip * CORES + 1 - core

    def device_of(step):
        return lax.rem(chip + step, chips) * CORES + core

    barrier = pltpu.get_barrier_semaphore()
    pl.semaphore_signal(barrier, inc=1, device_id=(seq, partner), device_id_type=MESH)

    @pl.loop(1, chips)
    def _(step):
        pl.semaphore_signal(barrier, inc=1, device_id=(seq, device_of(step)), device_id_type=MESH)

    pl.semaphore_wait(barrier, chips)

    own = pltpu.make_async_copy(shard, full.at[me], local)
    own.start()

    def outgoing(step):
        return pltpu.make_async_remote_copy(
            src_ref=shard,
            dst_ref=full.at[me],
            send_sem=send.at[step],
            recv_sem=recv.at[step],
            device_id=(seq, device_of(step)),
            device_id_type=MESH,
        )

    def arrived(step):
        source = lax.rem(chip + chips - step, chips) * CORES + core
        return pltpu.make_async_remote_copy(
            src_ref=shard,
            dst_ref=full.at[source],
            send_sem=send.at[step],
            recv_sem=recv.at[step],
            device_id=(seq, device_of(step)),
            device_id_type=MESH,
        )

    def across(step):
        source = lax.rem(chip + chips - step, chips) * CORES + core
        return pltpu.make_async_remote_copy(
            src_ref=full.at[source],
            dst_ref=full.at[source],
            send_sem=core_send.at[step],
            recv_sem=core_recv.at[step],
            device_id=(seq, partner),
            device_id_type=MESH,
        )

    def from_across(step):
        source = lax.rem(chip + chips - step, chips) * CORES + 1 - core
        return pltpu.make_async_remote_copy(
            src_ref=full.at[source],
            dst_ref=full.at[source],
            send_sem=core_send.at[step],
            recv_sem=core_recv.at[step],
            device_id=(seq, partner),
            device_id_type=MESH,
        )

    @pl.loop(1, chips)
    def _(step):
        outgoing(step).start()

    own.wait()
    across(0).start()

    @pl.loop(1, chips)
    def _(step):
        arrived(step).wait_recv()
        across(step).start()

    @pl.loop(0, chips)
    def _(step):
        from_across(step).wait_recv()
        across(step).wait_send()

    @pl.loop(1, chips)
    def _(step):
        outgoing(step).wait_send()


def gather_shards(shard):
    count = lax.axis_size("fsdp")
    chips = count // CORES
    rows, columns = shard.shape
    full = pl.pallas_call(
        functools.partial(gather_kernel, chips),
        out_shape=jax.ShapeDtypeStruct((count, rows, columns), shard.dtype),
        in_specs=[ANY],
        out_specs=ANY,
        scratch_shapes=[
            pltpu.SemaphoreType.DMA((chips,)),
            pltpu.SemaphoreType.DMA((chips,)),
            pltpu.SemaphoreType.DMA((chips,)),
            pltpu.SemaphoreType.DMA((chips,)),
            pltpu.SemaphoreType.DMA,
        ],
        compiler_params=pltpu.CompilerParams(collective_id=0, has_side_effects=True),
        name="gather_weights",
    )(shard)
    return full.reshape(count * rows, columns)


def scatter_kernel(chips, number, *refs):
    parts, totals = refs[:number], refs[number : 2 * number]
    halves = refs[2 * number : 3 * number]
    landed = refs[3 * number : 4 * number]
    mine = refs[4 * number : 5 * number]
    theirs = refs[5 * number : 6 * number]
    core_send, core_recv, send, recv, seq_send, seq_recv = refs[6 * number :]
    seq, me = lax.axis_index("seq"), lax.axis_index("fsdp")
    chip, core = me // CORES, me % CORES
    partner = chip * CORES + 1 - core

    def device_of(step):
        return lax.rem(chip + step, chips) * CORES + core

    barrier = pltpu.get_barrier_semaphore()
    pl.semaphore_signal(barrier, inc=1, device_id=(seq, partner), device_id_type=MESH)
    pl.semaphore_signal(barrier, inc=1, device_id=(1 - seq, me), device_id_type=MESH)

    @pl.loop(1, chips)
    def _(step):
        pl.semaphore_signal(barrier, inc=1, device_id=(seq, device_of(step)), device_id_type=MESH)

    pl.semaphore_wait(barrier, chips + 1)

    def across(i):
        return pltpu.make_async_remote_copy(
            src_ref=parts[i].at[:, 1 - core],
            dst_ref=halves[i],
            send_sem=core_send.at[i],
            recv_sem=core_recv.at[i],
            device_id=(seq, partner),
            device_id_type=MESH,
        )

    for i in range(number):
        across(i).start()

    def outgoing(i, step):
        target = lax.rem(chip + step, chips)
        return pltpu.make_async_remote_copy(
            src_ref=halves[i].at[target],
            dst_ref=landed[i].at[chip],
            send_sem=send.at[i, step],
            recv_sem=recv.at[i, step],
            device_id=(seq, target * CORES + core),
            device_id_type=MESH,
        )

    for i in range(number):
        across(i).wait_recv()

        @pl.loop(1, chips)
        def _(step):
            target = lax.rem(chip + step, chips)
            halves[i][target] = (
                halves[i][target].astype(jnp.float32) + parts[i][target, core].astype(jnp.float32)
            ).astype(jnp.bfloat16)
            outgoing(i, step).start()

        landed[i][chip] = (
            halves[i][chip].astype(jnp.float32) + parts[i][chip, core].astype(jnp.float32)
        ).astype(jnp.bfloat16)

    for i in range(number):

        @pl.loop(1, chips)
        def _(step):
            outgoing(i, step).wait_recv()

        mine[i][...] = jnp.sum(landed[i][...].astype(jnp.float32), axis=0)
        swap = pltpu.make_async_remote_copy(
            src_ref=mine[i],
            dst_ref=theirs[i],
            send_sem=seq_send.at[i],
            recv_sem=seq_recv.at[i],
            device_id=(1 - seq, me),
            device_id_type=MESH,
        )
        swap.start()

    for i in range(number):
        swap = pltpu.make_async_remote_copy(
            src_ref=mine[i],
            dst_ref=theirs[i],
            send_sem=seq_send.at[i],
            recv_sem=seq_recv.at[i],
            device_id=(1 - seq, me),
            device_id_type=MESH,
        )
        swap.wait_recv()
        totals[i][...] = mine[i][...] + theirs[i][...]
        swap.wait_send()
        across(i).wait_send()

        @pl.loop(1, chips)
        def _(step):
            outgoing(i, step).wait_send()


def scatter_sums(fulls, identity):
    count = lax.axis_size("fsdp")
    chips = count // CORES
    number = len(fulls)
    rows = fulls[0].shape[0] // count
    widths = [full.shape[1] for full in fulls]
    parts = [full.reshape(chips, CORES, rows, full.shape[1]) for full in fulls]
    half = [pltpu.VMEM((chips, rows, width), jnp.bfloat16) for width in widths]
    one = [pltpu.VMEM((rows, width), jnp.float32) for width in widths]
    return pl.pallas_call(
        functools.partial(scatter_kernel, chips, number),
        out_shape=[jax.ShapeDtypeStruct((rows, width), jnp.float32) for width in widths],
        in_specs=[VMEM] * number,
        out_specs=[VMEM] * number,
        scratch_shapes=half
        + half
        + one
        + one
        + [
            pltpu.SemaphoreType.DMA((number,)),
            pltpu.SemaphoreType.DMA((number,)),
            pltpu.SemaphoreType.DMA((number, chips)),
            pltpu.SemaphoreType.DMA((number, chips)),
            pltpu.SemaphoreType.DMA((number,)),
            pltpu.SemaphoreType.DMA((number,)),
        ],
        compiler_params=pltpu.CompilerParams(
            collective_id=identity, has_side_effects=True, vmem_limit_bytes=48 * 2**20
        ),
        name="scatter_gradients",
    )(*parts)


def exchange_rows(rows):
    slots = lax.axis_size("fsdp")
    blocks = rows.reshape(slots, rows.shape[0] // slots, *rows.shape[1:])
    return lax.all_to_all(blocks, "fsdp", split_axis=0, concat_axis=0, tiled=True).reshape(
        rows.shape
    )


def on_device(
    tokens,
    positions,
    routes,
    cotangent,
    first_gain,
    w_query,
    w_key,
    w_value,
    w_out,
    second_gain,
    w_router,
    w_gate,
    w_up,
    w_down,
):
    width = tokens.shape[2]
    rows = tokens.shape[1]
    heads_all = w_query.shape[1] // HD
    kv_all = w_key.shape[1] // HD
    group = heads_all // kv_all
    q_width, kv_width = heads_all * HD, kv_all * HD
    scale = HD ** (-0.5)
    slots = lax.axis_size("fsdp")
    experts = slots // CORES
    seq = lax.axis_index("seq")
    parity = lax.axis_index("fsdp") % CORES
    share = 24
    places = CORES * share

    x_own = tokens[0]
    x_before = lax.ppermute(x_own, "seq", [(0, 1)])
    pos_before = lax.ppermute(positions, "seq", [(0, 1)])

    own_gate, own_up, own_down = (w_gate[0], w_up[0], w_down[0])
    other_gate, other_up, other_down = from_partner((own_gate, own_up, own_down), "fsdp", 0)
    gate_full = join_halves(own_gate, other_gate, parity)
    up_full = join_halves(own_up, other_up, parity)
    down_full = join_halves(own_down, other_down, parity)

    chosen = routes[0]
    ids = jnp.arange(experts, dtype=jnp.int32)
    mask = jnp.any(chosen[:, :, None] == ids[None, None, :], axis=1)
    mask_low = mask.astype(jnp.bfloat16)
    earlier = (jnp.arange(rows)[:, None] > jnp.arange(rows)[None, :]).astype(jnp.bfloat16)
    rank = jnp.where(mask, dot_plain(earlier, mask_low).astype(jnp.int32), -1)
    onehot_wide = rank.T[:, None, :] == jnp.arange(places, dtype=jnp.int32)[None, :, None]
    onehot = onehot_wide.astype(jnp.bfloat16).reshape(experts * places, rows)

    grad_low = cotangent[0]
    grad_output = grad_low.astype(jnp.float32)
    grad_received = exchange_rows(dot_plain(onehot, grad_low).astype(jnp.bfloat16))

    small = jnp.concatenate(
        [
            w_router,
            first_gain[:, None],
            second_gain[:, None],
            jnp.zeros((w_router.shape[0], SMALL - experts - 2), jnp.bfloat16),
        ],
        axis=1,
    )
    gathered = gather_shards(jnp.concatenate([w_query, w_key, w_value, w_out, small], axis=1))
    at = 0
    pieces = []
    for columns in (q_width, kv_width, kv_width, width, SMALL):
        pieces.append(gathered[:, at : at + columns])
        at += columns
    query_full, key_full, value_full, out_full, small_full = pieces
    router_full = small_full[:, :experts]
    gain_first = small_full[:, experts].astype(jnp.float32)
    gain_second = small_full[:, experts + 1].astype(jnp.float32)

    x_both = jnp.concatenate([x_before, x_own], axis=0).astype(jnp.float32)
    pos_both = jnp.concatenate([pos_before[0], positions[0]], axis=0)
    inputs = x_both[rows:]
    inverse = rope_base ** (-(2.0 * jnp.arange(HD // 2, dtype=jnp.float32)) / HD)
    angle = pos_both.astype(jnp.float32)[:, None] * inverse[None, :]
    cosine = jnp.cos(angle)[:, None, :]
    sine_table = jnp.sin(angle)[:, None, :]
    inverse_one = lax.rsqrt(jnp.mean(x_both * x_both, axis=-1, keepdims=True) + epsilon)
    normed_both = (x_both * inverse_one * gain_first).astype(jnp.bfloat16)
    normed_own = normed_both[rows:]
    query_pre = dot_plain(normed_own, query_full).reshape(rows, heads_all, HD)
    key_pre = dot_plain(normed_both, key_full).reshape(2 * rows, kv_all, HD)
    query_rot = (rotate(query_pre, cosine[rows:], sine_table[rows:]) * scale).astype(jnp.bfloat16)
    keyed = rotate(key_pre, cosine, sine_table).astype(jnp.bfloat16)
    valued = dot_plain(normed_both, value_full).astype(jnp.bfloat16).reshape(2 * rows, kv_all, HD)
    grouped = query_rot.reshape(rows, kv_all, group, HD)
    key_at = jnp.arange(2 * rows)[None, :]
    allowed = (key_at - rows <= jnp.arange(rows)[:, None]) & ((key_at >= rows) | (seq == 1))
    scores = jnp.einsum("qkgd,pkd->kgqp", grouped, keyed, preferred_element_type=jnp.float32)
    scores = jnp.where(allowed, scores, masked_score)
    peak = jnp.max(scores, axis=-1, keepdims=True)
    raised = jnp.exp(scores - peak)
    probs = raised / jnp.sum(raised, axis=-1, keepdims=True)
    probs_low = probs.astype(jnp.bfloat16)
    attended = (
        jnp.einsum("kgqp,pkd->qkgd", probs_low, valued, preferred_element_type=jnp.float32)
        .astype(jnp.bfloat16)
        .reshape(rows, q_width)
    )
    middle = inputs + dot_plain(attended, out_full)

    inverse_two = lax.rsqrt(jnp.mean(middle * middle, axis=-1, keepdims=True) + epsilon)
    normed_two = (middle * inverse_two * gain_second).astype(jnp.bfloat16)
    expert_rows = exchange_rows(dot_plain(onehot, normed_two).astype(jnp.bfloat16))
    logits = jnp.where(mask, dot_plain(normed_two, router_full), masked_score)
    lifted = jnp.where(mask, jnp.exp(logits - jnp.max(logits, axis=-1, keepdims=True)), 0.0)
    gates = lifted / jnp.sum(lifted, axis=-1, keepdims=True)
    gates_wide = jnp.where(onehot_wide, gates.T[:, None, :], 0.0)
    gate_sent = jnp.sum(gates_wide, axis=-1).reshape(slots, share)
    gate_slot = lax.all_to_all(gate_sent, "fsdp", split_axis=0, concat_axis=0, tiled=True)
    gate_slot = gate_slot.reshape(-1, 1)

    gate_pre = dot_plain(expert_rows, gate_full)
    up_pre = dot_plain(expert_rows, up_full)
    sigmoid_gate = jax.nn.sigmoid(gate_pre)
    silu_gate = gate_pre * sigmoid_gate
    hidden = (silu_gate * up_pre).astype(jnp.bfloat16)
    part_out = dot_plain(hidden, down_full).astype(jnp.bfloat16)
    returned = exchange_rows(part_out)

    grad_parts = (gate_slot * grad_received.astype(jnp.float32)).astype(jnp.bfloat16)
    grad_hidden = dot_right(grad_parts, down_full)
    grad_gate_pre = (
        grad_hidden * up_pre * sigmoid_gate * (1.0 + gate_pre * (1.0 - sigmoid_gate))
    ).astype(jnp.bfloat16)
    grad_up_pre = (grad_hidden * silu_gate).astype(jnp.bfloat16)
    grad_expert_rows = (
        dot_right(grad_gate_pre, gate_full) + dot_right(grad_up_pre, up_full)
    ).astype(jnp.bfloat16)
    grad_slots = exchange_rows(grad_expert_rows)

    def pair_sum(full):
        middle_row = full.shape[0] // 2
        mine = jnp.where(parity == 0, full[:middle_row], full[middle_row:])
        other = jnp.where(parity == 0, full[middle_row:], full[:middle_row]).astype(jnp.bfloat16)
        low = (mine + from_partner(other, "fsdp", 0).astype(jnp.float32)).astype(jnp.bfloat16)
        return low.astype(jnp.float32) + from_partner(low, "seq", 0).astype(jnp.float32)

    grad_down = pair_sum(dot_left(hidden, grad_parts))
    grad_gate = pair_sum(dot_left(expert_rows, grad_gate_pre))
    grad_up = pair_sum(dot_left(expert_rows, grad_up_pre))

    gates_high = gates_wide.astype(jnp.bfloat16)
    gates_rest = (gates_wide - gates_high.astype(jnp.float32)).astype(jnp.bfloat16)
    flat = (experts * places, rows)
    mixed = dot_left(gates_high.reshape(flat), returned) + dot_left(
        gates_rest.reshape(flat), returned
    )
    layer_out = (middle + mixed).astype(jnp.bfloat16)
    products = dot_right(returned, grad_low).reshape(experts, places, rows)
    grad_gates = jnp.sum(jnp.where(onehot_wide, products, 0.0), axis=1).T
    grad_picked = gates * (grad_gates - jnp.sum(gates * grad_gates, axis=-1, keepdims=True))
    grad_logits = grad_picked.astype(jnp.bfloat16)
    grad_router = dot_left(normed_two, grad_logits)
    grad_normed_two = dot_right(grad_logits, router_full) + dot_left(onehot, grad_slots)

    normed = middle * inverse_two
    scaled = grad_normed_two * gain_second
    grad_middle = grad_output + inverse_two * (
        scaled - normed * jnp.mean(scaled * normed, axis=-1, keepdims=True)
    )
    grad_gain_second = jnp.sum(grad_normed_two * normed, axis=0)
    grad_branch = grad_middle.astype(jnp.bfloat16)
    grad_out_full = dot_left(attended, grad_branch).astype(jnp.bfloat16)
    small_two = jnp.concatenate(
        [
            grad_router,
            grad_gain_second[:, None],
            jnp.zeros((width, SMALL - experts - 1), jnp.float32),
        ],
        axis=1,
    ).astype(jnp.bfloat16)

    grad_heads = (
        dot_right(grad_branch, out_full).astype(jnp.bfloat16).reshape(rows, kv_all, group, HD)
    )
    grad_probs = jnp.einsum(
        "qkgd,pkd->kgqp", grad_heads, valued, preferred_element_type=jnp.float32
    )
    grad_scores = (
        probs * (grad_probs - jnp.sum(probs * grad_probs, axis=-1, keepdims=True))
    ).astype(jnp.bfloat16)
    grad_value_in = (
        jnp.einsum("kgqp,qkgd->pkd", probs_low, grad_heads, preferred_element_type=jnp.float32)
        .astype(jnp.bfloat16)
        .reshape(2 * rows, kv_width)
    )
    grad_query_rot = (
        jnp.einsum("kgqp,pkd->qkgd", grad_scores, keyed, preferred_element_type=jnp.float32)
        .astype(jnp.bfloat16)
        .astype(jnp.float32)
        .reshape(rows, heads_all, HD)
    )
    grad_key_rot = (
        jnp.einsum("kgqp,qkgd->pkd", grad_scores, grouped, preferred_element_type=jnp.float32)
        .astype(jnp.bfloat16)
        .astype(jnp.float32)
    )
    grad_query_in = (
        (rotate(grad_query_rot, cosine[rows:], -sine_table[rows:]) * scale)
        .astype(jnp.bfloat16)
        .reshape(rows, q_width)
    )
    grad_key_in = (
        rotate(grad_key_rot, cosine, -sine_table).astype(jnp.bfloat16).reshape(2 * rows, kv_width)
    )
    grad_query_full = dot_left(normed_own, grad_query_in).astype(jnp.bfloat16)
    grad_key_full = dot_left(normed_both, grad_key_in).astype(jnp.bfloat16)
    grad_value_full = dot_left(normed_both, grad_value_in).astype(jnp.bfloat16)
    grad_both = dot_right(grad_key_in, key_full) + dot_right(grad_value_in, value_full)
    grad_before = grad_both[:rows].astype(jnp.bfloat16)
    grad_after = lax.ppermute(grad_before, "seq", [(1, 0)]).astype(jnp.float32)
    grad_own = grad_both[rows:] + dot_right(grad_query_in, query_full)
    normed_x = x_both * inverse_one
    grad_gain_first = jnp.sum(grad_own * normed_x[rows:], axis=0) + jnp.sum(
        grad_both[:rows] * normed_x[:rows], axis=0
    )
    small_one = jnp.concatenate(
        [grad_gain_first[:, None], jnp.zeros((width, SMALL - 1), jnp.float32)], axis=1
    ).astype(jnp.bfloat16)
    scaled_one = (grad_own + grad_after) * gain_first
    grad_tokens = grad_middle + inverse_one[rows:] * (
        scaled_one
        - normed_x[rows:] * jnp.mean(scaled_one * normed_x[rows:], axis=-1, keepdims=True)
    )

    sums = scatter_sums(
        [grad_out_full, small_two, grad_query_full, grad_key_full, grad_value_full, small_one], 1
    )
    return (
        layer_out[None],
        grad_tokens[None],
        sums[5][:, 0],
        sums[2],
        sums[3],
        sums[4],
        sums[0],
        sums[1][:, experts],
        sums[1][:, :experts],
        grad_gate[None],
        grad_up[None],
        grad_down[None],
    )


def solution(mesh):
    rows = P("fsdp", "seq", None)
    matrix, cube = P("fsdp", None), P("fsdp", None, None)
    return jax.shard_map(
        on_device,
        mesh=mesh,
        in_specs=(
            rows,
            P("fsdp", "seq"),
            rows,
            rows,
            P("fsdp"),
            matrix,
            matrix,
            matrix,
            matrix,
            P("fsdp"),
            matrix,
            cube,
            cube,
            cube,
        ),
        out_specs=(
            rows,
            rows,
            P("fsdp"),
            matrix,
            matrix,
            matrix,
            matrix,
            P("fsdp"),
            matrix,
            cube,
            cube,
            cube,
        ),
        check_vma=False,
    )
```

```python
import functools

import jax
import jax.numpy as jnp
from jax import lax
from jax.experimental import pallas as pl
from jax.experimental.pallas import tpu as pltpu
from jax.sharding import PartitionSpec as P

HD = 64
CORES = 2
SMALL = 128

epsilon = 1e-06
rope_base = 10000.0
masked_score = -1e30
MESH = pl.DeviceIdType.MESH
ANY = pl.BlockSpec(memory_space=pl.ANY)
VMEM = pl.BlockSpec(memory_space=pltpu.VMEM)


def from_partner(array, axis, apart):
    return lax.ppermute(array, axis, [(i, i ^ 1 << apart) for i in range(lax.axis_size(axis))])


def dot_plain(left, right):
    return jnp.dot(left, right, preferred_element_type=jnp.float32)


def dot_left(left, right):
    return lax.dot_general(
        left, right, (((0,), (0,)), ((), ())), preferred_element_type=jnp.float32
    )


def dot_right(left, right):
    return lax.dot_general(
        left, right, (((1,), (1,)), ((), ())), preferred_element_type=jnp.float32
    )


def rms_scale(values, gain):
    return values * lax.rsqrt(jnp.mean(values * values, axis=-1, keepdims=True) + epsilon) * gain


def rotate(values, cosine, sine_table):
    middle = values.shape[-1] // 2
    first_half = values[..., :middle]
    second_half = values[..., middle:]
    return jnp.concatenate(
        [
            first_half * cosine - second_half * sine_table,
            second_half * cosine + first_half * sine_table,
        ],
        axis=-1,
    )


def join_halves(own, other, parity):
    return jnp.where(
        parity == 0, jnp.concatenate([own, other], axis=0), jnp.concatenate([other, own], axis=0)
    )


LONG = 4


def coordinates():
    seq, me = lax.axis_index("seq"), lax.axis_index("fsdp")
    return seq, me // 32, (me // 8) % LONG, (me // 2) % LONG, me % CORES


def device(seq, y, x, z, core):
    return (seq, ((y * LONG + x) * LONG + z) * CORES + core)


def enter(targets):
    barrier = pltpu.get_barrier_semaphore()
    for target in targets:
        pl.semaphore_signal(barrier, inc=1, device_id=target, device_id_type=MESH)
    pl.semaphore_wait(barrier, len(targets))


def neighbours():
    seq, y, x, z, core = coordinates()
    return [
        device(seq, y, x, z, 1 - core),
        device(seq, 1 - y, x, z, core),
        device(seq, y, lax.rem(x + 1, LONG), z, core),
        device(seq, y, lax.rem(x + 3, LONG), z, core),
        device(seq, y, x, lax.rem(z + 1, LONG), core),
        device(seq, y, x, lax.rem(z + 3, LONG), core),
        device(1 - seq, y, x, z, core),
    ]


def gather_kernel(shard_a, shard_b, x_own, pos_own, full_a, full_b, x_other, pos_other, *sems):
    send, recv, core_send, core_recv, seq_send, seq_recv, local = sems
    seq, y, x, z, core = coordinates()
    enter(neighbours())
    other_seq = device(1 - seq, y, x, z, core)
    swaps = [
        pltpu.make_async_remote_copy(
            src_ref=source,
            dst_ref=target,
            send_sem=seq_send.at[i],
            recv_sem=seq_recv.at[i],
            device_id=other_seq,
            device_id_type=MESH,
        )
        for i, (source, target) in enumerate(((x_own, x_other), (pos_own, pos_other)))
    ]
    fulls = (full_a, full_b)
    first_at, second_at = (x, z), (z, x)

    def along(i, stage, shift):
        if (i == 0) == (stage == 0):
            return device(seq, y, lax.rem(x + shift, LONG), z, core)
        return device(seq, y, x, lax.rem(z + shift, LONG), core)

    def block(i, stage, shift, ys):
        at = lax.rem((first_at if stage == 0 else second_at)[i] + shift, LONG)
        if stage == 0:
            xs, zs = (at, z) if i == 0 else (x, at)
        else:
            xs, zs = (slice(None), at) if i == 0 else (at, slice(None))
        return fulls[i].at[ys, xs, zs, core]

    def copy(i, k, part, target):
        return pltpu.make_async_remote_copy(
            src_ref=part,
            dst_ref=part,
            send_sem=send.at[i, k],
            recv_sem=recv.at[i, k],
            device_id=target,
            device_id_type=MESH,
        )

    both = slice(None)
    own = []
    started = []

    def start(i, k, part, target):
        moved = copy(i, k, part, target)
        moved.start()
        started.append(moved)

    crossing = []

    def cross(i, k, index):
        for side, wait in ((core, False), (1 - core, True)):
            part = fulls[i].at[(*index, side)]
            moved = pltpu.make_async_remote_copy(
                src_ref=part,
                dst_ref=part,
                send_sem=core_send.at[i, k],
                recv_sem=core_recv.at[i, k],
                device_id=device(seq, y, x, z, 1 - core),
                device_id_type=MESH,
            )
            if wait:
                crossing.append((moved, last))
            else:
                moved.start()
                last = moved

    for i, shard in enumerate((shard_a, shard_b)):
        kept = pltpu.make_async_copy(shard, fulls[i].at[y, x, z, core], local.at[i])
        kept.start()
        own.append(kept)
        outgoing = pltpu.make_async_remote_copy(
            src_ref=shard,
            dst_ref=fulls[i].at[y, x, z, core],
            send_sem=send.at[i, 0],
            recv_sem=recv.at[i, 0],
            device_id=device(seq, 1 - y, x, z, core),
            device_id_type=MESH,
        )
        outgoing.start()
        started.append(outgoing)
    for moved in swaps:
        moved.start()
    for i in range(2):
        own[i].wait()
        copy(i, 0, fulls[i].at[1 - y, x, z, core], other_seq).wait_recv()

    for stage in range(2):
        base = 1 + 4 * stage
        for i in range(2):
            start(i, base, block(i, stage, 0, both), along(i, stage, 1))
            start(i, base + 1, block(i, stage, 0, both), along(i, stage, 3))
            if stage == 1:
                at = second_at[i]
                cross(i, 0, (both, both, at) if i == 0 else (both, at, both))
        for i in range(2):
            copy(i, base, block(i, stage, 3, both), other_seq).wait_recv()
            start(i, base + 2, block(i, stage, 3, 0), along(i, stage, 1))
            copy(i, base + 1, block(i, stage, 1, both), other_seq).wait_recv()
            start(i, base + 3, block(i, stage, 1, 1), along(i, stage, 3))
            if stage == 1:
                for k, shift in ((1, 3), (2, 1)):
                    at = lax.rem(second_at[i] + shift, LONG)
                    cross(i, k, (both, both, at) if i == 0 else (both, at, both))
        for i in range(2):
            copy(i, base + 2, block(i, stage, 2, 0), other_seq).wait_recv()
            copy(i, base + 3, block(i, stage, 2, 1), other_seq).wait_recv()
            if stage == 1:
                at = lax.rem(second_at[i] + 2, LONG)
                cross(i, 3, (both, both, at) if i == 0 else (both, at, both))

    for arriving, leaving in crossing:
        arriving.wait_recv()
        leaving.wait_send()
    for moved in started:
        moved.wait_send()
    for moved in swaps:
        moved.wait()


def gather_shards(shard_a, shard_b, x_own, pos_own):
    count = lax.axis_size("fsdp")
    chips = (count // (LONG * LONG * CORES), LONG, LONG, CORES)
    shards = (shard_a, shard_b)
    outs = [jax.ShapeDtypeStruct((*chips, *shard.shape), shard.dtype) for shard in shards]
    outs += [jax.ShapeDtypeStruct(array.shape, array.dtype) for array in (x_own, pos_own)]
    full_a, full_b, x_other, pos_other = pl.pallas_call(
        gather_kernel,
        out_shape=outs,
        in_specs=[ANY] * 4,
        out_specs=[ANY] * 4,
        scratch_shapes=[
            pltpu.SemaphoreType.DMA((2, 9)),
            pltpu.SemaphoreType.DMA((2, 9)),
            pltpu.SemaphoreType.DMA((2, 4)),
            pltpu.SemaphoreType.DMA((2, 4)),
            pltpu.SemaphoreType.DMA((2,)),
            pltpu.SemaphoreType.DMA((2,)),
            pltpu.SemaphoreType.DMA((2,)),
        ],
        compiler_params=pltpu.CompilerParams(collective_id=0, has_side_effects=True),
        name="gather_weights",
    )(shard_a, shard_b, x_own, pos_own)
    height = count * shard_a.shape[0]
    return (
        full_a.reshape(height, shard_a.shape[1]),
        full_b.reshape(height, shard_b.shape[1]),
        x_other,
        pos_other,
    )


def widen(values):
    return values.astype(jnp.float32)


def scatter_kernel(groups, *refs):
    number = len(groups)
    parts, totals = refs[:number], refs[number : 2 * number]
    halves, landed, second, landed_two, third, landed_three = (
        refs[k * number : (k + 1) * number] for k in range(2, 8)
    )
    core_send, core_recv, send, recv = refs[8 * number :]
    seq, y, x, z, core = coordinates()
    far_y = [
        device(seq, 1 - y, x, z, core),
        device(1 - seq, y, x, z, core),
        device(1 - seq, 1 - y, x, z, core),
    ]
    lines = [
        [device(seq, y, lax.rem(x + j, LONG), z, core) for j in (1, 2, 3)],
        [device(seq, y, x, lax.rem(z + j, LONG), core) for j in (1, 2, 3)],
    ]
    enter([device(seq, y, x, z, 1 - core)] + far_y + lines[0] + lines[1])

    def index(i, at):
        return (slice(None), slice(None), at) if groups[i] == 0 else (slice(None), at)

    first_at = [z if group == 0 else x for group in groups]
    second_at = [x if group == 0 else z for group in groups]
    first_line = [lines[1] if group == 0 else lines[0] for group in groups]
    second_line = [lines[0] if group == 0 else lines[1] for group in groups]

    def remote(source, target, to, sems, i, k):
        return pltpu.make_async_remote_copy(
            src_ref=source,
            dst_ref=target,
            send_sem=sems[0].at[i, k],
            recv_sem=sems[1].at[i, k],
            device_id=to,
            device_id_type=MESH,
        )

    def part_of(i, at, side):
        if groups[i] == 0:
            return parts[i].at[:, :, at, side]
        return parts[i].at[:, at, :, side]

    order = (2, 1, 3, 0)
    waiting = []
    across = {}
    for j in order:
        for i in range(number):
            at = lax.rem(first_at[i] + j, LONG)
            moved = remote(
                part_of(i, at, 1 - core),
                halves[i].at[j],
                device(seq, y, x, z, 1 - core),
                (core_send, core_recv),
                i,
                j,
            )
            moved.start()
            across[i, j] = moved
    for j in order:
        for i in range(number):
            across[i, j].wait_recv()
            at = lax.rem(first_at[i] + j, LONG)
            both = widen(halves[i][j]) + widen(part_of(i, at, core)[...])
            halves[i][j] = both.astype(jnp.bfloat16)
            if j:
                moved = remote(
                    halves[i].at[j],
                    landed[i].at[j - 1],
                    first_line[i][j - 1],
                    (send, recv),
                    i,
                    j - 1,
                )
                moved.start()
                waiting.append(moved)
    hops = {}
    for i in range(number):
        for j in (1, 2, 3):
            remote(halves[i].at[j], landed[i].at[j - 1], far_y[0], (send, recv), i, j - 1).wait_recv()
        total = widen(halves[i][0])
        for j in range(3):
            total = total + widen(landed[i][j])
        second[i][...] = total.astype(jnp.bfloat16)
        for j in (2, 1, 3):
            at = lax.rem(second_at[i] + j, LONG)
            moved = remote(
                second[i].at[:, at],
                landed_two[i].at[j - 1],
                second_line[i][j - 1],
                (send, recv),
                i,
                2 + j,
            )
            moved.start()
            waiting.append(moved)
            hops[i, j] = moved
    for i in range(number):
        for j in (1, 2, 3):
            hops[i, j].wait_recv()
        total = widen(second[i][:, second_at[i]])
        for j in range(3):
            total = total + widen(landed_two[i][j])
        third[i][...] = total.astype(jnp.bfloat16)
        landed_three[i][seq * 2 + y] = third[i][y]
        for k, wanted in enumerate((1 - y, y, 1 - y)):
            moved = remote(
                third[i].at[wanted],
                landed_three[i].at[seq * 2 + y],
                far_y[k],
                (send, recv),
                i,
                6 + k,
            )
            moved.start()
            waiting.append(moved)
            hops[i, 3 + k] = moved
    for i in range(number):
        for k in range(3):
            hops[i, 3 + k].wait_recv()
        total = widen(landed_three[i][0])
        for k in range(1, 4):
            total = total + widen(landed_three[i][k])
        totals[i][...] = total
    for moved in waiting:
        moved.wait_send()
    for i in range(number):
        for j in order:
            across[i, j].wait_send()


def scatter_sums(fulls, groups, identity):
    count = lax.axis_size("fsdp")
    number = len(fulls)
    rows = fulls[0].shape[0] // count
    widths = [full.shape[1] for full in fulls]
    ys = count // (LONG * LONG * CORES)
    parts = [full.reshape(ys, LONG, LONG, CORES, rows, full.shape[1]) for full in fulls]

    def room(*lead):
        return [pltpu.VMEM((*lead, rows, width), jnp.bfloat16) for width in widths]

    return pl.pallas_call(
        functools.partial(scatter_kernel, groups),
        out_shape=[jax.ShapeDtypeStruct((rows, width), jnp.float32) for width in widths],
        in_specs=[VMEM] * number,
        out_specs=[VMEM] * number,
        scratch_shapes=room(LONG, ys, LONG)
        + room(LONG - 1, ys, LONG)
        + room(ys, LONG)
        + room(LONG - 1, ys)
        + room(ys)
        + room(2 * ys)
        + [
            pltpu.SemaphoreType.DMA((number, LONG)),
            pltpu.SemaphoreType.DMA((number, LONG)),
            pltpu.SemaphoreType.DMA((number, 9)),
            pltpu.SemaphoreType.DMA((number, 9)),
        ],
        compiler_params=pltpu.CompilerParams(
            collective_id=identity, has_side_effects=True, vmem_limit_bytes=48 * 2**20
        ),
        name="scatter_gradients",
    )(*parts)


def exchange_rows(rows):
    slots = lax.axis_size("fsdp")
    blocks = rows.reshape(slots, rows.shape[0] // slots, *rows.shape[1:])
    return lax.all_to_all(blocks, "fsdp", split_axis=0, concat_axis=0, tiled=True).reshape(
        rows.shape
    )


def on_device(
    tokens,
    positions,
    routes,
    cotangent,
    first_gain,
    w_query,
    w_key,
    w_value,
    w_out,
    second_gain,
    w_router,
    w_gate,
    w_up,
    w_down,
):
    width = tokens.shape[2]
    rows = tokens.shape[1]
    heads_all = w_query.shape[1] // HD
    kv_all = w_key.shape[1] // HD
    group = heads_all // kv_all
    q_width, kv_width = heads_all * HD, kv_all * HD
    scale = HD ** (-0.5)
    slots = lax.axis_size("fsdp")
    experts = slots // CORES
    seq = lax.axis_index("seq")
    parity = lax.axis_index("fsdp") % CORES
    share = 24
    places = CORES * share

    x_own = tokens[0]

    own_gate, own_up, own_down = (w_gate[0], w_up[0], w_down[0])
    other_gate, other_up, other_down = from_partner((own_gate, own_up, own_down), "fsdp", 0)
    gate_full = join_halves(own_gate, other_gate, parity)
    up_full = join_halves(own_up, other_up, parity)
    down_full = join_halves(own_down, other_down, parity)

    chosen = routes[0]
    ids = jnp.arange(experts, dtype=jnp.int32)
    mask = jnp.any(chosen[:, :, None] == ids[None, None, :], axis=1)
    mask_low = mask.astype(jnp.bfloat16)
    earlier = (jnp.arange(rows)[:, None] > jnp.arange(rows)[None, :]).astype(jnp.bfloat16)
    rank = jnp.where(mask, dot_plain(earlier, mask_low).astype(jnp.int32), -1)
    onehot_wide = rank.T[:, None, :] == jnp.arange(places, dtype=jnp.int32)[None, :, None]
    onehot = onehot_wide.astype(jnp.bfloat16).reshape(experts * places, rows)

    grad_low = cotangent[0]
    grad_output = grad_low.astype(jnp.float32)
    beside = jnp.zeros((rows, SMALL - experts), jnp.bfloat16)
    early = jnp.concatenate([grad_low, mask_low, beside], axis=1)
    early_sent = dot_plain(onehot, early).astype(jnp.bfloat16)

    small = jnp.concatenate(
        [
            w_router,
            first_gain[:, None],
            second_gain[:, None],
            jnp.zeros((w_router.shape[0], SMALL - experts - 2), jnp.bfloat16),
        ],
        axis=1,
    )
    full_a, full_b, x_before, pos_before = gather_shards(
        jnp.concatenate([w_query, w_key], axis=1),
        jnp.concatenate([w_value, w_out, small], axis=1),
        x_own,
        positions,
    )
    early_sent, full_a = lax.optimization_barrier((early_sent, full_a))
    early_received = exchange_rows(early_sent)
    grad_received = early_received[:, :width]
    slot_mask = early_received[:, width : width + experts] > 0
    query_full, key_full = full_a[:, :q_width], full_a[:, q_width:]
    value_full = full_b[:, :kv_width]
    out_full = full_b[:, kv_width : kv_width + width]
    small_full = full_b[:, kv_width + width :]
    router_full = small_full[:, :experts]
    gain_first = small_full[:, experts].astype(jnp.float32)
    gain_second = small_full[:, experts + 1].astype(jnp.float32)

    x_both = jnp.concatenate([x_before, x_own], axis=0).astype(jnp.float32)
    pos_both = jnp.concatenate([pos_before[0], positions[0]], axis=0)
    inputs = x_both[rows:]
    inverse = rope_base ** (-(2.0 * jnp.arange(HD // 2, dtype=jnp.float32)) / HD)
    angle = pos_both.astype(jnp.float32)[:, None] * inverse[None, :]
    cosine = jnp.cos(angle)[:, None, :]
    sine_table = jnp.sin(angle)[:, None, :]
    inverse_one = lax.rsqrt(jnp.mean(x_both * x_both, axis=-1, keepdims=True) + epsilon)
    normed_both = (x_both * inverse_one * gain_first).astype(jnp.bfloat16)
    normed_own = normed_both[rows:]
    query_pre = dot_plain(normed_own, query_full).reshape(rows, heads_all, HD)
    key_pre = dot_plain(normed_both, key_full).reshape(2 * rows, kv_all, HD)
    query_rot = (rotate(query_pre, cosine[rows:], sine_table[rows:]) * scale).astype(jnp.bfloat16)
    keyed = rotate(key_pre, cosine, sine_table).astype(jnp.bfloat16)
    valued = dot_plain(normed_both, value_full).astype(jnp.bfloat16).reshape(2 * rows, kv_all, HD)
    grouped = query_rot.reshape(rows, kv_all, group, HD)
    key_at = jnp.arange(2 * rows)[None, :]
    allowed = (key_at - rows <= jnp.arange(rows)[:, None]) & ((key_at >= rows) | (seq == 1))
    scores = jnp.einsum("qkgd,pkd->kgqp", grouped, keyed, preferred_element_type=jnp.float32)
    scores = jnp.where(allowed, scores, masked_score)
    peak = jnp.max(scores, axis=-1, keepdims=True)
    raised = jnp.exp(scores - peak)
    probs = raised / jnp.sum(raised, axis=-1, keepdims=True)
    probs_low = probs.astype(jnp.bfloat16)
    attended = (
        jnp.einsum("kgqp,pkd->qkgd", probs_low, valued, preferred_element_type=jnp.float32)
        .astype(jnp.bfloat16)
        .reshape(rows, q_width)
    )
    middle = inputs + dot_plain(attended, out_full)

    inverse_two = lax.rsqrt(jnp.mean(middle * middle, axis=-1, keepdims=True) + epsilon)
    normed_two = (middle * inverse_two * gain_second).astype(jnp.bfloat16)
    expert_rows = exchange_rows(dot_plain(onehot, normed_two).astype(jnp.bfloat16))
    logits = jnp.where(mask, dot_plain(normed_two, router_full), masked_score)
    lifted = jnp.where(mask, jnp.exp(logits - jnp.max(logits, axis=-1, keepdims=True)), 0.0)
    gates = lifted / jnp.sum(lifted, axis=-1, keepdims=True)
    gates_wide = jnp.where(onehot_wide, gates.T[:, None, :], 0.0)

    own_expert = ids == lax.axis_index("fsdp") // CORES
    slot_logits = jnp.where(slot_mask, dot_plain(expert_rows, router_full), masked_score)
    slot_lifted = jnp.exp(slot_logits - jnp.max(slot_logits, axis=-1, keepdims=True))
    gate_slot = jnp.sum(
        jnp.where(slot_mask & own_expert, slot_lifted, 0.0), axis=-1, keepdims=True
    ) / jnp.sum(slot_lifted, axis=-1, keepdims=True)

    gate_pre = dot_plain(expert_rows, gate_full)
    up_pre = dot_plain(expert_rows, up_full)
    sigmoid_gate = jax.nn.sigmoid(gate_pre)
    silu_gate = gate_pre * sigmoid_gate
    hidden = (silu_gate * up_pre).astype(jnp.bfloat16)
    part_out = dot_plain(hidden, down_full).astype(jnp.bfloat16)
    returned = exchange_rows(part_out)

    grad_parts = (gate_slot * grad_received.astype(jnp.float32)).astype(jnp.bfloat16)
    grad_hidden = dot_right(grad_parts, down_full)
    grad_gate_pre = (
        grad_hidden * up_pre * sigmoid_gate * (1.0 + gate_pre * (1.0 - sigmoid_gate))
    ).astype(jnp.bfloat16)
    grad_up_pre = (grad_hidden * silu_gate).astype(jnp.bfloat16)
    grad_expert_rows = (
        dot_right(grad_gate_pre, gate_full) + dot_right(grad_up_pre, up_full)
    ).astype(jnp.bfloat16)
    grad_slots = exchange_rows(grad_expert_rows)

    def pair_sum(full):
        middle_row = full.shape[0] // 2
        mine = jnp.where(parity == 0, full[:middle_row], full[middle_row:])
        other = jnp.where(parity == 0, full[middle_row:], full[:middle_row]).astype(jnp.bfloat16)
        low = (mine + from_partner(other, "fsdp", 0).astype(jnp.float32)).astype(jnp.bfloat16)
        return low.astype(jnp.float32) + from_partner(low, "seq", 0).astype(jnp.float32)

    grad_down = pair_sum(dot_left(hidden, grad_parts))
    grad_gate = pair_sum(dot_left(expert_rows, grad_gate_pre))
    grad_up = pair_sum(dot_left(expert_rows, grad_up_pre))

    gates_high = gates_wide.astype(jnp.bfloat16)
    gates_rest = (gates_wide - gates_high.astype(jnp.float32)).astype(jnp.bfloat16)
    flat = (experts * places, rows)
    mixed = dot_left(gates_high.reshape(flat), returned) + dot_left(
        gates_rest.reshape(flat), returned
    )
    layer_out = (middle + mixed).astype(jnp.bfloat16)
    products = dot_right(returned, grad_low).reshape(experts, places, rows)
    grad_gates = jnp.sum(jnp.where(onehot_wide, products, 0.0), axis=1).T
    grad_picked = gates * (grad_gates - jnp.sum(gates * grad_gates, axis=-1, keepdims=True))
    grad_logits = grad_picked.astype(jnp.bfloat16)
    grad_router = dot_left(normed_two, grad_logits)
    grad_normed_two = dot_right(grad_logits, router_full) + dot_left(onehot, grad_slots)

    normed = middle * inverse_two
    scaled = grad_normed_two * gain_second
    grad_middle = grad_output + inverse_two * (
        scaled - normed * jnp.mean(scaled * normed, axis=-1, keepdims=True)
    )
    grad_gain_second = jnp.sum(grad_normed_two * normed, axis=0)
    grad_branch = grad_middle.astype(jnp.bfloat16)
    grad_out_full = dot_left(attended, grad_branch).astype(jnp.bfloat16)
    grad_heads = (
        dot_right(grad_branch, out_full).astype(jnp.bfloat16).reshape(rows, kv_all, group, HD)
    )
    grad_probs = jnp.einsum(
        "qkgd,pkd->kgqp", grad_heads, valued, preferred_element_type=jnp.float32
    )
    grad_scores = (
        probs * (grad_probs - jnp.sum(probs * grad_probs, axis=-1, keepdims=True))
    ).astype(jnp.bfloat16)
    grad_value_in = (
        jnp.einsum("kgqp,qkgd->pkd", probs_low, grad_heads, preferred_element_type=jnp.float32)
        .astype(jnp.bfloat16)
        .reshape(2 * rows, kv_width)
    )
    grad_query_rot = (
        jnp.einsum("kgqp,pkd->qkgd", grad_scores, keyed, preferred_element_type=jnp.float32)
        .astype(jnp.bfloat16)
        .astype(jnp.float32)
        .reshape(rows, heads_all, HD)
    )
    grad_key_rot = (
        jnp.einsum("kgqp,qkgd->pkd", grad_scores, grouped, preferred_element_type=jnp.float32)
        .astype(jnp.bfloat16)
        .astype(jnp.float32)
    )
    grad_query_in = (
        (rotate(grad_query_rot, cosine[rows:], -sine_table[rows:]) * scale)
        .astype(jnp.bfloat16)
        .reshape(rows, q_width)
    )
    grad_key_in = (
        rotate(grad_key_rot, cosine, -sine_table).astype(jnp.bfloat16).reshape(2 * rows, kv_width)
    )
    grad_query_full = dot_left(normed_own, grad_query_in).astype(jnp.bfloat16)
    grad_key_full = dot_left(normed_both, grad_key_in).astype(jnp.bfloat16)
    grad_value_full = dot_left(normed_both, grad_value_in).astype(jnp.bfloat16)
    grad_both = dot_right(grad_key_in, key_full) + dot_right(grad_value_in, value_full)
    grad_before = grad_both[:rows].astype(jnp.bfloat16)
    grad_after = lax.ppermute(grad_before, "seq", [(1, 0)]).astype(jnp.float32)
    grad_own = grad_both[rows:] + dot_right(grad_query_in, query_full)
    normed_x = x_both * inverse_one
    grad_gain_first = jnp.sum(grad_own * normed_x[rows:], axis=0) + jnp.sum(
        grad_both[:rows] * normed_x[:rows], axis=0
    )
    small_grad = jnp.concatenate(
        [
            grad_router,
            grad_gain_first[:, None],
            grad_gain_second[:, None],
            jnp.zeros((width, SMALL - experts - 2), jnp.float32),
        ],
        axis=1,
    ).astype(jnp.bfloat16)
    scaled_one = (grad_own + grad_after) * gain_first
    grad_tokens = grad_middle + inverse_one[rows:] * (
        scaled_one
        - normed_x[rows:] * jnp.mean(scaled_one * normed_x[rows:], axis=-1, keepdims=True)
    )

    sum_out, sum_key, sum_query, sum_value, sum_small = scatter_sums(
        [grad_out_full, grad_key_full, grad_query_full, grad_value_full, small_grad],
        (0, 0, 1, 1, 1),
        1,
    )
    return (
        layer_out[None],
        grad_tokens[None],
        sum_small[:, experts],
        sum_query,
        sum_key,
        sum_value,
        sum_out,
        sum_small[:, experts + 1],
        sum_small[:, :experts],
        grad_gate[None],
        grad_up[None],
        grad_down[None],
    )


def solution(mesh):
    rows = P("fsdp", "seq", None)
    matrix, cube = P("fsdp", None), P("fsdp", None, None)
    return jax.shard_map(
        on_device,
        mesh=mesh,
        in_specs=(
            rows,
            P("fsdp", "seq"),
            rows,
            rows,
            P("fsdp"),
            matrix,
            matrix,
            matrix,
            matrix,
            P("fsdp"),
            matrix,
            cube,
            cube,
            cube,
        ),
        out_specs=(
            rows,
            rows,
            P("fsdp"),
            matrix,
            matrix,
            matrix,
            matrix,
            P("fsdp"),
            matrix,
            cube,
            cube,
            cube,
        ),
        check_vma=False,
    )
```

```python
import functools

import jax
import jax.numpy as jnp
from jax import lax
from jax.experimental import pallas as pl
from jax.experimental.pallas import tpu as pltpu
from jax.sharding import PartitionSpec as P

HD = 64
CORES = 2
SMALL = 128

epsilon = 1e-06
rope_base = 10000.0
masked_score = -1e30
MESH = pl.DeviceIdType.MESH
ANY = pl.BlockSpec(memory_space=pl.ANY)
VMEM = pl.BlockSpec(memory_space=pltpu.VMEM)


def dot_plain(left, right):
    return jnp.dot(left, right, preferred_element_type=jnp.float32)


def dot_left(left, right):
    return lax.dot_general(
        left, right, (((0,), (0,)), ((), ())), preferred_element_type=jnp.float32
    )


def dot_right(left, right):
    return lax.dot_general(
        left, right, (((1,), (1,)), ((), ())), preferred_element_type=jnp.float32
    )


def rms_scale(values, gain):
    return values * lax.rsqrt(jnp.mean(values * values, axis=-1, keepdims=True) + epsilon) * gain


def in_two(values):
    high = lax.reduce_precision(values, 8, 7)
    return high.astype(jnp.bfloat16), (values - high).astype(jnp.bfloat16)


def rotate(values, cosine, sine_table):
    middle = values.shape[-1] // 2
    first_half = values[..., :middle]
    second_half = values[..., middle:]
    return jnp.concatenate(
        [
            first_half * cosine - second_half * sine_table,
            second_half * cosine + first_half * sine_table,
        ],
        axis=-1,
    )


LONG = 4


def coordinates():
    seq, me = lax.axis_index("seq"), lax.axis_index("fsdp")
    return seq, me // 32, (me // 8) % LONG, (me // 2) % LONG, me % CORES


def device(seq, y, x, z, core):
    return (seq, ((y * LONG + x) * LONG + z) * CORES + core)


def enter(targets):
    barrier = pltpu.get_barrier_semaphore()
    for target in targets:
        pl.semaphore_signal(barrier, inc=1, device_id=target, device_id_type=MESH)
    pl.semaphore_wait(barrier, len(targets))


def neighbours():
    seq, y, x, z, core = coordinates()
    return [
        device(seq, y, x, z, 1 - core),
        device(seq, 1 - y, x, z, core),
        device(seq, y, lax.rem(x + 1, LONG), z, core),
        device(seq, y, lax.rem(x + 3, LONG), z, core),
        device(seq, y, x, lax.rem(z + 1, LONG), core),
        device(seq, y, x, lax.rem(z + 3, LONG), core),
        device(1 - seq, y, x, z, core),
    ]


def gather_kernel(shard_a, shard_b, x_own, pos_own, full_a, full_b, x_other, pos_other, *sems):
    send, recv, core_send, core_recv, seq_send, seq_recv, local = sems
    seq, y, x, z, core = coordinates()
    enter(neighbours())
    other_seq = device(1 - seq, y, x, z, core)
    swaps = [
        pltpu.make_async_remote_copy(
            src_ref=source,
            dst_ref=target,
            send_sem=seq_send.at[i],
            recv_sem=seq_recv.at[i],
            device_id=other_seq,
            device_id_type=MESH,
        )
        for i, (source, target) in enumerate(((x_own, x_other), (pos_own, pos_other)))
    ]
    fulls = (full_a, full_b)
    first_at, second_at = (x, z), (z, x)

    def along(i, stage, shift):
        if (i == 0) == (stage == 0):
            return device(seq, y, lax.rem(x + shift, LONG), z, core)
        return device(seq, y, x, lax.rem(z + shift, LONG), core)

    def block(i, stage, shift, ys):
        at = lax.rem((first_at if stage == 0 else second_at)[i] + shift, LONG)
        if stage == 0:
            xs, zs = (at, z) if i == 0 else (x, at)
        else:
            xs, zs = (slice(None), at) if i == 0 else (at, slice(None))
        return fulls[i].at[ys, xs, zs, core]

    def copy(i, k, part, target):
        return pltpu.make_async_remote_copy(
            src_ref=part,
            dst_ref=part,
            send_sem=send.at[i, k],
            recv_sem=recv.at[i, k],
            device_id=target,
            device_id_type=MESH,
        )

    both = slice(None)
    own = []
    started = []

    def start(i, k, part, target):
        moved = copy(i, k, part, target)
        moved.start()
        started.append(moved)

    crossing = []

    def cross(i, k, index):
        for side, wait in ((core, False), (1 - core, True)):
            part = fulls[i].at[(*index, side)]
            moved = pltpu.make_async_remote_copy(
                src_ref=part,
                dst_ref=part,
                send_sem=core_send.at[i, k],
                recv_sem=core_recv.at[i, k],
                device_id=device(seq, y, x, z, 1 - core),
                device_id_type=MESH,
            )
            if wait:
                crossing.append((moved, last))
            else:
                moved.start()
                last = moved

    for i, shard in enumerate((shard_a, shard_b)):
        kept = pltpu.make_async_copy(shard, fulls[i].at[y, x, z, core], local.at[i])
        kept.start()
        own.append(kept)
        outgoing = pltpu.make_async_remote_copy(
            src_ref=shard,
            dst_ref=fulls[i].at[y, x, z, core],
            send_sem=send.at[i, 0],
            recv_sem=recv.at[i, 0],
            device_id=device(seq, 1 - y, x, z, core),
            device_id_type=MESH,
        )
        outgoing.start()
        started.append(outgoing)
    for moved in swaps:
        moved.start()
    for i in range(2):
        own[i].wait()
        copy(i, 0, fulls[i].at[1 - y, x, z, core], other_seq).wait_recv()

    for stage in range(2):
        base = 1 + 4 * stage
        for i in range(2):
            start(i, base, block(i, stage, 0, both), along(i, stage, 1))
            start(i, base + 1, block(i, stage, 0, both), along(i, stage, 3))
            if stage == 1:
                at = second_at[i]
                cross(i, 0, (both, both, at) if i == 0 else (both, at, both))
        for i in range(2):
            copy(i, base, block(i, stage, 3, both), other_seq).wait_recv()
            start(i, base + 2, block(i, stage, 3, 0), along(i, stage, 1))
            copy(i, base + 1, block(i, stage, 1, both), other_seq).wait_recv()
            start(i, base + 3, block(i, stage, 1, 1), along(i, stage, 3))
            if stage == 1:
                for k, shift in ((1, 3), (2, 1)):
                    at = lax.rem(second_at[i] + shift, LONG)
                    cross(i, k, (both, both, at) if i == 0 else (both, at, both))
        for i in range(2):
            copy(i, base + 2, block(i, stage, 2, 0), other_seq).wait_recv()
            copy(i, base + 3, block(i, stage, 2, 1), other_seq).wait_recv()
            if stage == 1:
                at = lax.rem(second_at[i] + 2, LONG)
                cross(i, 3, (both, both, at) if i == 0 else (both, at, both))

    for arriving, leaving in crossing:
        arriving.wait_recv()
        leaving.wait_send()
    for moved in started:
        moved.wait_send()
    for moved in swaps:
        moved.wait()


def gather_shards(shard_a, shard_b, x_own, pos_own):
    count = lax.axis_size("fsdp")
    chips = (count // (LONG * LONG * CORES), LONG, LONG, CORES)
    shards = (shard_a, shard_b)
    outs = [jax.ShapeDtypeStruct((*chips, *shard.shape), shard.dtype) for shard in shards]
    outs += [jax.ShapeDtypeStruct(array.shape, array.dtype) for array in (x_own, pos_own)]
    full_a, full_b, x_other, pos_other = pl.pallas_call(
        gather_kernel,
        out_shape=outs,
        in_specs=[ANY] * 4,
        out_specs=[ANY] * 4,
        scratch_shapes=[
            pltpu.SemaphoreType.DMA((2, 9)),
            pltpu.SemaphoreType.DMA((2, 9)),
            pltpu.SemaphoreType.DMA((2, 4)),
            pltpu.SemaphoreType.DMA((2, 4)),
            pltpu.SemaphoreType.DMA((2,)),
            pltpu.SemaphoreType.DMA((2,)),
            pltpu.SemaphoreType.DMA((2,)),
        ],
        compiler_params=pltpu.CompilerParams(collective_id=0, has_side_effects=True),
        name="gather_weights",
    )(shard_a, shard_b, x_own, pos_own)
    height = count * shard_a.shape[0]
    return (
        full_a.reshape(height, shard_a.shape[1]),
        full_b.reshape(height, shard_b.shape[1]),
        x_other,
        pos_other,
    )


def widen(values):
    return values.astype(jnp.float32)


def scatter_kernel(groups, *refs):
    number = len(groups)
    parts, totals = refs[:number], refs[number : 2 * number]
    halves, landed, second, landed_two, third, landed_three = (
        refs[k * number : (k + 1) * number] for k in range(2, 8)
    )
    core_send, core_recv, send, recv = refs[8 * number :]
    seq, y, x, z, core = coordinates()
    far_y = [
        device(seq, 1 - y, x, z, core),
        device(1 - seq, y, x, z, core),
        device(1 - seq, 1 - y, x, z, core),
    ]
    lines = [
        [device(seq, y, lax.rem(x + j, LONG), z, core) for j in (1, 2, 3)],
        [device(seq, y, x, lax.rem(z + j, LONG), core) for j in (1, 2, 3)],
    ]
    enter([device(seq, y, x, z, 1 - core)] + far_y + lines[0] + lines[1])

    def index(i, at):
        return (slice(None), slice(None), at) if groups[i] == 0 else (slice(None), at)

    first_at = [z if group == 0 else x for group in groups]
    second_at = [x if group == 0 else z for group in groups]
    first_line = [lines[1] if group == 0 else lines[0] for group in groups]
    second_line = [lines[0] if group == 0 else lines[1] for group in groups]

    def remote(source, target, to, sems, i, k):
        return pltpu.make_async_remote_copy(
            src_ref=source,
            dst_ref=target,
            send_sem=sems[0].at[i, k],
            recv_sem=sems[1].at[i, k],
            device_id=to,
            device_id_type=MESH,
        )

    def part_of(i, at, side):
        if groups[i] == 0:
            return parts[i].at[:, :, at, side]
        return parts[i].at[:, at, :, side]

    order = (2, 1, 3, 0)
    waiting = []
    across = {}
    for j in order:
        for i in range(number):
            at = lax.rem(first_at[i] + j, LONG)
            moved = remote(
                part_of(i, at, 1 - core),
                halves[i].at[j],
                device(seq, y, x, z, 1 - core),
                (core_send, core_recv),
                i,
                j,
            )
            moved.start()
            across[i, j] = moved
    for j in order:
        for i in range(number):
            across[i, j].wait_recv()
            at = lax.rem(first_at[i] + j, LONG)
            both = widen(halves[i][j]) + widen(part_of(i, at, core)[...])
            halves[i][j] = both.astype(jnp.bfloat16)
            if j:
                moved = remote(
                    halves[i].at[j],
                    landed[i].at[j - 1],
                    first_line[i][j - 1],
                    (send, recv),
                    i,
                    j - 1,
                )
                moved.start()
                waiting.append(moved)
    hops = {}
    for i in range(number):
        for j in (1, 2, 3):
            remote(halves[i].at[j], landed[i].at[j - 1], far_y[0], (send, recv), i, j - 1).wait_recv()
        total = widen(halves[i][0])
        for j in range(3):
            total = total + widen(landed[i][j])
        second[i][...] = total.astype(jnp.bfloat16)
        for j in (2, 1, 3):
            at = lax.rem(second_at[i] + j, LONG)
            moved = remote(
                second[i].at[:, at],
                landed_two[i].at[j - 1],
                second_line[i][j - 1],
                (send, recv),
                i,
                2 + j,
            )
            moved.start()
            waiting.append(moved)
            hops[i, j] = moved
    for i in range(number):
        for j in (1, 2, 3):
            hops[i, j].wait_recv()
        total = widen(second[i][:, second_at[i]])
        for j in range(3):
            total = total + widen(landed_two[i][j])
        third[i][...] = total.astype(jnp.bfloat16)
        landed_three[i][seq * 2 + y] = third[i][y]
        for k, wanted in enumerate((1 - y, y, 1 - y)):
            moved = remote(
                third[i].at[wanted],
                landed_three[i].at[seq * 2 + y],
                far_y[k],
                (send, recv),
                i,
                6 + k,
            )
            moved.start()
            waiting.append(moved)
            hops[i, 3 + k] = moved
    for i in range(number):
        for k in range(3):
            hops[i, 3 + k].wait_recv()
        total = widen(landed_three[i][0])
        for k in range(1, 4):
            total = total + widen(landed_three[i][k])
        totals[i][...] = total
    for moved in waiting:
        moved.wait_send()
    for i in range(number):
        for j in order:
            across[i, j].wait_send()


def scatter_sums(fulls, groups, identity):
    count = lax.axis_size("fsdp")
    number = len(fulls)
    rows = fulls[0].shape[0] // count
    widths = [full.shape[1] for full in fulls]
    ys = count // (LONG * LONG * CORES)
    parts = [full.reshape(ys, LONG, LONG, CORES, rows, full.shape[1]) for full in fulls]

    def room(*lead):
        return [pltpu.VMEM((*lead, rows, width), jnp.bfloat16) for width in widths]

    return pl.pallas_call(
        functools.partial(scatter_kernel, groups),
        out_shape=[jax.ShapeDtypeStruct((rows, width), jnp.float32) for width in widths],
        in_specs=[VMEM] * number,
        out_specs=[VMEM] * number,
        scratch_shapes=room(LONG, ys, LONG)
        + room(LONG - 1, ys, LONG)
        + room(ys, LONG)
        + room(LONG - 1, ys)
        + room(ys)
        + room(2 * ys)
        + [
            pltpu.SemaphoreType.DMA((number, LONG)),
            pltpu.SemaphoreType.DMA((number, LONG)),
            pltpu.SemaphoreType.DMA((number, 9)),
            pltpu.SemaphoreType.DMA((number, 9)),
        ],
        compiler_params=pltpu.CompilerParams(
            collective_id=identity, has_side_effects=True, vmem_limit_bytes=48 * 2**20
        ),
        name="scatter_gradients",
    )(*parts)


CHUNKS = 4
SAME, CROSS = 32, 16
BLOCK = SAME + CROSS


def chip_at(sign, step):
    seq, y, x, z, core = coordinates()
    chunk, inner = step // 8, step % 8
    dy, dx = inner // LONG, inner % LONG
    dz = (dx + chunk) % LONG
    return ((y + dy) % 2 * LONG + (x + sign * dx + LONG) % LONG) * LONG + (
        z + sign * dz + LONG
    ) % LONG


def expert_kernel(
    onehot,
    gates,
    normed,
    grad_low,
    own_gate,
    own_up,
    own_down,
    out_ref,
    back_ref,
    dots_ref,
    d_gate,
    d_up,
    d_down,
    picks,
    x_send,
    g_send,
    x_land,
    g_land,
    out_rows,
    back_land,
    gate_pre,
    up_pre,
    hidden,
    d_gate_pre,
    d_up_pre,
    w_gate,
    w_up,
    w_down,
    pair_send,
    pair_land,
    pair_send_down,
    pair_land_down,
    seq_send,
    seq_land,
    seq_send_down,
    seq_land_down,
    x_sems,
    g_sems,
    back_sems,
    self_sems,
    out_sems,
    weight_sems,
    sum_sems,
):
    seq, y, x, z, core = coordinates()
    me = lax.axis_index("fsdp")
    width = normed.shape[1]
    chips = onehot.shape[0]
    steps = chips // CHUNKS
    depth = steps * BLOCK
    partner = (seq, me + 1 - 2 * core)
    other_seq = (1 - seq, me)

    barrier = pltpu.get_barrier_semaphore()
    for target in (partner, other_seq):
        pl.semaphore_signal(barrier, inc=1, device_id=target, device_id_type=MESH)

    @pl.loop(1, chips)
    def _(step):
        for side in range(CORES):
            pl.semaphore_signal(
                barrier,
                inc=1,
                device_id=(seq, chip_at(-1, step) * CORES + side),
                device_id_type=MESH,
            )

    pl.semaphore_wait(barrier, CORES * chips)

    def remote(source, target, sends, recvs, to):
        return pltpu.make_async_remote_copy(
            src_ref=source,
            dst_ref=target,
            send_sem=sends,
            recv_sem=recvs,
            device_id=to,
            device_id_type=MESH,
        )

    weights = []
    for i, (own, full) in enumerate(((own_gate, w_gate), (own_up, w_up), (own_down, w_down))):
        height = own.shape[0]
        place = full.at[pl.ds(pl.multiple_of(core * height, height), height)]
        kept = pltpu.make_async_copy(own, place, weight_sems.at[2, i])
        sent = remote(own, place, weight_sems.at[0, i], weight_sems.at[1, i], partner)
        kept.start()
        sent.start()
        weights.append((kept, sent))

    def send_block(source, target, sems, kind, sign, step):
        chip = chip_at(sign, step)
        chunk = step // steps
        row = pl.multiple_of(step * BLOCK, 16)
        same, cross = pl.ds(row, SAME), pl.ds(pl.multiple_of(row + SAME, 16), CROSS)

        @pl.when(step == 0)
        def _():
            pltpu.make_async_copy(source.at[same], target.at[same], self_sems.at[kind]).start()

        @pl.when(step > 0)
        def _():
            remote(
                source.at[same],
                target.at[same],
                sems.at[0, chunk],
                sems.at[1, chunk],
                (seq, chip * CORES + core),
            ).start()

        remote(
            source.at[cross],
            target.at[cross],
            sems.at[0, chunk],
            sems.at[1, chunk],
            (seq, chip * CORES + 1 - core),
        ).start()

    def whole(buffer, sems, chunk, first):
        rows = pl.ds(SAME, depth - SAME) if first else pl.ds(pl.multiple_of(chunk * depth, 16), depth)
        part = buffer.at[rows]
        return remote(part, part, sems.at[0, chunk], sems.at[1, chunk], partner)

    def wait_chunk(source, target, sems, kind, chunk):
        @pl.when(chunk == 0)
        def _():
            pltpu.make_async_copy(
                source.at[pl.ds(0, SAME)], target.at[pl.ds(0, SAME)], self_sems.at[kind]
            ).wait()
            whole(target, sems, 0, True).wait_recv()

        @pl.when(chunk > 0)
        def _():
            whole(target, sems, chunk, False).wait_recv()

    def wait_sends(source, sems):
        for chunk in range(CHUNKS):
            whole(source, sems, chunk, chunk == 0).wait_send()

    @pl.loop(0, chips)
    def _(step):
        chip = chip_at(1, step)
        rows = pl.ds(pl.multiple_of(step * BLOCK, 16), BLOCK)
        picks[rows, :] = onehot[chip]
        x_send[rows, width:] = gates[chip]

    for values, buffer, target, sems, kind in (
        (normed, x_send, x_land, x_sems, 0),
        (grad_low, g_send, g_land, g_sems, 1),
    ):

        @pl.loop(0, CHUNKS)
        def _(chunk):
            rows = pl.ds(pl.multiple_of(chunk * depth, 16), depth)
            buffer[rows, :width] = dot_plain(picks[rows, :], values[...]).astype(jnp.bfloat16)

            @pl.loop(0, steps)
            def _(inner):
                send_block(buffer, target, sems, kind, 1, chunk * steps + inner)

    for kept, sent in weights:
        kept.wait()
        sent.wait()

    @pl.loop(0, CHUNKS)
    def _(chunk):
        rows = pl.ds(pl.multiple_of(chunk * depth, 16), depth)
        wait_chunk(x_send, x_land, x_sems, 0, chunk)
        served = x_land[rows, :width]
        gate = dot_plain(served, w_gate[...])
        up = dot_plain(served, w_up[...])
        gate_pre[rows, :] = gate
        up_pre[rows, :] = up
        low = (gate * jax.nn.sigmoid(gate) * up).astype(jnp.bfloat16)
        hidden[rows, :] = low
        out_rows[rows, :] = dot_plain(low, w_down[...]).astype(jnp.bfloat16)

        @pl.loop(0, steps)
        def _(inner):
            step = chunk * steps + inner
            row = pl.multiple_of(step * BLOCK, 16)
            chip = chip_at(-1, step)
            out_ref[chip, :SAME, :] = out_rows[pl.ds(row, SAME), :]
            remote(
                out_rows.at[pl.ds(pl.multiple_of(row + SAME, 16), CROSS)],
                out_ref.at[chip, pl.ds(SAME, CROSS)],
                out_sems.at[0],
                out_sems.at[1],
                partner,
            ).start()

    wait_sends(x_send, x_sems)

    @pl.loop(0, CHUNKS)
    def _(chunk):
        rows = pl.ds(pl.multiple_of(chunk * depth, 16), depth)
        wait_chunk(g_send, g_land, g_sems, 1, chunk)
        grads = g_land[rows, :].astype(jnp.float32)
        dots = jnp.sum(grads * out_rows[rows, :].astype(jnp.float32), axis=1, keepdims=True)
        high = dots.astype(jnp.bfloat16).astype(jnp.float32)
        lane = lax.broadcasted_iota(jnp.int32, (depth, SMALL), 1)
        x_send[rows, width:] = jnp.where(
            lane == 0, high, jnp.where(lane == 1, dots - high, 0.0)
        ).astype(jnp.bfloat16)
        weight = jnp.sum(x_land[rows, width:].astype(jnp.float32), axis=1, keepdims=True)
        low = (weight * grads).astype(jnp.bfloat16)
        g_land[rows, :] = low
        d_hidden = dot_right(low, w_down[...])
        gate, up = gate_pre[rows, :], up_pre[rows, :]
        sigmoid = jax.nn.sigmoid(gate)
        one = (d_hidden * up * sigmoid * (1.0 + gate * (1.0 - sigmoid))).astype(jnp.bfloat16)
        two = (d_hidden * (gate * sigmoid)).astype(jnp.bfloat16)
        d_gate_pre[rows, :] = one
        d_up_pre[rows, :] = two
        x_send[rows, :width] = (dot_right(one, w_gate[...]) + dot_right(two, w_up[...])).astype(
            jnp.bfloat16
        )

        @pl.loop(0, steps)
        def _(inner):
            send_block(x_send, back_land, back_sems, 2, -1, chunk * steps + inner)

    tile = 256
    half = own_gate.shape[0]
    half_down = own_down.shape[0]

    def product(side, which, at):
        start = pl.multiple_of(side * half + at * tile, tile)
        return dot_left(x_land[:, pl.ds(start, tile)], (d_gate_pre, d_up_pre)[which][...])

    def product_down(side, at):
        start = pl.multiple_of(side * half_down, half_down)
        columns = pl.ds(pl.multiple_of(at * half, half), half)
        return dot_left(hidden[:, pl.ds(start, half_down)], g_land[:, columns]), columns

    def both_tiles(side, keep):
        @pl.loop(0, half // tile)
        def _(at):
            for which in range(2):
                keep(which, pl.ds(pl.multiple_of(at * tile, tile), tile), product(side, which, at))

    def keep_other(which, rows, values):
        pair_send[which, rows, :] = values.astype(jnp.bfloat16)

    def keep_own(which, rows, values):
        (d_gate, d_up)[which][rows, :] = values

    both_tiles(1 - core, keep_other)

    @pl.loop(0, width // half)
    def _(at):
        values, columns = product_down(1 - core, at)
        pair_send_down[:, columns] = values.astype(jnp.bfloat16)

    pairs = [
        remote(pair_send, pair_land, sum_sems.at[0, 0], sum_sems.at[1, 0], partner),
        remote(pair_send_down, pair_land_down, sum_sems.at[0, 1], sum_sems.at[1, 1], partner),
    ]
    for moved in pairs:
        moved.start()
    both_tiles(core, keep_own)

    @pl.loop(0, width // half)
    def _(at):
        values, columns = product_down(core, at)
        d_down[:, columns] = values

    pairs[0].wait_recv()
    for which, mine in enumerate((d_gate, d_up)):
        seq_send[which] = (mine[...] + pair_land[which].astype(jnp.float32)).astype(jnp.bfloat16)
    pairs[1].wait_recv()
    seq_send_down[...] = (d_down[...] + pair_land_down[...].astype(jnp.float32)).astype(
        jnp.bfloat16
    )
    sums = [
        remote(seq_send, seq_land, sum_sems.at[0, 2], sum_sems.at[1, 2], other_seq),
        remote(seq_send_down, seq_land_down, sum_sems.at[0, 3], sum_sems.at[1, 3], other_seq),
    ]
    for moved in sums:
        moved.start()

    back_ref[...] = jnp.zeros_like(back_ref)

    @pl.loop(0, CHUNKS)
    def _(chunk):
        rows = pl.ds(pl.multiple_of(chunk * depth, 16), depth)
        wait_chunk(x_send, back_land, back_sems, 2, chunk)
        back_ref[...] += dot_left(picks[rows, :], back_land[rows, :width])

    @pl.loop(0, chips)
    def _(step):
        rows = pl.ds(pl.multiple_of(step * BLOCK, 16), BLOCK)
        dots_ref[chip_at(1, step)] = back_land[rows, width:]

    sums[0].wait_recv()
    for which, mine in enumerate((d_gate, d_up)):
        mine[...] = seq_send[which].astype(jnp.float32) + seq_land[which].astype(jnp.float32)
    sums[1].wait_recv()
    d_down[...] = seq_send_down[...].astype(jnp.float32) + seq_land_down[...].astype(jnp.float32)
    outs = out_rows.at[pl.ds(0, chips * CROSS)]
    remote(outs, outs, out_sems.at[0], out_sems.at[1], partner).wait()
    wait_sends(g_send, g_sems)
    wait_sends(x_send, back_sems)
    for moved in pairs + sums:
        moved.wait_send()


def run_experts(onehot, gates, normed, grad_low, own_gate, own_up, own_down):
    chips, _, rows = onehot.shape
    width, hidden = normed.shape[1], own_gate.shape[1]
    slots = chips * BLOCK
    low, high = jnp.bfloat16, jnp.float32
    dma = pltpu.SemaphoreType.DMA
    half, half_down = own_gate.shape[0], own_down.shape[0]
    return pl.pallas_call(
        expert_kernel,
        out_shape=[
            jax.ShapeDtypeStruct((chips, BLOCK, width), low),
            jax.ShapeDtypeStruct((rows, width), high),
            jax.ShapeDtypeStruct((chips, BLOCK, SMALL), low),
            jax.ShapeDtypeStruct(own_gate.shape, high),
            jax.ShapeDtypeStruct(own_up.shape, high),
            jax.ShapeDtypeStruct(own_down.shape, high),
        ],
        in_specs=[VMEM] * 7,
        out_specs=[VMEM] * 6,
        scratch_shapes=[
            pltpu.VMEM((slots, rows), low),
            pltpu.VMEM((slots, width + SMALL), low),
            pltpu.VMEM((slots, width), low),
            pltpu.VMEM((slots, width + SMALL), low),
            pltpu.VMEM((slots, width), low),
            pltpu.VMEM((slots, width), low),
            pltpu.VMEM((slots, width + SMALL), low),
            pltpu.VMEM((slots, hidden), high),
            pltpu.VMEM((slots, hidden), high),
            pltpu.VMEM((slots, hidden), low),
            pltpu.VMEM((slots, hidden), low),
            pltpu.VMEM((slots, hidden), low),
            pltpu.VMEM((CORES * half, hidden), low),
            pltpu.VMEM((CORES * half, hidden), low),
            pltpu.VMEM((CORES * half_down, width), low),
            pltpu.VMEM((2, half, hidden), low),
            pltpu.VMEM((2, half, hidden), low),
            pltpu.VMEM((half_down, width), low),
            pltpu.VMEM((half_down, width), low),
            pltpu.VMEM((2, half, hidden), low),
            pltpu.VMEM((2, half, hidden), low),
            pltpu.VMEM((half_down, width), low),
            pltpu.VMEM((half_down, width), low),
            dma((2, CHUNKS)),
            dma((2, CHUNKS)),
            dma((2, CHUNKS)),
            dma((3,)),
            dma((2,)),
            dma((3, 3)),
            dma((2, 4)),
        ],
        compiler_params=pltpu.CompilerParams(
            collective_id=2, has_side_effects=True, vmem_limit_bytes=60 * 2**20
        ),
        name="experts",
    )(onehot, gates, normed, grad_low, own_gate, own_up, own_down)


def from_experts(blocks):
    groups = [
        [chip * CORES + core for chip in range(blocks.shape[0])] for core in range(CORES)
    ]
    return lax.all_to_all(
        blocks, "fsdp", split_axis=0, concat_axis=0, tiled=True, axis_index_groups=groups
    )


def on_device(
    tokens,
    positions,
    routes,
    cotangent,
    first_gain,
    w_query,
    w_key,
    w_value,
    w_out,
    second_gain,
    w_router,
    w_gate,
    w_up,
    w_down,
):
    width = tokens.shape[2]
    rows = tokens.shape[1]
    heads_all = w_query.shape[1] // HD
    kv_all = w_key.shape[1] // HD
    group = heads_all // kv_all
    q_width, kv_width = heads_all * HD, kv_all * HD
    scale = HD ** (-0.5)
    slots = lax.axis_size("fsdp")
    experts = slots // CORES
    seq = lax.axis_index("seq")
    places = BLOCK

    x_own = tokens[0]

    chosen = routes[0]
    ids = jnp.arange(experts, dtype=jnp.int32)
    mask = jnp.any(chosen[:, :, None] == ids[None, None, :], axis=1)
    mask_low = mask.astype(jnp.bfloat16)
    earlier = (jnp.arange(rows)[:, None] > jnp.arange(rows)[None, :]).astype(jnp.bfloat16)
    rank = jnp.where(mask, dot_plain(earlier, mask_low).astype(jnp.int32), -1)
    onehot_wide = rank.T[:, None, :] == jnp.arange(places, dtype=jnp.int32)[None, :, None]
    onehot = onehot_wide.astype(jnp.bfloat16).reshape(experts * places, rows)

    grad_low = cotangent[0]
    grad_output = grad_low.astype(jnp.float32)

    small = jnp.concatenate(
        [
            w_router,
            first_gain[:, None],
            second_gain[:, None],
            jnp.zeros((w_router.shape[0], SMALL - experts - 2), jnp.bfloat16),
        ],
        axis=1,
    )
    full_a, full_b, x_before, pos_before = gather_shards(
        jnp.concatenate([w_query, w_key], axis=1),
        jnp.concatenate([w_value, w_out, small], axis=1),
        x_own,
        positions,
    )
    query_full, key_full = full_a[:, :q_width], full_a[:, q_width:]
    value_full = full_b[:, :kv_width]
    out_full = full_b[:, kv_width : kv_width + width]
    small_full = full_b[:, kv_width + width :]
    router_full = small_full[:, :experts]
    gain_first = small_full[:, experts].astype(jnp.float32)
    gain_second = small_full[:, experts + 1].astype(jnp.float32)

    x_both = jnp.concatenate([x_before, x_own], axis=0).astype(jnp.float32)
    pos_both = jnp.concatenate([pos_before[0], positions[0]], axis=0)
    inputs = x_both[rows:]
    inverse = rope_base ** (-(2.0 * jnp.arange(HD // 2, dtype=jnp.float32)) / HD)
    angle = pos_both.astype(jnp.float32)[:, None] * inverse[None, :]
    cosine = jnp.cos(angle)[:, None, :]
    sine_table = jnp.sin(angle)[:, None, :]
    inverse_one = lax.rsqrt(jnp.mean(x_both * x_both, axis=-1, keepdims=True) + epsilon)
    normed_both = (x_both * inverse_one * gain_first).astype(jnp.bfloat16)
    normed_own = normed_both[rows:]
    query_pre = dot_plain(normed_own, query_full).reshape(rows, heads_all, HD)
    key_pre = dot_plain(normed_both, key_full).reshape(2 * rows, kv_all, HD)
    query_rot = (rotate(query_pre, cosine[rows:], sine_table[rows:]) * scale).astype(jnp.bfloat16)
    keyed = rotate(key_pre, cosine, sine_table).astype(jnp.bfloat16)
    valued = dot_plain(normed_both, value_full).astype(jnp.bfloat16).reshape(2 * rows, kv_all, HD)
    grouped = query_rot.reshape(rows, kv_all, group, HD)
    key_at = jnp.arange(2 * rows)[None, :]
    allowed = (key_at - rows <= jnp.arange(rows)[:, None]) & ((key_at >= rows) | (seq == 1))
    scores = jnp.einsum("qkgd,pkd->kgqp", grouped, keyed, preferred_element_type=jnp.float32)
    scores = jnp.where(allowed, scores, masked_score)
    peak = jnp.max(scores, axis=-1, keepdims=True)
    raised = jnp.exp(scores - peak)
    probs = raised / jnp.sum(raised, axis=-1, keepdims=True)
    probs_low = probs.astype(jnp.bfloat16)
    attended = (
        jnp.einsum("kgqp,pkd->qkgd", probs_low, valued, preferred_element_type=jnp.float32)
        .astype(jnp.bfloat16)
        .reshape(rows, q_width)
    )
    middle = inputs + dot_plain(attended, out_full)

    inverse_two = lax.rsqrt(jnp.mean(middle * middle, axis=-1, keepdims=True) + epsilon)
    normed_two = (middle * inverse_two * gain_second).astype(jnp.bfloat16)
    logits = jnp.where(mask, dot_plain(normed_two, router_full), masked_score)
    lifted = jnp.where(mask, jnp.exp(logits - jnp.max(logits, axis=-1, keepdims=True)), 0.0)
    gates = lifted / jnp.sum(lifted, axis=-1, keepdims=True)
    gates_wide = jnp.where(onehot_wide, gates.T[:, None, :], 0.0)
    gate_slots = jnp.sum(gates_wide, axis=-1, keepdims=True)
    gate_high, gate_rest = in_two(gate_slots)
    gates_sent = jnp.pad(
        jnp.concatenate([gate_high, gate_rest], axis=2), ((0, 0), (0, 0), (0, SMALL - 2))
    )

    part_out, grad_routed, dots, grad_gate, grad_up, grad_down = run_experts(
        onehot.reshape(experts, places, rows),
        gates_sent,
        normed_two,
        grad_low,
        w_gate[0],
        w_up[0],
        w_down[0],
    )
    returned = from_experts(part_out).reshape(experts * places, width)

    gates_high, gates_rest = in_two(gates_wide)
    flat = (experts * places, rows)
    mixed = dot_left(gates_high.reshape(flat), returned) + dot_left(
        gates_rest.reshape(flat), returned
    )
    layer_out = (middle + mixed).astype(jnp.bfloat16)
    dot_slots = dots[:, :, 0:1].astype(jnp.float32) + dots[:, :, 1:2].astype(jnp.float32)
    grad_gates = jnp.sum(jnp.where(onehot_wide, dot_slots, 0.0), axis=1).T
    grad_picked = gates * (grad_gates - jnp.sum(gates * grad_gates, axis=-1, keepdims=True))
    grad_logits = grad_picked.astype(jnp.bfloat16)
    grad_router = dot_left(normed_two, grad_logits)
    grad_normed_two = dot_right(grad_logits, router_full) + grad_routed

    normed = middle * inverse_two
    scaled = grad_normed_two * gain_second
    grad_middle = grad_output + inverse_two * (
        scaled - normed * jnp.mean(scaled * normed, axis=-1, keepdims=True)
    )
    grad_gain_second = jnp.sum(grad_normed_two * normed, axis=0)
    grad_branch = grad_middle.astype(jnp.bfloat16)
    grad_out_full = dot_left(attended, grad_branch).astype(jnp.bfloat16)
    grad_heads = (
        dot_right(grad_branch, out_full).astype(jnp.bfloat16).reshape(rows, kv_all, group, HD)
    )
    grad_probs = jnp.einsum(
        "qkgd,pkd->kgqp", grad_heads, valued, preferred_element_type=jnp.float32
    )
    grad_scores = (
        probs * (grad_probs - jnp.sum(probs * grad_probs, axis=-1, keepdims=True))
    ).astype(jnp.bfloat16)
    grad_value_in = (
        jnp.einsum("kgqp,qkgd->pkd", probs_low, grad_heads, preferred_element_type=jnp.float32)
        .astype(jnp.bfloat16)
        .reshape(2 * rows, kv_width)
    )
    grad_query_rot = (
        jnp.einsum("kgqp,pkd->qkgd", grad_scores, keyed, preferred_element_type=jnp.float32)
        .astype(jnp.bfloat16)
        .astype(jnp.float32)
        .reshape(rows, heads_all, HD)
    )
    grad_key_rot = (
        jnp.einsum("kgqp,qkgd->pkd", grad_scores, grouped, preferred_element_type=jnp.float32)
        .astype(jnp.bfloat16)
        .astype(jnp.float32)
    )
    grad_query_in = (
        (rotate(grad_query_rot, cosine[rows:], -sine_table[rows:]) * scale)
        .astype(jnp.bfloat16)
        .reshape(rows, q_width)
    )
    grad_key_in = (
        rotate(grad_key_rot, cosine, -sine_table).astype(jnp.bfloat16).reshape(2 * rows, kv_width)
    )
    grad_query_full = dot_left(normed_own, grad_query_in).astype(jnp.bfloat16)
    grad_key_full = dot_left(normed_both, grad_key_in).astype(jnp.bfloat16)
    grad_value_full = dot_left(normed_both, grad_value_in).astype(jnp.bfloat16)
    grad_both = dot_right(grad_key_in, key_full) + dot_right(grad_value_in, value_full)
    grad_before = grad_both[:rows].astype(jnp.bfloat16)
    grad_after = lax.ppermute(grad_before, "seq", [(1, 0)]).astype(jnp.float32)
    grad_own = grad_both[rows:] + dot_right(grad_query_in, query_full)
    normed_x = x_both * inverse_one
    grad_gain_first = jnp.sum(grad_own * normed_x[rows:], axis=0) + jnp.sum(
        grad_both[:rows] * normed_x[:rows], axis=0
    )
    small_grad = jnp.concatenate(
        [
            grad_router,
            grad_gain_first[:, None],
            grad_gain_second[:, None],
            jnp.zeros((width, SMALL - experts - 2), jnp.float32),
        ],
        axis=1,
    ).astype(jnp.bfloat16)
    scaled_one = (grad_own + grad_after) * gain_first
    grad_tokens = grad_middle + inverse_one[rows:] * (
        scaled_one
        - normed_x[rows:] * jnp.mean(scaled_one * normed_x[rows:], axis=-1, keepdims=True)
    )

    sum_out, sum_key, sum_query, sum_value, sum_small = scatter_sums(
        [grad_out_full, grad_key_full, grad_query_full, grad_value_full, small_grad],
        (0, 0, 1, 1, 1),
        1,
    )
    return (
        layer_out[None],
        grad_tokens[None],
        sum_small[:, experts],
        sum_query,
        sum_key,
        sum_value,
        sum_out,
        sum_small[:, experts + 1],
        sum_small[:, :experts],
        grad_gate[None],
        grad_up[None],
        grad_down[None],
    )


def solution(mesh):
    rows = P("fsdp", "seq", None)
    matrix, cube = P("fsdp", None), P("fsdp", None, None)
    return jax.shard_map(
        on_device,
        mesh=mesh,
        in_specs=(
            rows,
            P("fsdp", "seq"),
            rows,
            rows,
            P("fsdp"),
            matrix,
            matrix,
            matrix,
            matrix,
            P("fsdp"),
            matrix,
            cube,
            cube,
            cube,
        ),
        out_specs=(
            rows,
            rows,
            P("fsdp"),
            matrix,
            matrix,
            matrix,
            matrix,
            P("fsdp"),
            matrix,
            cube,
            cube,
            cube,
        ),
        check_vma=False,
    )
```

```python
import functools

import jax
import jax.numpy as jnp
from jax import lax
from jax.experimental import pallas as pl
from jax.experimental.pallas import tpu as pltpu
from jax.sharding import PartitionSpec as P

HD = 64
CORES = 2
SMALL = 128

epsilon = 1e-06
rope_base = 10000.0
masked_score = -1e30
MESH = pl.DeviceIdType.MESH
ANY = pl.BlockSpec(memory_space=pl.ANY)
VMEM = pl.BlockSpec(memory_space=pltpu.VMEM)


def dot_plain(left, right):
    return jnp.dot(left, right, preferred_element_type=jnp.float32)


def dot_left(left, right):
    return lax.dot_general(
        left, right, (((0,), (0,)), ((), ())), preferred_element_type=jnp.float32
    )


def dot_right(left, right):
    return lax.dot_general(
        left, right, (((1,), (1,)), ((), ())), preferred_element_type=jnp.float32
    )


def rms_scale(values, gain):
    return values * lax.rsqrt(jnp.mean(values * values, axis=-1, keepdims=True) + epsilon) * gain


def in_two(values):
    high = lax.reduce_precision(values, 8, 7)
    return high.astype(jnp.bfloat16), (values - high).astype(jnp.bfloat16)


def rotate(values, cosine, sine_table):
    middle = values.shape[-1] // 2
    first_half = values[..., :middle]
    second_half = values[..., middle:]
    return jnp.concatenate(
        [
            first_half * cosine - second_half * sine_table,
            second_half * cosine + first_half * sine_table,
        ],
        axis=-1,
    )


LONG = 4


def coordinates():
    seq, me = lax.axis_index("seq"), lax.axis_index("fsdp")
    return seq, me // 32, (me // 8) % LONG, (me // 2) % LONG, me % CORES


def device(seq, y, x, z, core):
    return (seq, ((y * LONG + x) * LONG + z) * CORES + core)


def enter(targets):
    barrier = pltpu.get_barrier_semaphore()
    for target in targets:
        pl.semaphore_signal(barrier, inc=1, device_id=target, device_id_type=MESH)
    pl.semaphore_wait(barrier, len(targets))


def neighbours():
    seq, y, x, z, core = coordinates()
    return [
        device(seq, y, x, z, 1 - core),
        device(seq, 1 - y, x, z, core),
        device(seq, y, lax.rem(x + 1, LONG), z, core),
        device(seq, y, lax.rem(x + 3, LONG), z, core),
        device(seq, y, x, lax.rem(z + 1, LONG), core),
        device(seq, y, x, lax.rem(z + 3, LONG), core),
        device(1 - seq, y, x, z, core),
    ]


def gather_kernel(shard_a, shard_b, x_own, pos_own, full_a, full_b, x_other, pos_other, *sems):
    send, recv, core_send, core_recv, seq_send, seq_recv, local = sems
    seq, y, x, z, core = coordinates()
    enter(neighbours())
    other_seq = device(1 - seq, y, x, z, core)
    swaps = [
        pltpu.make_async_remote_copy(
            src_ref=source,
            dst_ref=target,
            send_sem=seq_send.at[i],
            recv_sem=seq_recv.at[i],
            device_id=other_seq,
            device_id_type=MESH,
        )
        for i, (source, target) in enumerate(((x_own, x_other), (pos_own, pos_other)))
    ]
    fulls = (full_a, full_b)
    first_at, second_at = (x, z), (z, x)

    def along(i, stage, shift):
        if (i == 0) == (stage == 0):
            return device(seq, y, lax.rem(x + shift, LONG), z, core)
        return device(seq, y, x, lax.rem(z + shift, LONG), core)

    def block(i, stage, shift, ys):
        at = lax.rem((first_at if stage == 0 else second_at)[i] + shift, LONG)
        if stage == 0:
            xs, zs = (at, z) if i == 0 else (x, at)
        else:
            xs, zs = (slice(None), at) if i == 0 else (at, slice(None))
        return fulls[i].at[ys, xs, zs, core]

    def copy(i, k, part, target):
        return pltpu.make_async_remote_copy(
            src_ref=part,
            dst_ref=part,
            send_sem=send.at[i, k],
            recv_sem=recv.at[i, k],
            device_id=target,
            device_id_type=MESH,
        )

    both = slice(None)
    own = []
    started = []

    def start(i, k, part, target):
        moved = copy(i, k, part, target)
        moved.start()
        started.append(moved)

    crossing = []

    def cross(i, k, index):
        for side, wait in ((core, False), (1 - core, True)):
            part = fulls[i].at[(*index, side)]
            moved = pltpu.make_async_remote_copy(
                src_ref=part,
                dst_ref=part,
                send_sem=core_send.at[i, k],
                recv_sem=core_recv.at[i, k],
                device_id=device(seq, y, x, z, 1 - core),
                device_id_type=MESH,
            )
            if wait:
                crossing.append((moved, last))
            else:
                moved.start()
                last = moved

    for i, shard in enumerate((shard_a, shard_b)):
        kept = pltpu.make_async_copy(shard, fulls[i].at[y, x, z, core], local.at[i])
        kept.start()
        own.append(kept)
        outgoing = pltpu.make_async_remote_copy(
            src_ref=shard,
            dst_ref=fulls[i].at[y, x, z, core],
            send_sem=send.at[i, 0],
            recv_sem=recv.at[i, 0],
            device_id=device(seq, 1 - y, x, z, core),
            device_id_type=MESH,
        )
        outgoing.start()
        started.append(outgoing)
    for moved in swaps:
        moved.start()
    for i in range(2):
        own[i].wait()
        copy(i, 0, fulls[i].at[1 - y, x, z, core], other_seq).wait_recv()

    for stage in range(2):
        base = 1 + 4 * stage
        for i in range(2):
            start(i, base, block(i, stage, 0, both), along(i, stage, 1))
            start(i, base + 1, block(i, stage, 0, both), along(i, stage, 3))
            if stage == 1:
                at = second_at[i]
                cross(i, 0, (both, both, at) if i == 0 else (both, at, both))
        for i in range(2):
            copy(i, base, block(i, stage, 3, both), other_seq).wait_recv()
            start(i, base + 2, block(i, stage, 3, 0), along(i, stage, 1))
            copy(i, base + 1, block(i, stage, 1, both), other_seq).wait_recv()
            start(i, base + 3, block(i, stage, 1, 1), along(i, stage, 3))
            if stage == 1:
                for k, shift in ((1, 3), (2, 1)):
                    at = lax.rem(second_at[i] + shift, LONG)
                    cross(i, k, (both, both, at) if i == 0 else (both, at, both))
        for i in range(2):
            copy(i, base + 2, block(i, stage, 2, 0), other_seq).wait_recv()
            copy(i, base + 3, block(i, stage, 2, 1), other_seq).wait_recv()
            if stage == 1:
                at = lax.rem(second_at[i] + 2, LONG)
                cross(i, 3, (both, both, at) if i == 0 else (both, at, both))

    for arriving, leaving in crossing:
        arriving.wait_recv()
        leaving.wait_send()
    for moved in started:
        moved.wait_send()
    for moved in swaps:
        moved.wait()


def gather_shards(shard_a, shard_b, x_own, pos_own):
    count = lax.axis_size("fsdp")
    chips = (count // (LONG * LONG * CORES), LONG, LONG, CORES)
    shards = (shard_a, shard_b)
    outs = [jax.ShapeDtypeStruct((*chips, *shard.shape), shard.dtype) for shard in shards]
    outs += [jax.ShapeDtypeStruct(array.shape, array.dtype) for array in (x_own, pos_own)]
    full_a, full_b, x_other, pos_other = pl.pallas_call(
        gather_kernel,
        out_shape=outs,
        in_specs=[ANY] * 4,
        out_specs=[ANY] * 4,
        scratch_shapes=[
            pltpu.SemaphoreType.DMA((2, 9)),
            pltpu.SemaphoreType.DMA((2, 9)),
            pltpu.SemaphoreType.DMA((2, 4)),
            pltpu.SemaphoreType.DMA((2, 4)),
            pltpu.SemaphoreType.DMA((2,)),
            pltpu.SemaphoreType.DMA((2,)),
            pltpu.SemaphoreType.DMA((2,)),
        ],
        compiler_params=pltpu.CompilerParams(collective_id=0, has_side_effects=True),
        name="gather_weights",
    )(shard_a, shard_b, x_own, pos_own)
    height = count * shard_a.shape[0]
    return (
        full_a.reshape(height, shard_a.shape[1]),
        full_b.reshape(height, shard_b.shape[1]),
        x_other,
        pos_other,
    )


def widen(values):
    return values.astype(jnp.float32)


def scatter_kernel(groups, before, *refs):
    number = len(groups)
    after, refs = refs[2 * number], refs[: 2 * number] + refs[2 * number + 1 :]
    parts, totals = refs[:number], refs[number : 2 * number]
    halves, landed, second, landed_two, third, landed_three = (
        refs[k * number : (k + 1) * number] for k in range(2, 8)
    )
    core_send, core_recv, send, recv, swap_sems = refs[8 * number :]
    seq, y, x, z, core = coordinates()
    far_y = [
        device(seq, 1 - y, x, z, core),
        device(1 - seq, y, x, z, core),
        device(1 - seq, 1 - y, x, z, core),
    ]
    lines = [
        [device(seq, y, lax.rem(x + j, LONG), z, core) for j in (1, 2, 3)],
        [device(seq, y, x, lax.rem(z + j, LONG), core) for j in (1, 2, 3)],
    ]
    enter([device(seq, y, x, z, 1 - core)] + far_y + lines[0] + lines[1])

    def index(i, at):
        return (slice(None), slice(None), at) if groups[i] == 0 else (slice(None), at)

    first_at = [z if group == 0 else x for group in groups]
    second_at = [x if group == 0 else z for group in groups]
    first_line = [lines[1] if group == 0 else lines[0] for group in groups]
    second_line = [lines[0] if group == 0 else lines[1] for group in groups]

    def remote(source, target, to, sems, i, k):
        return pltpu.make_async_remote_copy(
            src_ref=source,
            dst_ref=target,
            send_sem=sems[0].at[i, k],
            recv_sem=sems[1].at[i, k],
            device_id=to,
            device_id_type=MESH,
        )

    def part_of(i, at, side):
        if groups[i] == 0:
            return parts[i].at[:, :, at, side]
        return parts[i].at[:, at, :, side]

    order = (2, 1, 3, 0)
    waiting = []
    across = {}
    for j in order:
        for i in range(number):
            at = lax.rem(first_at[i] + j, LONG)
            moved = remote(
                part_of(i, at, 1 - core),
                halves[i].at[j],
                device(seq, y, x, z, 1 - core),
                (core_send, core_recv),
                i,
                j,
            )
            moved.start()
            across[i, j] = moved
    swap = pltpu.make_async_remote_copy(
        src_ref=before,
        dst_ref=after,
        send_sem=swap_sems.at[0],
        recv_sem=swap_sems.at[1],
        device_id=far_y[1],
        device_id_type=MESH,
    )
    swap.start()
    for j in order:
        for i in range(number):
            across[i, j].wait_recv()
            at = lax.rem(first_at[i] + j, LONG)
            both = widen(halves[i][j]) + widen(part_of(i, at, core)[...])
            halves[i][j] = both.astype(jnp.bfloat16)
            if j:
                moved = remote(
                    halves[i].at[j],
                    landed[i].at[j - 1],
                    first_line[i][j - 1],
                    (send, recv),
                    i,
                    j - 1,
                )
                moved.start()
                waiting.append(moved)
    hops = {}
    for i in range(number):
        for j in (1, 2, 3):
            remote(halves[i].at[j], landed[i].at[j - 1], far_y[0], (send, recv), i, j - 1).wait_recv()
        total = widen(halves[i][0])
        for j in range(3):
            total = total + widen(landed[i][j])
        second[i][...] = total.astype(jnp.bfloat16)
        for j in (2, 1, 3):
            at = lax.rem(second_at[i] + j, LONG)
            moved = remote(
                second[i].at[:, at],
                landed_two[i].at[j - 1],
                second_line[i][j - 1],
                (send, recv),
                i,
                2 + j,
            )
            moved.start()
            waiting.append(moved)
            hops[i, j] = moved
    for i in range(number):
        for j in (1, 2, 3):
            hops[i, j].wait_recv()
        total = widen(second[i][:, second_at[i]])
        for j in range(3):
            total = total + widen(landed_two[i][j])
        third[i][...] = total.astype(jnp.bfloat16)
        landed_three[i][seq * 2 + y] = third[i][y]
        for k, wanted in enumerate((1 - y, y, 1 - y)):
            moved = remote(
                third[i].at[wanted],
                landed_three[i].at[seq * 2 + y],
                far_y[k],
                (send, recv),
                i,
                6 + k,
            )
            moved.start()
            waiting.append(moved)
            hops[i, 3 + k] = moved
    for i in range(number):
        for k in range(3):
            hops[i, 3 + k].wait_recv()
        total = widen(landed_three[i][0])
        for k in range(1, 4):
            total = total + widen(landed_three[i][k])
        totals[i][...] = total
    for moved in waiting:
        moved.wait_send()
    for i in range(number):
        for j in order:
            across[i, j].wait_send()
    swap.wait()


def scatter_sums(fulls, groups, before, identity):
    count = lax.axis_size("fsdp")
    number = len(fulls)
    rows = fulls[0].shape[0] // count
    widths = [full.shape[1] for full in fulls]
    ys = count // (LONG * LONG * CORES)
    parts = [full.reshape(ys, LONG, LONG, CORES, rows, full.shape[1]) for full in fulls]

    def room(*lead):
        return [pltpu.VMEM((*lead, rows, width), jnp.bfloat16) for width in widths]

    return pl.pallas_call(
        functools.partial(scatter_kernel, groups),
        out_shape=[jax.ShapeDtypeStruct((rows, width), jnp.float32) for width in widths]
        + [jax.ShapeDtypeStruct(before.shape, before.dtype)],
        in_specs=[ANY] + [VMEM] * number,
        out_specs=[VMEM] * number + [ANY],
        scratch_shapes=room(LONG, ys, LONG)
        + room(LONG - 1, ys, LONG)
        + room(ys, LONG)
        + room(LONG - 1, ys)
        + room(ys)
        + room(2 * ys)
        + [
            pltpu.SemaphoreType.DMA((number, LONG)),
            pltpu.SemaphoreType.DMA((number, LONG)),
            pltpu.SemaphoreType.DMA((number, 9)),
            pltpu.SemaphoreType.DMA((number, 9)),
            pltpu.SemaphoreType.DMA((2,)),
        ],
        compiler_params=pltpu.CompilerParams(
            collective_id=identity, has_side_effects=True, vmem_limit_bytes=48 * 2**20
        ),
        name="scatter_gradients",
    )(before, *parts)


CHUNKS = 4
SAME, CROSS = 32, 16
BLOCK = SAME + CROSS
PLANE = LONG * LONG


def chip_at(sign, step, other_y=0):
    seq, y, x, z, core = coordinates()
    inner = step % PLANE
    dx = inner % LONG
    dz = (dx + inner // LONG) % LONG
    return ((y + other_y) % 2 * LONG + (x + sign * dx + LONG) % LONG) * LONG + (
        z + sign * dz + LONG
    ) % LONG


def remote(source, target, sends, recvs, to):
    return pltpu.make_async_remote_copy(
        src_ref=source,
        dst_ref=target,
        send_sem=sends,
        recv_sem=recvs,
        device_id=to,
        device_id_type=MESH,
    )


class Rows:
    def __init__(self, source, target, sems, self_sems, sign):
        self.source, self.target, self.sems, self.self_sems = source, target, sems, self_sems
        self.sign, self.steps = sign, 2 * PLANE // CHUNKS
        self.depth = self.steps * BLOCK
        self.seq, _, _, _, self.core = coordinates()
        self.partner = (self.seq, lax.axis_index("fsdp") + 1 - 2 * self.core)

    def rows(self, chunk):
        return pl.ds(pl.multiple_of(chunk * self.depth, 16), self.depth)

    def own(self, step):
        rows = pl.ds(pl.multiple_of(step * BLOCK, 16), SAME)
        return pltpu.make_async_copy(
            self.source.at[rows], self.target.at[rows], self.self_sems.at[step // PLANE]
        )

    def send(self, chunk):
        @pl.loop(0, self.steps)
        def _(inner):
            step = chunk * self.steps + inner
            chip = chip_at(self.sign, step)
            row = pl.multiple_of(step * BLOCK, 16)
            same, cross = pl.ds(row, SAME), pl.ds(pl.multiple_of(row + SAME, 16), CROSS)

            @pl.when(step % PLANE == 0)
            def _():
                self.own(step).start()

            sems = (self.sems.at[0, chunk], self.sems.at[1, chunk])

            @pl.when(step % PLANE > 0)
            def _():
                to = (self.seq, chip * CORES + self.core)
                remote(self.source.at[same], self.target.at[same], *sems, to).start()

            to = (self.seq, chip * CORES + 1 - self.core)
            remote(self.source.at[cross], self.target.at[cross], *sems, to).start()

    def whole(self, buffer, chunk, first):
        rows = self.rows(chunk)
        if first:
            rows = pl.ds(pl.multiple_of(chunk * self.depth + SAME, 16), self.depth - SAME)
        part = buffer.at[rows]
        return remote(part, part, self.sems.at[0, chunk], self.sems.at[1, chunk], self.partner)

    def wait(self, chunk):
        @pl.when(chunk % 2 == 0)
        def _():
            self.own(chunk * self.steps).wait()
            self.whole(self.target, chunk, True).wait_recv()

        @pl.when(chunk % 2 == 1)
        def _():
            self.whole(self.target, chunk, False).wait_recv()

    def wait_sends(self):
        for chunk in range(CHUNKS):
            self.whole(self.source, chunk, chunk % 2 == 0).wait_send()


def expert_kernel(
    table,
    normed,
    grad_low,
    own_gate,
    own_up,
    own_down,
    out_ref,
    back_ref,
    d_gate,
    d_up,
    d_down,
    table_both,
    normed_both,
    grad_both,
    picks,
    x_send,
    g_send,
    x_land,
    g_land,
    out_rows,
    back_land,
    back_sum,
    back_sum_land,
    gate_pre,
    up_pre,
    hidden,
    d_gate_pre,
    d_up_pre,
    w_gate,
    w_up,
    w_down,
    pair_send,
    pair_land,
    pair_send_down,
    pair_land_down,
    seq_send,
    seq_land,
    seq_send_down,
    seq_land_down,
    x_sems,
    g_sems,
    back_sems,
    self_sems,
    out_sems,
    weight_sems,
    sum_sems,
    near_sems,
):
    seq, y, x, z, core = coordinates()
    me = lax.axis_index("fsdp")
    rows_own, width = normed.shape
    partner = (seq, me + 1 - 2 * core)
    other_seq = (1 - seq, me)
    other_y = device(seq, 1 - y, x, z, core)

    barrier = pltpu.get_barrier_semaphore()
    for target in (partner, other_seq, other_y):
        pl.semaphore_signal(barrier, inc=1, device_id=target, device_id_type=MESH)

    @pl.loop(1, PLANE)
    def _(step):
        for side in range(CORES):
            pl.semaphore_signal(
                barrier,
                inc=1,
                device_id=(seq, chip_at(-1, step) * CORES + side),
                device_id_type=MESH,
            )

    pl.semaphore_wait(barrier, CORES * PLANE + 1)

    mine = pl.ds(pl.multiple_of(y * PLANE, PLANE), PLANE)
    theirs = pl.ds(pl.multiple_of((1 - y) * PLANE, PLANE), PLANE)
    near = [
        remote(source, target.at[1], near_sems.at[0, i], near_sems.at[1, i], other_y)
        for i, (source, target) in enumerate(
            ((table.at[theirs], table_both), (normed, normed_both), (grad_low, grad_both))
        )
    ]
    for moved in near:
        moved.start()

    weights = []
    for i, (own, full) in enumerate(((own_gate, w_gate), (own_up, w_up), (own_down, w_down))):
        height = own.shape[0]
        place = full.at[pl.ds(pl.multiple_of(core * height, height), height)]
        kept = pltpu.make_async_copy(own, place, weight_sems.at[2, i])
        sent = remote(own, place, weight_sems.at[0, i], weight_sems.at[1, i], partner)
        kept.start()
        sent.start()
        weights.append((kept, sent))

    x_rows = Rows(x_send.at[:, pl.ds(0, width)], x_land, x_sems, self_sems.at[0], 1)
    g_rows = Rows(g_send, g_land, g_sems, self_sems.at[1], 1)
    back_rows = Rows(x_send, back_land, back_sems, self_sems.at[2], -1)
    steps, depth = x_rows.steps, x_rows.depth

    table_both[0] = table[mine]
    normed_both[0] = normed[...]
    grad_both[0] = grad_low[...]
    place = lax.broadcasted_iota(jnp.int32, (BLOCK, rows_own), 0).astype(jnp.float32)

    def entry(step):
        return table_both[step // PLANE, chip_at(1, step) % PLANE]

    def send_x(chunk):
        @pl.loop(0, steps)
        def _(inner):
            step = chunk * steps + inner
            found = jnp.where(entry(step)[0:1] == place, 1.0, 0.0)
            picks[pl.ds(pl.multiple_of(step * BLOCK, 16), BLOCK), :] = found.astype(jnp.bfloat16)

        rows = x_rows.rows(chunk)
        values = dot_plain(picks[rows, :], normed_both[chunk // 2])
        x_send[rows, :width] = values.astype(jnp.bfloat16)
        x_rows.send(chunk)

    def send_g(chunk):
        @pl.loop(0, steps)
        def _(inner):
            step = chunk * steps + inner
            line = entry(step)
            weight = jnp.where(line[0:1] == place, line[1:2], 0.0)
            high = weight.astype(jnp.bfloat16)
            rest = (weight - high.astype(jnp.float32)).astype(jnp.bfloat16)
            rows = pl.ds(pl.multiple_of(step * BLOCK, 16), BLOCK)
            values = dot_plain(high, grad_both[step // PLANE]) + dot_plain(
                rest, grad_both[step // PLANE]
            )
            g_send[rows, :] = values.astype(jnp.bfloat16)

        g_rows.send(chunk)

    for chunk in (0, 1):
        send_x(chunk)
    near[0].wait_recv()
    near[1].wait_recv()
    for chunk in (2, 3):
        send_x(chunk)
    near[2].wait_recv()

    @pl.loop(0, CHUNKS)
    def _(turn):
        send_g((turn + 2) % CHUNKS)

    for kept, sent in weights:
        kept.wait()
        sent.wait()

    @pl.loop(0, CHUNKS)
    def _(chunk):
        rows = x_rows.rows(chunk)
        x_rows.wait(chunk)
        served = x_land[rows, :]
        gate = dot_plain(served, w_gate[...])
        up = dot_plain(served, w_up[...])
        gate_pre[rows, :] = gate
        up_pre[rows, :] = up
        low = (gate * jax.nn.sigmoid(gate) * up).astype(jnp.bfloat16)
        hidden[rows, :] = low
        out_rows[rows, :] = dot_plain(low, w_down[...]).astype(jnp.bfloat16)

        @pl.loop(0, steps)
        def _(inner):
            step = chunk * steps + inner
            row = pl.multiple_of(step * BLOCK, 16)
            chip = chip_at(-1, step, step // PLANE)
            out_ref[chip, :SAME, :] = out_rows[pl.ds(row, SAME), :]
            remote(
                out_rows.at[pl.ds(pl.multiple_of(row + SAME, 16), CROSS)],
                out_ref.at[chip, pl.ds(SAME, CROSS)],
                out_sems.at[0],
                out_sems.at[1],
                partner,
            ).start()

    x_rows.wait_sends()

    lane = lax.broadcasted_iota(jnp.int32, (depth, SMALL), 1)
    expert = me // CORES

    @pl.loop(0, CHUNKS)
    def _(turn):
        chunk = (turn + 2) % CHUNKS
        rows = g_rows.rows(chunk)
        g_rows.wait(chunk)
        low = g_land[rows, :]
        dots = jnp.sum(
            low.astype(jnp.float32) * out_rows[rows, :].astype(jnp.float32), axis=1, keepdims=True
        )
        high = dots.astype(jnp.bfloat16).astype(jnp.float32)
        x_send[rows, width:] = jnp.where(
            lane == expert, high, jnp.where(lane == expert + 2 * PLANE, dots - high, 0.0)
        ).astype(jnp.bfloat16)
        d_hidden = dot_right(low, w_down[...])
        gate, up = gate_pre[rows, :], up_pre[rows, :]
        sigmoid = jax.nn.sigmoid(gate)
        one = (d_hidden * up * sigmoid * (1.0 + gate * (1.0 - sigmoid))).astype(jnp.bfloat16)
        two = (d_hidden * (gate * sigmoid)).astype(jnp.bfloat16)
        d_gate_pre[rows, :] = one
        d_up_pre[rows, :] = two
        x_send[rows, :width] = (dot_right(one, w_gate[...]) + dot_right(two, w_up[...])).astype(
            jnp.bfloat16
        )
        back_rows.send(chunk)

    tile = 256
    half = own_gate.shape[0]
    half_down = own_down.shape[0]

    def product(side, which, at):
        start = pl.multiple_of(side * half + at * tile, tile)
        return dot_left(x_land[:, pl.ds(start, tile)], (d_gate_pre, d_up_pre)[which][...])

    def product_down(side, at):
        start = pl.multiple_of(side * half_down, half_down)
        columns = pl.ds(pl.multiple_of(at * half, half), half)
        return dot_left(hidden[:, pl.ds(start, half_down)], g_land[:, columns]), columns

    def both_tiles(side, keep):
        @pl.loop(0, half // tile)
        def _(at):
            for which in range(2):
                keep(which, pl.ds(pl.multiple_of(at * tile, tile), tile), product(side, which, at))

    def keep_other(which, rows, values):
        pair_send[which, rows, :] = values.astype(jnp.bfloat16)

    def keep_own(which, rows, values):
        (d_gate, d_up)[which][rows, :] = values

    both_tiles(1 - core, keep_other)

    @pl.loop(0, width // half)
    def _(at):
        values, columns = product_down(1 - core, at)
        pair_send_down[:, columns] = values.astype(jnp.bfloat16)

    pairs = [
        remote(pair_send, pair_land, sum_sems.at[0, 0], sum_sems.at[1, 0], partner),
        remote(pair_send_down, pair_land_down, sum_sems.at[0, 1], sum_sems.at[1, 1], partner),
    ]
    for moved in pairs:
        moved.start()
    both_tiles(core, keep_own)

    @pl.loop(0, width // half)
    def _(at):
        values, columns = product_down(core, at)
        d_down[:, columns] = values

    pairs[0].wait_recv()
    for which, mine_sum in enumerate((d_gate, d_up)):
        seq_send[which] = (mine_sum[...] + pair_land[which].astype(jnp.float32)).astype(
            jnp.bfloat16
        )
    pairs[1].wait_recv()
    seq_send_down[...] = (d_down[...] + pair_land_down[...].astype(jnp.float32)).astype(
        jnp.bfloat16
    )
    sums = [
        remote(seq_send, seq_land, sum_sems.at[0, 2], sum_sems.at[1, 2], other_seq),
        remote(seq_send_down, seq_land_down, sum_sems.at[0, 3], sum_sems.at[1, 3], other_seq),
    ]
    for moved in sums:
        moved.start()

    back_ref[...] = jnp.zeros_like(back_ref)

    def combine(chunk):
        rows = back_rows.rows(chunk)
        back_rows.wait(chunk)
        back_ref[...] += dot_left(picks[rows, :], back_land[rows, :])

    @pl.loop(2, CHUNKS)
    def _(chunk):
        combine(chunk)

    back_sum[...] = back_ref[...].astype(jnp.bfloat16)
    over = remote(back_sum, back_sum_land, near_sems.at[0, 3], near_sems.at[1, 3], other_y)
    over.start()
    back_ref[...] = jnp.zeros_like(back_ref)

    @pl.loop(0, 2)
    def _(chunk):
        combine(chunk)

    over.wait_recv()
    back_ref[...] += back_sum_land[...].astype(jnp.float32)

    sums[0].wait_recv()
    for which, mine_sum in enumerate((d_gate, d_up)):
        mine_sum[...] = seq_send[which].astype(jnp.float32) + seq_land[which].astype(jnp.float32)
    sums[1].wait_recv()
    d_down[...] = seq_send_down[...].astype(jnp.float32) + seq_land_down[...].astype(jnp.float32)
    outs = out_rows.at[pl.ds(0, 2 * PLANE * CROSS)]
    remote(outs, outs, out_sems.at[0], out_sems.at[1], partner).wait()
    g_rows.wait_sends()
    back_rows.wait_sends()
    for moved in pairs + sums + near + [over]:
        moved.wait_send()


def run_experts(table, normed, grad_low, own_gate, own_up, own_down):
    chips = table.shape[0]
    rows, width = normed.shape
    hidden = own_gate.shape[1]
    slots = chips * BLOCK
    low, high = jnp.bfloat16, jnp.float32
    dma = pltpu.SemaphoreType.DMA
    half, half_down = own_gate.shape[0], own_down.shape[0]
    return pl.pallas_call(
        expert_kernel,
        out_shape=[
            jax.ShapeDtypeStruct((chips, BLOCK, width), low),
            jax.ShapeDtypeStruct((rows, width + SMALL), high),
            jax.ShapeDtypeStruct(own_gate.shape, high),
            jax.ShapeDtypeStruct(own_up.shape, high),
            jax.ShapeDtypeStruct(own_down.shape, high),
        ],
        in_specs=[VMEM] * 6,
        out_specs=[VMEM] * 5,
        scratch_shapes=[
            pltpu.VMEM((2, PLANE, *table.shape[1:]), high),
            pltpu.VMEM((2, rows, width), low),
            pltpu.VMEM((2, rows, width), low),
            pltpu.VMEM((slots, rows), low),
            pltpu.VMEM((slots, width + SMALL), low),
            pltpu.VMEM((slots, width), low),
            pltpu.VMEM((slots, width), low),
            pltpu.VMEM((slots, width), low),
            pltpu.VMEM((slots, width), low),
            pltpu.VMEM((slots, width + SMALL), low),
            pltpu.VMEM((rows, width + SMALL), low),
            pltpu.VMEM((rows, width + SMALL), low),
            pltpu.VMEM((slots, hidden), high),
            pltpu.VMEM((slots, hidden), high),
            pltpu.VMEM((slots, hidden), low),
            pltpu.VMEM((slots, hidden), low),
            pltpu.VMEM((slots, hidden), low),
            pltpu.VMEM((CORES * half, hidden), low),
            pltpu.VMEM((CORES * half, hidden), low),
            pltpu.VMEM((CORES * half_down, width), low),
            pltpu.VMEM((2, half, hidden), low),
            pltpu.VMEM((2, half, hidden), low),
            pltpu.VMEM((half_down, width), low),
            pltpu.VMEM((half_down, width), low),
            pltpu.VMEM((2, half, hidden), low),
            pltpu.VMEM((2, half, hidden), low),
            pltpu.VMEM((half_down, width), low),
            pltpu.VMEM((half_down, width), low),
            dma((2, CHUNKS)),
            dma((2, CHUNKS)),
            dma((2, CHUNKS)),
            dma((3, 2)),
            dma((2,)),
            dma((3, 3)),
            dma((2, 4)),
            dma((2, 4)),
        ],
        compiler_params=pltpu.CompilerParams(
            collective_id=2, has_side_effects=True, vmem_limit_bytes=60 * 2**20
        ),
        name="experts",
    )(table, normed, grad_low, own_gate, own_up, own_down)


def from_experts(blocks):
    groups = [
        [chip * CORES + core for chip in range(blocks.shape[0])] for core in range(CORES)
    ]
    return lax.all_to_all(
        blocks, "fsdp", split_axis=0, concat_axis=0, tiled=True, axis_index_groups=groups
    )


def on_device(
    tokens,
    positions,
    routes,
    cotangent,
    first_gain,
    w_query,
    w_key,
    w_value,
    w_out,
    second_gain,
    w_router,
    w_gate,
    w_up,
    w_down,
):
    width = tokens.shape[2]
    rows = tokens.shape[1]
    heads_all = w_query.shape[1] // HD
    kv_all = w_key.shape[1] // HD
    group = heads_all // kv_all
    q_width, kv_width = heads_all * HD, kv_all * HD
    scale = HD ** (-0.5)
    slots = lax.axis_size("fsdp")
    experts = slots // CORES
    seq = lax.axis_index("seq")
    places = BLOCK

    x_own = tokens[0]

    chosen = routes[0]
    ids = jnp.arange(experts, dtype=jnp.int32)
    mask = jnp.any(chosen[:, :, None] == ids[None, None, :], axis=1)
    mask_low = mask.astype(jnp.bfloat16)
    earlier = (jnp.arange(rows)[:, None] > jnp.arange(rows)[None, :]).astype(jnp.bfloat16)
    rank = jnp.where(mask, dot_plain(earlier, mask_low).astype(jnp.int32), -1)
    onehot_wide = rank.T[:, None, :] == jnp.arange(places, dtype=jnp.int32)[None, :, None]
    grad_low = cotangent[0]
    grad_output = grad_low.astype(jnp.float32)

    small = jnp.concatenate(
        [
            w_router,
            first_gain[:, None],
            second_gain[:, None],
            jnp.zeros((w_router.shape[0], SMALL - experts - 2), jnp.bfloat16),
        ],
        axis=1,
    )
    full_a, full_b, x_before, pos_before = gather_shards(
        jnp.concatenate([w_query, w_key], axis=1),
        jnp.concatenate([w_value, w_out, small], axis=1),
        x_own,
        positions,
    )
    query_full, key_full = full_a[:, :q_width], full_a[:, q_width:]
    value_full = full_b[:, :kv_width]
    out_full = full_b[:, kv_width : kv_width + width]
    small_full = full_b[:, kv_width + width :]
    router_full = small_full[:, :experts]
    gain_first = small_full[:, experts].astype(jnp.float32)
    gain_second = small_full[:, experts + 1].astype(jnp.float32)

    x_both = jnp.concatenate([x_before, x_own], axis=0).astype(jnp.float32)
    pos_both = jnp.concatenate([pos_before[0], positions[0]], axis=0)
    inputs = x_both[rows:]
    inverse = rope_base ** (-(2.0 * jnp.arange(HD // 2, dtype=jnp.float32)) / HD)
    angle = pos_both.astype(jnp.float32)[:, None] * inverse[None, :]
    cosine = jnp.cos(angle)[:, None, :]
    sine_table = jnp.sin(angle)[:, None, :]
    inverse_one = lax.rsqrt(jnp.mean(x_both * x_both, axis=-1, keepdims=True) + epsilon)
    normed_both = (x_both * inverse_one * gain_first).astype(jnp.bfloat16)
    normed_own = normed_both[rows:]
    query_pre = dot_plain(normed_own, query_full).reshape(rows, heads_all, HD)
    key_pre = dot_plain(normed_both, key_full).reshape(2 * rows, kv_all, HD)
    query_rot = (rotate(query_pre, cosine[rows:], sine_table[rows:]) * scale).astype(jnp.bfloat16)
    keyed = rotate(key_pre, cosine, sine_table).astype(jnp.bfloat16)
    valued = dot_plain(normed_both, value_full).astype(jnp.bfloat16).reshape(2 * rows, kv_all, HD)
    grouped = query_rot.reshape(rows, kv_all, group, HD)
    key_at = jnp.arange(2 * rows)[None, :]
    allowed = (key_at - rows <= jnp.arange(rows)[:, None]) & ((key_at >= rows) | (seq == 1))
    scores = jnp.einsum("qkgd,pkd->kgqp", grouped, keyed, preferred_element_type=jnp.float32)
    scores = jnp.where(allowed, scores, masked_score)
    peak = jnp.max(scores, axis=-1, keepdims=True)
    raised = jnp.exp(scores - peak)
    probs = raised / jnp.sum(raised, axis=-1, keepdims=True)
    probs_low = probs.astype(jnp.bfloat16)
    attended = (
        jnp.einsum("kgqp,pkd->qkgd", probs_low, valued, preferred_element_type=jnp.float32)
        .astype(jnp.bfloat16)
        .reshape(rows, q_width)
    )
    middle = inputs + dot_plain(attended, out_full)

    inverse_two = lax.rsqrt(jnp.mean(middle * middle, axis=-1, keepdims=True) + epsilon)
    normed_two = (middle * inverse_two * gain_second).astype(jnp.bfloat16)
    logits = jnp.where(mask, dot_plain(normed_two, router_full), masked_score)
    lifted = jnp.where(mask, jnp.exp(logits - jnp.max(logits, axis=-1, keepdims=True)), 0.0)
    gates = lifted / jnp.sum(lifted, axis=-1, keepdims=True)
    table = jnp.stack([rank.T.astype(jnp.float32), gates.T], axis=1)
    part_out, grad_back, grad_gate, grad_up, grad_down = run_experts(
        table, normed_two, grad_low, w_gate[0], w_up[0], w_down[0]
    )
    grad_routed, dots = grad_back[:, :width], grad_back[:, width:]
    returned = from_experts(part_out).reshape(experts * places, width)

    gates_wide = jnp.where(onehot_wide, gates.T[:, None, :], 0.0)
    gates_high, gates_rest = in_two(gates_wide)
    flat = (experts * places, rows)
    mixed = dot_left(gates_high.reshape(flat), returned) + dot_left(
        gates_rest.reshape(flat), returned
    )
    layer_out = (middle + mixed).astype(jnp.bfloat16)
    weighted = dots[:, :experts] + dots[:, experts : 2 * experts]
    grad_picked = weighted - gates * jnp.sum(weighted, axis=-1, keepdims=True)
    grad_logits = grad_picked.astype(jnp.bfloat16)
    grad_router = dot_left(normed_two, grad_logits)
    grad_normed_two = dot_right(grad_logits, router_full) + grad_routed

    normed = middle * inverse_two
    scaled = grad_normed_two * gain_second
    grad_middle = grad_output + inverse_two * (
        scaled - normed * jnp.mean(scaled * normed, axis=-1, keepdims=True)
    )
    grad_gain_second = jnp.sum(grad_normed_two * normed, axis=0)
    grad_branch = grad_middle.astype(jnp.bfloat16)
    grad_out_full = dot_left(attended, grad_branch).astype(jnp.bfloat16)
    grad_heads = (
        dot_right(grad_branch, out_full).astype(jnp.bfloat16).reshape(rows, kv_all, group, HD)
    )
    grad_probs = jnp.einsum(
        "qkgd,pkd->kgqp", grad_heads, valued, preferred_element_type=jnp.float32
    )
    grad_scores = (
        probs * (grad_probs - jnp.sum(probs * grad_probs, axis=-1, keepdims=True))
    ).astype(jnp.bfloat16)
    grad_value_in = (
        jnp.einsum("kgqp,qkgd->pkd", probs_low, grad_heads, preferred_element_type=jnp.float32)
        .astype(jnp.bfloat16)
        .reshape(2 * rows, kv_width)
    )
    grad_query_rot = (
        jnp.einsum("kgqp,pkd->qkgd", grad_scores, keyed, preferred_element_type=jnp.float32)
        .astype(jnp.bfloat16)
        .astype(jnp.float32)
        .reshape(rows, heads_all, HD)
    )
    grad_key_rot = (
        jnp.einsum("kgqp,qkgd->pkd", grad_scores, grouped, preferred_element_type=jnp.float32)
        .astype(jnp.bfloat16)
        .astype(jnp.float32)
    )
    grad_query_in = (
        (rotate(grad_query_rot, cosine[rows:], -sine_table[rows:]) * scale)
        .astype(jnp.bfloat16)
        .reshape(rows, q_width)
    )
    grad_key_in = (
        rotate(grad_key_rot, cosine, -sine_table).astype(jnp.bfloat16).reshape(2 * rows, kv_width)
    )
    grad_query_full = dot_left(normed_own, grad_query_in).astype(jnp.bfloat16)
    grad_key_full = dot_left(normed_both, grad_key_in).astype(jnp.bfloat16)
    grad_value_full = dot_left(normed_both, grad_value_in).astype(jnp.bfloat16)
    grad_both = dot_right(grad_key_in, key_full) + dot_right(grad_value_in, value_full)
    grad_before = grad_both[:rows].astype(jnp.bfloat16)
    grad_own = grad_both[rows:] + dot_right(grad_query_in, query_full)
    normed_x = x_both * inverse_one
    grad_gain_first = jnp.sum(grad_own * normed_x[rows:], axis=0) + jnp.sum(
        grad_both[:rows] * normed_x[:rows], axis=0
    )
    small_grad = jnp.concatenate(
        [
            grad_router,
            grad_gain_first[:, None],
            grad_gain_second[:, None],
            jnp.zeros((width, SMALL - experts - 2), jnp.float32),
        ],
        axis=1,
    ).astype(jnp.bfloat16)
    sum_out, sum_key, sum_query, sum_value, sum_small, grad_after = scatter_sums(
        [grad_out_full, grad_key_full, grad_query_full, grad_value_full, small_grad],
        (0, 0, 1, 1, 1),
        grad_before,
        1,
    )
    scaled_one = (grad_own + grad_after.astype(jnp.float32)) * gain_first
    grad_tokens = grad_middle + inverse_one[rows:] * (
        scaled_one
        - normed_x[rows:] * jnp.mean(scaled_one * normed_x[rows:], axis=-1, keepdims=True)
    )
    return (
        layer_out[None],
        grad_tokens[None],
        sum_small[:, experts],
        sum_query,
        sum_key,
        sum_value,
        sum_out,
        sum_small[:, experts + 1],
        sum_small[:, :experts],
        grad_gate[None],
        grad_up[None],
        grad_down[None],
    )


def solution(mesh):
    rows = P("fsdp", "seq", None)
    matrix, cube = P("fsdp", None), P("fsdp", None, None)
    return jax.shard_map(
        on_device,
        mesh=mesh,
        in_specs=(
            rows,
            P("fsdp", "seq"),
            rows,
            rows,
            P("fsdp"),
            matrix,
            matrix,
            matrix,
            matrix,
            P("fsdp"),
            matrix,
            cube,
            cube,
            cube,
        ),
        out_specs=(
            rows,
            rows,
            P("fsdp"),
            matrix,
            matrix,
            matrix,
            matrix,
            P("fsdp"),
            matrix,
            cube,
            cube,
            cube,
        ),
        check_vma=False,
    )
```

```python
import functools

import jax
import jax.numpy as jnp
from jax import lax
from jax.experimental import pallas as pl
from jax.experimental.pallas import tpu as pltpu
from jax.sharding import PartitionSpec as P

HD = 64
CORES = 2
SMALL = 128

epsilon = 1e-06
rope_base = 10000.0
masked_score = -1e30
MESH = pl.DeviceIdType.MESH
ANY = pl.BlockSpec(memory_space=pl.ANY)
VMEM = pl.BlockSpec(memory_space=pltpu.VMEM)


def dot_plain(left, right):
    return jnp.dot(left, right, preferred_element_type=jnp.float32)


def dot_left(left, right):
    return lax.dot_general(
        left, right, (((0,), (0,)), ((), ())), preferred_element_type=jnp.float32
    )


def dot_right(left, right):
    return lax.dot_general(
        left, right, (((1,), (1,)), ((), ())), preferred_element_type=jnp.float32
    )


def rms_scale(values, gain):
    return values * lax.rsqrt(jnp.mean(values * values, axis=-1, keepdims=True) + epsilon) * gain


def rotate(values, cosine, sine_table):
    middle = values.shape[-1] // 2
    first_half = values[..., :middle]
    second_half = values[..., middle:]
    return jnp.concatenate(
        [
            first_half * cosine - second_half * sine_table,
            second_half * cosine + first_half * sine_table,
        ],
        axis=-1,
    )


LONG = 4


def coordinates():
    seq, me = lax.axis_index("seq"), lax.axis_index("fsdp")
    return seq, me // 32, (me // 8) % LONG, (me // 2) % LONG, me % CORES


def device(seq, y, x, z, core):
    return (seq, ((y * LONG + x) * LONG + z) * CORES + core)


def enter(targets):
    barrier = pltpu.get_barrier_semaphore()
    for target in targets:
        pl.semaphore_signal(barrier, inc=1, device_id=target, device_id_type=MESH)
    pl.semaphore_wait(barrier, len(targets))


def neighbours():
    seq, y, x, z, core = coordinates()
    return [
        device(seq, y, x, z, 1 - core),
        device(seq, 1 - y, x, z, core),
        device(seq, y, lax.rem(x + 1, LONG), z, core),
        device(seq, y, lax.rem(x + 3, LONG), z, core),
        device(seq, y, x, lax.rem(z + 1, LONG), core),
        device(seq, y, x, lax.rem(z + 3, LONG), core),
        device(1 - seq, y, x, z, core),
    ]


def gather_kernel(shard_a, shard_b, x_own, pos_own, full_a, full_b, x_other, pos_other, *sems):
    send, recv, core_send, core_recv, seq_send, seq_recv, local = sems
    seq, y, x, z, core = coordinates()
    enter(neighbours())
    other_seq = device(1 - seq, y, x, z, core)
    swaps = [
        pltpu.make_async_remote_copy(
            src_ref=source,
            dst_ref=target,
            send_sem=seq_send.at[i],
            recv_sem=seq_recv.at[i],
            device_id=other_seq,
            device_id_type=MESH,
        )
        for i, (source, target) in enumerate(((x_own, x_other), (pos_own, pos_other)))
    ]
    fulls = (full_a, full_b)
    first_at, second_at = (x, z), (z, x)

    def along(i, stage, shift):
        if (i == 0) == (stage == 0):
            return device(seq, y, lax.rem(x + shift, LONG), z, core)
        return device(seq, y, x, lax.rem(z + shift, LONG), core)

    def block(i, stage, shift, ys):
        at = lax.rem((first_at if stage == 0 else second_at)[i] + shift, LONG)
        if stage == 0:
            xs, zs = (at, z) if i == 0 else (x, at)
        else:
            xs, zs = (slice(None), at) if i == 0 else (at, slice(None))
        return fulls[i].at[ys, xs, zs, core]

    def copy(i, k, part, target):
        return pltpu.make_async_remote_copy(
            src_ref=part,
            dst_ref=part,
            send_sem=send.at[i, k],
            recv_sem=recv.at[i, k],
            device_id=target,
            device_id_type=MESH,
        )

    both = slice(None)
    own = []
    started = []

    def start(i, k, part, target):
        moved = copy(i, k, part, target)
        moved.start()
        started.append(moved)

    crossing = []

    def cross(i, k, index):
        for side, wait in ((core, False), (1 - core, True)):
            part = fulls[i].at[(*index, side)]
            moved = pltpu.make_async_remote_copy(
                src_ref=part,
                dst_ref=part,
                send_sem=core_send.at[i, k],
                recv_sem=core_recv.at[i, k],
                device_id=device(seq, y, x, z, 1 - core),
                device_id_type=MESH,
            )
            if wait:
                crossing.append((moved, last))
            else:
                moved.start()
                last = moved

    for i, shard in enumerate((shard_a, shard_b)):
        kept = pltpu.make_async_copy(shard, fulls[i].at[y, x, z, core], local.at[i])
        kept.start()
        own.append(kept)
        outgoing = pltpu.make_async_remote_copy(
            src_ref=shard,
            dst_ref=fulls[i].at[y, x, z, core],
            send_sem=send.at[i, 0],
            recv_sem=recv.at[i, 0],
            device_id=device(seq, 1 - y, x, z, core),
            device_id_type=MESH,
        )
        outgoing.start()
        started.append(outgoing)
    for moved in swaps:
        moved.start()
    for i in range(2):
        own[i].wait()
        copy(i, 0, fulls[i].at[1 - y, x, z, core], other_seq).wait_recv()

    for stage in range(2):
        base = 1 + 4 * stage
        for i in range(2):
            start(i, base, block(i, stage, 0, both), along(i, stage, 1))
            start(i, base + 1, block(i, stage, 0, both), along(i, stage, 3))
            if stage == 1:
                at = second_at[i]
                cross(i, 0, (both, both, at) if i == 0 else (both, at, both))
        for i in range(2):
            copy(i, base, block(i, stage, 3, both), other_seq).wait_recv()
            start(i, base + 2, block(i, stage, 3, 0), along(i, stage, 1))
            copy(i, base + 1, block(i, stage, 1, both), other_seq).wait_recv()
            start(i, base + 3, block(i, stage, 1, 1), along(i, stage, 3))
            if stage == 1:
                for k, shift in ((1, 3), (2, 1)):
                    at = lax.rem(second_at[i] + shift, LONG)
                    cross(i, k, (both, both, at) if i == 0 else (both, at, both))
        for i in range(2):
            copy(i, base + 2, block(i, stage, 2, 0), other_seq).wait_recv()
            copy(i, base + 3, block(i, stage, 2, 1), other_seq).wait_recv()
            if stage == 1:
                at = lax.rem(second_at[i] + 2, LONG)
                cross(i, 3, (both, both, at) if i == 0 else (both, at, both))

    for arriving, leaving in crossing:
        arriving.wait_recv()
        leaving.wait_send()
    for moved in started:
        moved.wait_send()
    for moved in swaps:
        moved.wait()


def gather_shards(shard_a, shard_b, x_own, pos_own):
    count = lax.axis_size("fsdp")
    chips = (count // (LONG * LONG * CORES), LONG, LONG, CORES)
    shards = (shard_a, shard_b)
    outs = [jax.ShapeDtypeStruct((*chips, *shard.shape), shard.dtype) for shard in shards]
    outs += [jax.ShapeDtypeStruct(array.shape, array.dtype) for array in (x_own, pos_own)]
    full_a, full_b, x_other, pos_other = pl.pallas_call(
        gather_kernel,
        out_shape=outs,
        in_specs=[ANY] * 4,
        out_specs=[ANY] * 4,
        scratch_shapes=[
            pltpu.SemaphoreType.DMA((2, 9)),
            pltpu.SemaphoreType.DMA((2, 9)),
            pltpu.SemaphoreType.DMA((2, 4)),
            pltpu.SemaphoreType.DMA((2, 4)),
            pltpu.SemaphoreType.DMA((2,)),
            pltpu.SemaphoreType.DMA((2,)),
            pltpu.SemaphoreType.DMA((2,)),
        ],
        compiler_params=pltpu.CompilerParams(collective_id=0, has_side_effects=True),
        name="gather_weights",
    )(shard_a, shard_b, x_own, pos_own)
    height = count * shard_a.shape[0]
    return (
        full_a.reshape(height, shard_a.shape[1]),
        full_b.reshape(height, shard_b.shape[1]),
        x_other,
        pos_other,
    )


def widen(values):
    return values.astype(jnp.float32)


def scatter_kernel(groups, before, *refs):
    number = len(groups)
    after, refs = refs[2 * number], refs[: 2 * number] + refs[2 * number + 1 :]
    parts, totals = refs[:number], refs[number : 2 * number]
    halves, landed, second, landed_two, third, landed_three = (
        refs[k * number : (k + 1) * number] for k in range(2, 8)
    )
    core_send, core_recv, send, recv, swap_sems = refs[8 * number :]
    seq, y, x, z, core = coordinates()
    far_y = [
        device(seq, 1 - y, x, z, core),
        device(1 - seq, y, x, z, core),
        device(1 - seq, 1 - y, x, z, core),
    ]
    lines = [
        [device(seq, y, lax.rem(x + j, LONG), z, core) for j in (1, 2, 3)],
        [device(seq, y, x, lax.rem(z + j, LONG), core) for j in (1, 2, 3)],
    ]
    enter([device(seq, y, x, z, 1 - core)] + far_y + lines[0] + lines[1])

    def index(i, at):
        return (slice(None), slice(None), at) if groups[i] == 0 else (slice(None), at)

    first_at = [z if group == 0 else x for group in groups]
    second_at = [x if group == 0 else z for group in groups]
    first_line = [lines[1] if group == 0 else lines[0] for group in groups]
    second_line = [lines[0] if group == 0 else lines[1] for group in groups]

    def remote(source, target, to, sems, i, k):
        return pltpu.make_async_remote_copy(
            src_ref=source,
            dst_ref=target,
            send_sem=sems[0].at[i, k],
            recv_sem=sems[1].at[i, k],
            device_id=to,
            device_id_type=MESH,
        )

    def part_of(i, at, side):
        if groups[i] == 0:
            return parts[i].at[:, :, at, side]
        return parts[i].at[:, at, :, side]

    order = (2, 1, 3, 0)
    waiting = []
    across = {}
    for j in order:
        for i in range(number):
            at = lax.rem(first_at[i] + j, LONG)
            moved = remote(
                part_of(i, at, 1 - core),
                halves[i].at[j],
                device(seq, y, x, z, 1 - core),
                (core_send, core_recv),
                i,
                j,
            )
            moved.start()
            across[i, j] = moved
    swap = pltpu.make_async_remote_copy(
        src_ref=before,
        dst_ref=after,
        send_sem=swap_sems.at[0],
        recv_sem=swap_sems.at[1],
        device_id=far_y[1],
        device_id_type=MESH,
    )
    swap.start()
    for j in order:
        for i in range(number):
            across[i, j].wait_recv()
            at = lax.rem(first_at[i] + j, LONG)
            both = widen(halves[i][j]) + widen(part_of(i, at, core)[...])
            halves[i][j] = both.astype(jnp.bfloat16)
            if j:
                moved = remote(
                    halves[i].at[j],
                    landed[i].at[j - 1],
                    first_line[i][j - 1],
                    (send, recv),
                    i,
                    j - 1,
                )
                moved.start()
                waiting.append(moved)
    hops = {}
    for i in range(number):
        for j in (1, 2, 3):
            remote(halves[i].at[j], landed[i].at[j - 1], far_y[0], (send, recv), i, j - 1).wait_recv()
        total = widen(halves[i][0])
        for j in range(3):
            total = total + widen(landed[i][j])
        second[i][...] = total.astype(jnp.bfloat16)
        for j in (2, 1, 3):
            at = lax.rem(second_at[i] + j, LONG)
            moved = remote(
                second[i].at[:, at],
                landed_two[i].at[j - 1],
                second_line[i][j - 1],
                (send, recv),
                i,
                2 + j,
            )
            moved.start()
            waiting.append(moved)
            hops[i, j] = moved
    for i in range(number):
        for j in (1, 2, 3):
            hops[i, j].wait_recv()
        total = widen(second[i][:, second_at[i]])
        for j in range(3):
            total = total + widen(landed_two[i][j])
        third[i][...] = total.astype(jnp.bfloat16)
        landed_three[i][seq * 2 + y] = third[i][y]
        for k, wanted in enumerate((1 - y, y, 1 - y)):
            moved = remote(
                third[i].at[wanted],
                landed_three[i].at[seq * 2 + y],
                far_y[k],
                (send, recv),
                i,
                6 + k,
            )
            moved.start()
            waiting.append(moved)
            hops[i, 3 + k] = moved
    for i in range(number):
        for k in range(3):
            hops[i, 3 + k].wait_recv()
        total = widen(landed_three[i][0])
        for k in range(1, 4):
            total = total + widen(landed_three[i][k])
        totals[i][...] = total
    for moved in waiting:
        moved.wait_send()
    for i in range(number):
        for j in order:
            across[i, j].wait_send()
    swap.wait()


def scatter_sums(fulls, groups, before, identity):
    count = lax.axis_size("fsdp")
    number = len(fulls)
    rows = fulls[0].shape[0] // count
    widths = [full.shape[1] for full in fulls]
    ys = count // (LONG * LONG * CORES)
    parts = [full.reshape(ys, LONG, LONG, CORES, rows, full.shape[1]) for full in fulls]

    def room(*lead):
        return [pltpu.VMEM((*lead, rows, width), jnp.bfloat16) for width in widths]

    return pl.pallas_call(
        functools.partial(scatter_kernel, groups),
        out_shape=[jax.ShapeDtypeStruct((rows, width), jnp.float32) for width in widths]
        + [jax.ShapeDtypeStruct(before.shape, before.dtype)],
        in_specs=[ANY] + [VMEM] * number,
        out_specs=[VMEM] * number + [ANY],
        scratch_shapes=room(LONG, ys, LONG)
        + room(LONG - 1, ys, LONG)
        + room(ys, LONG)
        + room(LONG - 1, ys)
        + room(ys)
        + room(2 * ys)
        + [
            pltpu.SemaphoreType.DMA((number, LONG)),
            pltpu.SemaphoreType.DMA((number, LONG)),
            pltpu.SemaphoreType.DMA((number, 9)),
            pltpu.SemaphoreType.DMA((number, 9)),
            pltpu.SemaphoreType.DMA((2,)),
        ],
        compiler_params=pltpu.CompilerParams(
            collective_id=identity, has_side_effects=True, vmem_limit_bytes=48 * 2**20
        ),
        name="scatter_gradients",
    )(before, *parts)


CHUNKS = 4
SAME, CROSS = 32, 16
BLOCK = SAME + CROSS
PLANE = LONG * LONG


def chip_at(sign, step, other_y=0):
    seq, y, x, z, core = coordinates()
    inner = step % PLANE
    dx = inner % LONG
    dz = (dx + inner // LONG) % LONG
    return ((y + other_y) % 2 * LONG + (x + sign * dx + LONG) % LONG) * LONG + (
        z + sign * dz + LONG
    ) % LONG


def remote(source, target, sends, recvs, to):
    return pltpu.make_async_remote_copy(
        src_ref=source,
        dst_ref=target,
        send_sem=sends,
        recv_sem=recvs,
        device_id=to,
        device_id_type=MESH,
    )


class Rows:
    def __init__(self, source, target, sems, self_sems, sign):
        self.source, self.target, self.sems, self.self_sems = source, target, sems, self_sems
        self.sign, self.steps = sign, 2 * PLANE // CHUNKS
        self.depth = self.steps * BLOCK
        self.seq, _, _, _, self.core = coordinates()
        self.partner = (self.seq, lax.axis_index("fsdp") + 1 - 2 * self.core)

    def rows(self, chunk):
        return pl.ds(pl.multiple_of(chunk * self.depth, 16), self.depth)

    def own(self, step):
        rows = pl.ds(pl.multiple_of(step * BLOCK, 16), SAME)
        return pltpu.make_async_copy(
            self.source.at[rows], self.target.at[rows], self.self_sems.at[step // PLANE]
        )

    def send(self, chunk):
        @pl.loop(0, self.steps)
        def _(inner):
            step = chunk * self.steps + inner
            chip = chip_at(self.sign, step)
            row = pl.multiple_of(step * BLOCK, 16)
            same, cross = pl.ds(row, SAME), pl.ds(pl.multiple_of(row + SAME, 16), CROSS)

            @pl.when(step % PLANE == 0)
            def _():
                self.own(step).start()

            sems = (self.sems.at[0, chunk], self.sems.at[1, chunk])

            @pl.when(step % PLANE > 0)
            def _():
                to = (self.seq, chip * CORES + self.core)
                remote(self.source.at[same], self.target.at[same], *sems, to).start()

            to = (self.seq, chip * CORES + 1 - self.core)
            remote(self.source.at[cross], self.target.at[cross], *sems, to).start()

    def whole(self, buffer, chunk, first):
        rows = self.rows(chunk)
        if first:
            rows = pl.ds(pl.multiple_of(chunk * self.depth + SAME, 16), self.depth - SAME)
        part = buffer.at[rows]
        return remote(part, part, self.sems.at[0, chunk], self.sems.at[1, chunk], self.partner)

    def wait(self, chunk):
        @pl.when(chunk % 2 == 0)
        def _():
            self.own(chunk * self.steps).wait()
            self.whole(self.target, chunk, True).wait_recv()

        @pl.when(chunk % 2 == 1)
        def _():
            self.whole(self.target, chunk, False).wait_recv()

    def wait_sends(self):
        for chunk in range(CHUNKS):
            self.whole(self.source, chunk, chunk % 2 == 0).wait_send()


def expert_kernel(
    table,
    normed,
    grad_low,
    own_gate,
    own_up,
    own_down,
    out_ref,
    back_ref,
    d_gate,
    d_up,
    d_down,
    table_both,
    normed_both,
    grad_both,
    grad_twice,
    gated,
    picks,
    x_send,
    g_send,
    x_land,
    g_land,
    out_rows,
    back_land,
    back_sum,
    back_sum_land,
    gate_pre,
    up_pre,
    hidden,
    d_gate_pre,
    d_up_pre,
    w_gate,
    w_up,
    w_down,
    pair_send,
    pair_land,
    pair_send_down,
    pair_land_down,
    seq_send,
    seq_land,
    seq_send_down,
    seq_land_down,
    x_sems,
    g_sems,
    back_sems,
    self_sems,
    out_sems,
    weight_sems,
    sum_sems,
    near_sems,
):
    seq, y, x, z, core = coordinates()
    me = lax.axis_index("fsdp")
    rows_own, width = normed.shape
    partner = (seq, me + 1 - 2 * core)
    other_seq = (1 - seq, me)
    other_y = device(seq, 1 - y, x, z, core)

    barrier = pltpu.get_barrier_semaphore()
    for target in (partner, other_seq, other_y):
        pl.semaphore_signal(barrier, inc=1, device_id=target, device_id_type=MESH)

    @pl.loop(1, PLANE)
    def _(step):
        for side in range(CORES):
            pl.semaphore_signal(
                barrier,
                inc=1,
                device_id=(seq, chip_at(-1, step) * CORES + side),
                device_id_type=MESH,
            )

    pl.semaphore_wait(barrier, CORES * PLANE + 1)

    mine = pl.ds(pl.multiple_of(y * PLANE, PLANE), PLANE)
    theirs = pl.ds(pl.multiple_of((1 - y) * PLANE, PLANE), PLANE)
    near = [
        remote(source, target.at[1], near_sems.at[0, i], near_sems.at[1, i], other_y)
        for i, (source, target) in enumerate(
            ((table.at[theirs], table_both), (normed, normed_both), (grad_low, grad_both))
        )
    ]
    for moved in near:
        moved.start()

    weights = []
    for i, (own, full) in enumerate(((own_gate, w_gate), (own_up, w_up), (own_down, w_down))):
        height = own.shape[0]
        place = full.at[pl.ds(pl.multiple_of(core * height, height), height)]
        kept = pltpu.make_async_copy(own, place, weight_sems.at[2, i])
        sent = remote(own, place, weight_sems.at[0, i], weight_sems.at[1, i], partner)
        kept.start()
        sent.start()
        weights.append((kept, sent))

    x_rows = Rows(x_send.at[:, pl.ds(0, width)], x_land, x_sems, self_sems.at[0], 1)
    g_rows = Rows(g_send, g_land, g_sems, self_sems.at[1], 1)
    back_rows = Rows(x_send, back_land, back_sems, self_sems.at[2], -1)
    steps, depth = x_rows.steps, x_rows.depth

    table_both[0] = table[mine]
    normed_both[0] = normed[...]
    grad_both[0] = grad_low[...]
    place = lax.broadcasted_iota(jnp.int32, (BLOCK, rows_own), 0).astype(jnp.float32)

    def entry(step):
        return table_both[step // PLANE, chip_at(1, step) % PLANE]

    def send_x(chunk):
        @pl.loop(0, steps)
        def _(inner):
            step = chunk * steps + inner
            found = jnp.where(entry(step)[0:1] == place, 1.0, 0.0)
            picks[pl.ds(pl.multiple_of(step * BLOCK, 16), BLOCK), :] = found.astype(jnp.bfloat16)

        rows = x_rows.rows(chunk)
        values = dot_plain(picks[rows, :], normed_both[chunk // 2])
        x_send[rows, :width] = values.astype(jnp.bfloat16)
        x_rows.send(chunk)

    def send_g(chunk):
        @pl.loop(0, steps)
        def _(inner):
            line = entry(chunk * steps + inner)
            weight = jnp.where(line[0:1] == place, line[1:2], 0.0)
            high = weight.astype(jnp.bfloat16)
            rest = (weight - high.astype(jnp.float32)).astype(jnp.bfloat16)
            rows = pl.ds(pl.multiple_of(inner * BLOCK, 16), BLOCK)
            gated[rows, :rows_own] = high
            gated[rows, rows_own:] = rest

        g_send[g_rows.rows(chunk), :] = dot_plain(
            gated[...], grad_twice[pl.ds(pl.multiple_of(chunk // 2 * 2 * rows_own, 16), 2 * rows_own)]
        ).astype(jnp.bfloat16)
        g_rows.send(chunk)

    for chunk in (0, 1):
        send_x(chunk)
    near[0].wait_recv()
    near[1].wait_recv()
    for chunk in (2, 3):
        send_x(chunk)
    near[2].wait_recv()
    for i in range(4):
        grad_twice[pl.ds(i * rows_own, rows_own)] = grad_both[i // 2]

    @pl.loop(0, CHUNKS)
    def _(turn):
        send_g((turn + 2) % CHUNKS)

    for kept, sent in weights:
        kept.wait()
        sent.wait()

    @pl.loop(0, CHUNKS)
    def _(chunk):
        rows = x_rows.rows(chunk)
        x_rows.wait(chunk)
        served = x_land[rows, :]
        gate = dot_plain(served, w_gate[...])
        up = dot_plain(served, w_up[...])
        gate_pre[rows, :] = gate
        up_pre[rows, :] = up
        low = (gate * jax.nn.sigmoid(gate) * up).astype(jnp.bfloat16)
        hidden[rows, :] = low
        out_rows[rows, :] = dot_plain(low, w_down[...]).astype(jnp.bfloat16)

        @pl.loop(0, steps)
        def _(inner):
            step = chunk * steps + inner
            row = pl.multiple_of(step * BLOCK, 16)
            chip = chip_at(-1, step, step // PLANE)
            out_ref[chip, :SAME, :] = out_rows[pl.ds(row, SAME), :]
            remote(
                out_rows.at[pl.ds(pl.multiple_of(row + SAME, 16), CROSS)],
                out_ref.at[chip, pl.ds(SAME, CROSS)],
                out_sems.at[0],
                out_sems.at[1],
                partner,
            ).start()

    x_rows.wait_sends()

    lane = lax.broadcasted_iota(jnp.int32, (depth, SMALL), 1)
    expert = me // CORES

    @pl.loop(0, CHUNKS)
    def _(turn):
        chunk = (turn + 2) % CHUNKS
        rows = g_rows.rows(chunk)
        g_rows.wait(chunk)
        low = g_land[rows, :]
        dots = jnp.sum(
            low.astype(jnp.float32) * out_rows[rows, :].astype(jnp.float32), axis=1, keepdims=True
        )
        high = dots.astype(jnp.bfloat16).astype(jnp.float32)
        x_send[rows, width:] = jnp.where(
            lane == expert, high, jnp.where(lane == expert + 2 * PLANE, dots - high, 0.0)
        ).astype(jnp.bfloat16)
        d_hidden = dot_right(low, w_down[...])
        gate, up = gate_pre[rows, :], up_pre[rows, :]
        sigmoid = jax.nn.sigmoid(gate)
        one = (d_hidden * up * sigmoid * (1.0 + gate * (1.0 - sigmoid))).astype(jnp.bfloat16)
        two = (d_hidden * (gate * sigmoid)).astype(jnp.bfloat16)
        d_gate_pre[rows, :] = one
        d_up_pre[rows, :] = two
        x_send[rows, :width] = (dot_right(one, w_gate[...]) + dot_right(two, w_up[...])).astype(
            jnp.bfloat16
        )
        back_rows.send(chunk)

    tile = 256
    half = own_gate.shape[0]
    half_down = own_down.shape[0]

    def product(side, which, at):
        start = pl.multiple_of(side * half + at * tile, tile)
        return dot_left(x_land[:, pl.ds(start, tile)], (d_gate_pre, d_up_pre)[which][...])

    def product_down(side, at):
        start = pl.multiple_of(side * half_down, half_down)
        columns = pl.ds(pl.multiple_of(at * half, half), half)
        return dot_left(hidden[:, pl.ds(start, half_down)], g_land[:, columns]), columns

    pairs, sums = [], []

    def add_pair(k, mine_sum, sent, landed, seq_sent, seq_landed, own_part):
        moved = remote(sent, landed, sum_sems.at[0, k], sum_sems.at[1, k], partner)
        moved.start()
        own_part()
        moved.wait_recv()
        seq_sent[...] = (mine_sum[...] + landed[...].astype(jnp.float32)).astype(jnp.bfloat16)
        onward = remote(
            seq_sent, seq_landed, sum_sems.at[0, 3 + k], sum_sems.at[1, 3 + k], other_seq
        )
        onward.start()
        pairs.append(moved)
        sums.append(onward)

    @pl.loop(0, width // half)
    def _(at):
        values, columns = product_down(1 - core, at)
        pair_send_down[:, columns] = values.astype(jnp.bfloat16)

    def own_down_part():
        @pl.loop(0, width // half)
        def _(at):
            values, columns = product_down(core, at)
            d_down[:, columns] = values

    add_pair(
        2, d_down, pair_send_down, pair_land_down, seq_send_down, seq_land_down, own_down_part
    )
    for which, mine_sum in enumerate((d_gate, d_up)):

        @pl.loop(0, half // tile)
        def _(at):
            rows = pl.ds(pl.multiple_of(at * tile, tile), tile)
            pair_send[which, rows, :] = product(1 - core, which, at).astype(jnp.bfloat16)

        def own_part(which=which, mine_sum=mine_sum):
            @pl.loop(0, half // tile)
            def _(at):
                mine_sum[pl.ds(pl.multiple_of(at * tile, tile), tile), :] = product(core, which, at)

        add_pair(
            which,
            mine_sum,
            pair_send.at[which],
            pair_land.at[which],
            seq_send.at[which],
            seq_land.at[which],
            own_part,
        )

    back_ref[...] = jnp.zeros_like(back_ref)

    def combine(chunk):
        rows = back_rows.rows(chunk)
        back_rows.wait(chunk)
        back_ref[...] += dot_left(picks[rows, :], back_land[rows, :])

    @pl.loop(2, CHUNKS)
    def _(chunk):
        combine(chunk)

    back_sum[...] = back_ref[...].astype(jnp.bfloat16)
    over = remote(back_sum, back_sum_land, near_sems.at[0, 3], near_sems.at[1, 3], other_y)
    over.start()
    back_ref[...] = jnp.zeros_like(back_ref)

    @pl.loop(0, 2)
    def _(chunk):
        combine(chunk)

    over.wait_recv()
    back_ref[...] += back_sum_land[...].astype(jnp.float32)

    for moved in sums:
        moved.wait_recv()
    for which, mine_sum in enumerate((d_gate, d_up)):
        mine_sum[...] = seq_send[which].astype(jnp.float32) + seq_land[which].astype(jnp.float32)
    d_down[...] = seq_send_down[...].astype(jnp.float32) + seq_land_down[...].astype(jnp.float32)
    outs = out_rows.at[pl.ds(0, 2 * PLANE * CROSS)]
    remote(outs, outs, out_sems.at[0], out_sems.at[1], partner).wait()
    g_rows.wait_sends()
    back_rows.wait_sends()
    for moved in pairs + sums + near + [over]:
        moved.wait_send()


def run_experts(table, normed, grad_low, own_gate, own_up, own_down):
    chips = table.shape[0]
    rows, width = normed.shape
    hidden = own_gate.shape[1]
    slots = chips * BLOCK
    low, high = jnp.bfloat16, jnp.float32
    dma = pltpu.SemaphoreType.DMA
    half, half_down = own_gate.shape[0], own_down.shape[0]
    return pl.pallas_call(
        expert_kernel,
        out_shape=[
            jax.ShapeDtypeStruct((chips, BLOCK, width), low),
            jax.ShapeDtypeStruct((rows, width + SMALL), high),
            jax.ShapeDtypeStruct(own_gate.shape, high),
            jax.ShapeDtypeStruct(own_up.shape, high),
            jax.ShapeDtypeStruct(own_down.shape, high),
        ],
        in_specs=[VMEM] * 6,
        out_specs=[VMEM] * 5,
        scratch_shapes=[
            pltpu.VMEM((2, PLANE, *table.shape[1:]), high),
            pltpu.VMEM((2, rows, width), low),
            pltpu.VMEM((2, rows, width), low),
            pltpu.VMEM((4 * rows, width), low),
            pltpu.VMEM((slots // CHUNKS, 2 * rows), low),
            pltpu.VMEM((slots, rows), low),
            pltpu.VMEM((slots, width + SMALL), low),
            pltpu.VMEM((slots, width), low),
            pltpu.VMEM((slots, width), low),
            pltpu.VMEM((slots, width), low),
            pltpu.VMEM((slots, width), low),
            pltpu.VMEM((slots, width + SMALL), low),
            pltpu.VMEM((rows, width + SMALL), low),
            pltpu.VMEM((rows, width + SMALL), low),
            pltpu.VMEM((slots, hidden), high),
            pltpu.VMEM((slots, hidden), high),
            pltpu.VMEM((slots, hidden), low),
            pltpu.VMEM((slots, hidden), low),
            pltpu.VMEM((slots, hidden), low),
            pltpu.VMEM((CORES * half, hidden), low),
            pltpu.VMEM((CORES * half, hidden), low),
            pltpu.VMEM((CORES * half_down, width), low),
            pltpu.VMEM((2, half, hidden), low),
            pltpu.VMEM((2, half, hidden), low),
            pltpu.VMEM((half_down, width), low),
            pltpu.VMEM((half_down, width), low),
            pltpu.VMEM((2, half, hidden), low),
            pltpu.VMEM((2, half, hidden), low),
            pltpu.VMEM((half_down, width), low),
            pltpu.VMEM((half_down, width), low),
            dma((2, CHUNKS)),
            dma((2, CHUNKS)),
            dma((2, CHUNKS)),
            dma((3, 2)),
            dma((2,)),
            dma((3, 3)),
            dma((2, 6)),
            dma((2, 4)),
        ],
        compiler_params=pltpu.CompilerParams(
            collective_id=2, has_side_effects=True, vmem_limit_bytes=60 * 2**20
        ),
        name="experts",
    )(table, normed, grad_low, own_gate, own_up, own_down)


def from_experts(blocks):
    groups = [
        [chip * CORES + core for chip in range(blocks.shape[0])] for core in range(CORES)
    ]
    return lax.all_to_all(
        blocks, "fsdp", split_axis=0, concat_axis=0, tiled=True, axis_index_groups=groups
    )


def on_device(
    tokens,
    positions,
    routes,
    cotangent,
    first_gain,
    w_query,
    w_key,
    w_value,
    w_out,
    second_gain,
    w_router,
    w_gate,
    w_up,
    w_down,
):
    width = tokens.shape[2]
    rows = tokens.shape[1]
    heads_all = w_query.shape[1] // HD
    kv_all = w_key.shape[1] // HD
    group = heads_all // kv_all
    q_width, kv_width = heads_all * HD, kv_all * HD
    scale = HD ** (-0.5)
    slots = lax.axis_size("fsdp")
    experts = slots // CORES
    seq = lax.axis_index("seq")
    places = BLOCK

    x_own = tokens[0]

    chosen = routes[0]
    ids = jnp.arange(experts, dtype=jnp.int32)
    mask = jnp.any(chosen[:, :, None] == ids[None, None, :], axis=1)
    mask_low = mask.astype(jnp.bfloat16)
    earlier = (jnp.arange(rows)[:, None] > jnp.arange(rows)[None, :]).astype(jnp.bfloat16)
    rank = jnp.where(mask, dot_plain(earlier, mask_low).astype(jnp.int32), -1)
    onehot_wide = rank.T[:, None, :] == jnp.arange(places, dtype=jnp.int32)[None, :, None]
    grad_low = cotangent[0]
    grad_output = grad_low.astype(jnp.float32)

    small = jnp.concatenate(
        [
            w_router,
            first_gain[:, None],
            second_gain[:, None],
            jnp.zeros((w_router.shape[0], SMALL - experts - 2), jnp.bfloat16),
        ],
        axis=1,
    )
    full_a, full_b, x_before, pos_before = gather_shards(
        jnp.concatenate([w_query, w_key], axis=1),
        jnp.concatenate([w_value, w_out, small], axis=1),
        x_own,
        positions,
    )
    query_full, key_full = full_a[:, :q_width], full_a[:, q_width:]
    value_full = full_b[:, :kv_width]
    out_full = full_b[:, kv_width : kv_width + width]
    small_full = full_b[:, kv_width + width :]
    router_full = small_full[:, :experts]
    gain_first = small_full[:, experts].astype(jnp.float32)
    gain_second = small_full[:, experts + 1].astype(jnp.float32)

    x_both = jnp.concatenate([x_before, x_own], axis=0).astype(jnp.float32)
    pos_both = jnp.concatenate([pos_before[0], positions[0]], axis=0)
    inputs = x_both[rows:]
    inverse = rope_base ** (-(2.0 * jnp.arange(HD // 2, dtype=jnp.float32)) / HD)
    angle = pos_both.astype(jnp.float32)[:, None] * inverse[None, :]
    cosine = jnp.cos(angle)[:, None, :]
    sine_table = jnp.sin(angle)[:, None, :]
    inverse_one = lax.rsqrt(jnp.mean(x_both * x_both, axis=-1, keepdims=True) + epsilon)
    normed_both = (x_both * inverse_one * gain_first).astype(jnp.bfloat16)
    normed_own = normed_both[rows:]
    query_pre = dot_plain(normed_own, query_full).reshape(rows, heads_all, HD)
    key_pre = dot_plain(normed_both, key_full).reshape(2 * rows, kv_all, HD)
    query_rot = (rotate(query_pre, cosine[rows:], sine_table[rows:]) * scale).astype(jnp.bfloat16)
    keyed = rotate(key_pre, cosine, sine_table).astype(jnp.bfloat16)
    valued = dot_plain(normed_both, value_full).astype(jnp.bfloat16).reshape(2 * rows, kv_all, HD)
    grouped = query_rot.reshape(rows, kv_all, group, HD)
    key_at = jnp.arange(2 * rows)[None, :]
    allowed = (key_at - rows <= jnp.arange(rows)[:, None]) & ((key_at >= rows) | (seq == 1))
    scores = jnp.einsum("qkgd,pkd->kgqp", grouped, keyed, preferred_element_type=jnp.float32)
    scores = jnp.where(allowed, scores, masked_score)
    peak = jnp.max(scores, axis=-1, keepdims=True)
    raised = jnp.exp(scores - peak)
    probs = raised / jnp.sum(raised, axis=-1, keepdims=True)
    probs_low = probs.astype(jnp.bfloat16)
    attended = (
        jnp.einsum("kgqp,pkd->qkgd", probs_low, valued, preferred_element_type=jnp.float32)
        .astype(jnp.bfloat16)
        .reshape(rows, q_width)
    )
    middle = inputs + dot_plain(attended, out_full)

    inverse_two = lax.rsqrt(jnp.mean(middle * middle, axis=-1, keepdims=True) + epsilon)
    normed_two = (middle * inverse_two * gain_second).astype(jnp.bfloat16)
    logits = jnp.where(mask, dot_plain(normed_two, router_full), masked_score)
    lifted = jnp.where(mask, jnp.exp(logits - jnp.max(logits, axis=-1, keepdims=True)), 0.0)
    gates = lifted / jnp.sum(lifted, axis=-1, keepdims=True)
    table = jnp.stack([rank.T.astype(jnp.float32), gates.T], axis=1)
    part_out, grad_back, grad_gate, grad_up, grad_down = run_experts(
        table, normed_two, grad_low, w_gate[0], w_up[0], w_down[0]
    )
    grad_routed, dots = grad_back[:, :width], grad_back[:, width:]
    returned = from_experts(part_out).reshape(experts * places, width)

    gates_wide = jnp.where(onehot_wide, gates.T[:, None, :], 0.0)
    mixed = dot_left(gates_wide.astype(jnp.bfloat16).reshape(experts * places, rows), returned)
    layer_out = (middle + mixed).astype(jnp.bfloat16)
    weighted = dots[:, :experts] + dots[:, experts : 2 * experts]
    grad_picked = weighted - gates * jnp.sum(weighted, axis=-1, keepdims=True)
    grad_logits = grad_picked.astype(jnp.bfloat16)
    grad_router = dot_left(normed_two, grad_logits)
    grad_normed_two = dot_right(grad_logits, router_full) + grad_routed

    normed = middle * inverse_two
    scaled = grad_normed_two * gain_second
    grad_middle = grad_output + inverse_two * (
        scaled - normed * jnp.mean(scaled * normed, axis=-1, keepdims=True)
    )
    grad_gain_second = jnp.sum(grad_normed_two * normed, axis=0)
    grad_branch = grad_middle.astype(jnp.bfloat16)
    grad_out_full = dot_left(attended, grad_branch).astype(jnp.bfloat16)
    grad_heads = (
        dot_right(grad_branch, out_full).astype(jnp.bfloat16).reshape(rows, kv_all, group, HD)
    )
    grad_probs = jnp.einsum(
        "qkgd,pkd->kgqp", grad_heads, valued, preferred_element_type=jnp.float32
    )
    grad_scores = (
        probs * (grad_probs - jnp.sum(probs * grad_probs, axis=-1, keepdims=True))
    ).astype(jnp.bfloat16)
    grad_value_in = (
        jnp.einsum("kgqp,qkgd->pkd", probs_low, grad_heads, preferred_element_type=jnp.float32)
        .astype(jnp.bfloat16)
        .reshape(2 * rows, kv_width)
    )
    grad_query_rot = (
        jnp.einsum("kgqp,pkd->qkgd", grad_scores, keyed, preferred_element_type=jnp.float32)
        .astype(jnp.bfloat16)
        .astype(jnp.float32)
        .reshape(rows, heads_all, HD)
    )
    grad_key_rot = (
        jnp.einsum("kgqp,qkgd->pkd", grad_scores, grouped, preferred_element_type=jnp.float32)
        .astype(jnp.bfloat16)
        .astype(jnp.float32)
    )
    grad_query_in = (
        (rotate(grad_query_rot, cosine[rows:], -sine_table[rows:]) * scale)
        .astype(jnp.bfloat16)
        .reshape(rows, q_width)
    )
    grad_key_in = (
        rotate(grad_key_rot, cosine, -sine_table).astype(jnp.bfloat16).reshape(2 * rows, kv_width)
    )
    grad_query_full = dot_left(normed_own, grad_query_in).astype(jnp.bfloat16)
    grad_key_full = dot_left(normed_both, grad_key_in).astype(jnp.bfloat16)
    grad_value_full = dot_left(normed_both, grad_value_in).astype(jnp.bfloat16)
    grad_both = dot_right(grad_key_in, key_full) + dot_right(grad_value_in, value_full)
    grad_before = grad_both[:rows].astype(jnp.bfloat16)
    grad_own = grad_both[rows:] + dot_right(grad_query_in, query_full)
    normed_x = x_both * inverse_one
    grad_gain_first = jnp.sum(grad_own * normed_x[rows:], axis=0) + jnp.sum(
        grad_both[:rows] * normed_x[:rows], axis=0
    )
    small_grad = jnp.concatenate(
        [
            grad_router,
            grad_gain_first[:, None],
            grad_gain_second[:, None],
            jnp.zeros((width, SMALL - experts - 2), jnp.float32),
        ],
        axis=1,
    ).astype(jnp.bfloat16)
    sum_out, sum_key, sum_query, sum_value, sum_small, grad_after = scatter_sums(
        [grad_out_full, grad_key_full, grad_query_full, grad_value_full, small_grad],
        (0, 0, 1, 1, 1),
        grad_before,
        1,
    )
    scaled_one = (grad_own + grad_after.astype(jnp.float32)) * gain_first
    grad_tokens = grad_middle + inverse_one[rows:] * (
        scaled_one
        - normed_x[rows:] * jnp.mean(scaled_one * normed_x[rows:], axis=-1, keepdims=True)
    )
    return (
        layer_out[None],
        grad_tokens[None],
        sum_small[:, experts],
        sum_query,
        sum_key,
        sum_value,
        sum_out,
        sum_small[:, experts + 1],
        sum_small[:, :experts],
        grad_gate[None],
        grad_up[None],
        grad_down[None],
    )


def solution(mesh):
    rows = P("fsdp", "seq", None)
    matrix, cube = P("fsdp", None), P("fsdp", None, None)
    return jax.shard_map(
        on_device,
        mesh=mesh,
        in_specs=(
            rows,
            P("fsdp", "seq"),
            rows,
            rows,
            P("fsdp"),
            matrix,
            matrix,
            matrix,
            matrix,
            P("fsdp"),
            matrix,
            cube,
            cube,
            cube,
        ),
        out_specs=(
            rows,
            rows,
            P("fsdp"),
            matrix,
            matrix,
            matrix,
            matrix,
            P("fsdp"),
            matrix,
            cube,
            cube,
            cube,
        ),
        check_vma=False,
    )
```

```python
import functools

import jax
import jax.numpy as jnp
from jax import lax
from jax.experimental import pallas as pl
from jax.experimental.pallas import tpu as pltpu
from jax.sharding import PartitionSpec as P

HD = 64
CORES = 2
SMALL = 128

epsilon = 1e-06
rope_base = 10000.0
masked_score = -1e30
MESH = pl.DeviceIdType.MESH
ANY = pl.BlockSpec(memory_space=pl.ANY)
VMEM = pl.BlockSpec(memory_space=pltpu.VMEM)


def dot_plain(left, right):
    return jnp.dot(left, right, preferred_element_type=jnp.float32)


def dot_left(left, right):
    return lax.dot_general(
        left, right, (((0,), (0,)), ((), ())), preferred_element_type=jnp.float32
    )


def dot_right(left, right):
    return lax.dot_general(
        left, right, (((1,), (1,)), ((), ())), preferred_element_type=jnp.float32
    )


def rms_scale(values, gain):
    return values * lax.rsqrt(jnp.mean(values * values, axis=-1, keepdims=True) + epsilon) * gain


def rotate(values, cosine, sine_table):
    middle = values.shape[-1] // 2
    first_half = values[..., :middle]
    second_half = values[..., middle:]
    return jnp.concatenate(
        [
            first_half * cosine - second_half * sine_table,
            second_half * cosine + first_half * sine_table,
        ],
        axis=-1,
    )


LONG = 4


def coordinates():
    seq, me = lax.axis_index("seq"), lax.axis_index("fsdp")
    return seq, me // 32, (me // 8) % LONG, (me // 2) % LONG, me % CORES


def device(seq, y, x, z, core):
    return (seq, ((y * LONG + x) * LONG + z) * CORES + core)


def enter(targets):
    barrier = pltpu.get_barrier_semaphore()
    for target in targets:
        pl.semaphore_signal(barrier, inc=1, device_id=target, device_id_type=MESH)
    pl.semaphore_wait(barrier, len(targets))


def neighbours():
    seq, y, x, z, core = coordinates()
    return [
        device(seq, y, x, z, 1 - core),
        device(seq, 1 - y, x, z, core),
        device(seq, y, lax.rem(x + 1, LONG), z, core),
        device(seq, y, lax.rem(x + 3, LONG), z, core),
        device(seq, y, x, lax.rem(z + 1, LONG), core),
        device(seq, y, x, lax.rem(z + 3, LONG), core),
        device(1 - seq, y, x, z, core),
    ]


def gather_kernel(
    w_query,
    w_key,
    w_value,
    w_out,
    small,
    x_own,
    pos_own,
    full_a,
    full_b,
    x_other,
    pos_other,
    shard_a,
    shard_b,
    *sems,
):
    send, recv, core_send, core_recv, seq_send, seq_recv, local = sems
    for shard, pieces in ((shard_a, (w_query, w_key)), (shard_b, (w_value, w_out, small))):
        at = 0
        for piece in pieces:
            shard[:, at : at + piece.shape[1]] = piece[...]
            at += piece.shape[1]
    seq, y, x, z, core = coordinates()
    enter(neighbours())
    other_seq = device(1 - seq, y, x, z, core)
    swaps = [
        pltpu.make_async_remote_copy(
            src_ref=source,
            dst_ref=target,
            send_sem=seq_send.at[i],
            recv_sem=seq_recv.at[i],
            device_id=other_seq,
            device_id_type=MESH,
        )
        for i, (source, target) in enumerate(((x_own, x_other), (pos_own, pos_other)))
    ]
    fulls = (full_a, full_b)
    first_at, second_at = (x, z), (z, x)

    def along(i, stage, shift):
        if (i == 0) == (stage == 0):
            return device(seq, y, lax.rem(x + shift, LONG), z, core)
        return device(seq, y, x, lax.rem(z + shift, LONG), core)

    def block(i, stage, shift, ys):
        at = lax.rem((first_at if stage == 0 else second_at)[i] + shift, LONG)
        if stage == 0:
            xs, zs = (at, z) if i == 0 else (x, at)
        else:
            xs, zs = (slice(None), at) if i == 0 else (at, slice(None))
        return fulls[i].at[ys, xs, zs, core]

    def copy(i, k, part, target):
        return pltpu.make_async_remote_copy(
            src_ref=part,
            dst_ref=part,
            send_sem=send.at[i, k],
            recv_sem=recv.at[i, k],
            device_id=target,
            device_id_type=MESH,
        )

    both = slice(None)
    own = []
    started = []

    def start(i, k, part, target):
        moved = copy(i, k, part, target)
        moved.start()
        started.append(moved)

    crossing = []

    def cross(i, k, index):
        for side, wait in ((core, False), (1 - core, True)):
            part = fulls[i].at[(*index, side)]
            moved = pltpu.make_async_remote_copy(
                src_ref=part,
                dst_ref=part,
                send_sem=core_send.at[i, k],
                recv_sem=core_recv.at[i, k],
                device_id=device(seq, y, x, z, 1 - core),
                device_id_type=MESH,
            )
            if wait:
                crossing.append((moved, last))
            else:
                moved.start()
                last = moved

    for i, shard in enumerate((shard_a, shard_b)):
        kept = pltpu.make_async_copy(shard, fulls[i].at[y, x, z, core], local.at[i])
        kept.start()
        own.append(kept)
        outgoing = pltpu.make_async_remote_copy(
            src_ref=shard,
            dst_ref=fulls[i].at[y, x, z, core],
            send_sem=send.at[i, 0],
            recv_sem=recv.at[i, 0],
            device_id=device(seq, 1 - y, x, z, core),
            device_id_type=MESH,
        )
        outgoing.start()
        started.append(outgoing)
    for moved in swaps:
        moved.start()
    for i in range(2):
        own[i].wait()
        copy(i, 0, fulls[i].at[1 - y, x, z, core], other_seq).wait_recv()

    for stage in range(2):
        base = 1 + 4 * stage
        for i in range(2):
            start(i, base, block(i, stage, 0, both), along(i, stage, 1))
            start(i, base + 1, block(i, stage, 0, both), along(i, stage, 3))
            if stage == 1:
                at = second_at[i]
                cross(i, 0, (both, both, at) if i == 0 else (both, at, both))
        for i in range(2):
            copy(i, base, block(i, stage, 3, both), other_seq).wait_recv()
            start(i, base + 2, block(i, stage, 3, 0), along(i, stage, 1))
            copy(i, base + 1, block(i, stage, 1, both), other_seq).wait_recv()
            start(i, base + 3, block(i, stage, 1, 1), along(i, stage, 3))
            if stage == 1:
                for k, shift in ((1, 3), (2, 1)):
                    at = lax.rem(second_at[i] + shift, LONG)
                    cross(i, k, (both, both, at) if i == 0 else (both, at, both))
        for i in range(2):
            copy(i, base + 2, block(i, stage, 2, 0), other_seq).wait_recv()
            copy(i, base + 3, block(i, stage, 2, 1), other_seq).wait_recv()
            if stage == 1:
                at = lax.rem(second_at[i] + 2, LONG)
                cross(i, 3, (both, both, at) if i == 0 else (both, at, both))

    for arriving, leaving in crossing:
        arriving.wait_recv()
        leaving.wait_send()
    for moved in started:
        moved.wait_send()
    for moved in swaps:
        moved.wait()


def gather_shards(w_query, w_key, w_value, w_out, small, x_own, pos_own):
    count = lax.axis_size("fsdp")
    chips = (count // (LONG * LONG * CORES), LONG, LONG, CORES)
    height = w_query.shape[0]
    shards = [
        jax.ShapeDtypeStruct((height, sum(piece.shape[1] for piece in pieces)), w_query.dtype)
        for pieces in ((w_query, w_key), (w_value, w_out, small))
    ]
    outs = [jax.ShapeDtypeStruct((*chips, *shard.shape), shard.dtype) for shard in shards]
    outs += [jax.ShapeDtypeStruct(array.shape, array.dtype) for array in (x_own, pos_own)]
    full_a, full_b, x_other, pos_other = pl.pallas_call(
        gather_kernel,
        out_shape=outs,
        in_specs=[VMEM] * 5 + [ANY] * 2,
        out_specs=[ANY] * 4,
        scratch_shapes=[pltpu.VMEM(shard.shape, shard.dtype) for shard in shards]
        + [
            pltpu.SemaphoreType.DMA((2, 9)),
            pltpu.SemaphoreType.DMA((2, 9)),
            pltpu.SemaphoreType.DMA((2, 4)),
            pltpu.SemaphoreType.DMA((2, 4)),
            pltpu.SemaphoreType.DMA((2,)),
            pltpu.SemaphoreType.DMA((2,)),
            pltpu.SemaphoreType.DMA((2,)),
        ],
        compiler_params=pltpu.CompilerParams(collective_id=0, has_side_effects=True),
        name="gather_weights",
    )(w_query, w_key, w_value, w_out, small, x_own, pos_own)
    return (
        full_a.reshape(count * height, full_a.shape[-1]),
        full_b.reshape(count * height, full_b.shape[-1]),
        x_other,
        pos_other,
    )


def widen(values):
    return values.astype(jnp.float32)


def scatter_kernel(groups, before, *refs):
    number = len(groups)
    after, refs = refs[2 * number], refs[: 2 * number] + refs[2 * number + 1 :]
    parts, totals = refs[:number], refs[number : 2 * number]
    halves, landed, second, landed_two, third, landed_three = (
        refs[k * number : (k + 1) * number] for k in range(2, 8)
    )
    core_send, core_recv, send, recv, swap_sems = refs[8 * number :]
    seq, y, x, z, core = coordinates()
    far_y = [
        device(seq, 1 - y, x, z, core),
        device(1 - seq, y, x, z, core),
        device(1 - seq, 1 - y, x, z, core),
    ]
    lines = [
        [device(seq, y, lax.rem(x + j, LONG), z, core) for j in (1, 2, 3)],
        [device(seq, y, x, lax.rem(z + j, LONG), core) for j in (1, 2, 3)],
    ]
    enter([device(seq, y, x, z, 1 - core)] + far_y + lines[0] + lines[1])

    def index(i, at):
        return (slice(None), slice(None), at) if groups[i] == 0 else (slice(None), at)

    first_at = [z if group == 0 else x for group in groups]
    second_at = [x if group == 0 else z for group in groups]
    first_line = [lines[1] if group == 0 else lines[0] for group in groups]
    second_line = [lines[0] if group == 0 else lines[1] for group in groups]

    def remote(source, target, to, sems, i, k):
        return pltpu.make_async_remote_copy(
            src_ref=source,
            dst_ref=target,
            send_sem=sems[0].at[i, k],
            recv_sem=sems[1].at[i, k],
            device_id=to,
            device_id_type=MESH,
        )

    def part_of(i, at, side):
        if groups[i] == 0:
            return parts[i].at[:, :, at, side]
        return parts[i].at[:, at, :, side]

    order = (2, 1, 3, 0)
    waiting = []
    across = {}
    for j in order:
        for i in range(number):
            at = lax.rem(first_at[i] + j, LONG)
            moved = remote(
                part_of(i, at, 1 - core),
                halves[i].at[j],
                device(seq, y, x, z, 1 - core),
                (core_send, core_recv),
                i,
                j,
            )
            moved.start()
            across[i, j] = moved
    swap = pltpu.make_async_remote_copy(
        src_ref=before,
        dst_ref=after,
        send_sem=swap_sems.at[0],
        recv_sem=swap_sems.at[1],
        device_id=far_y[1],
        device_id_type=MESH,
    )
    swap.start()
    for j in order:
        for i in range(number):
            across[i, j].wait_recv()
            at = lax.rem(first_at[i] + j, LONG)
            both = widen(halves[i][j]) + widen(part_of(i, at, core)[...])
            halves[i][j] = both.astype(jnp.bfloat16)
            if j:
                moved = remote(
                    halves[i].at[j],
                    landed[i].at[j - 1],
                    first_line[i][j - 1],
                    (send, recv),
                    i,
                    j - 1,
                )
                moved.start()
                waiting.append(moved)
    hops = {}
    for i in range(number):
        for j in (1, 2, 3):
            remote(halves[i].at[j], landed[i].at[j - 1], far_y[0], (send, recv), i, j - 1).wait_recv()
        total = widen(halves[i][0])
        for j in range(3):
            total = total + widen(landed[i][j])
        second[i][...] = total.astype(jnp.bfloat16)
        for j in (2, 1, 3):
            at = lax.rem(second_at[i] + j, LONG)
            moved = remote(
                second[i].at[:, at],
                landed_two[i].at[j - 1],
                second_line[i][j - 1],
                (send, recv),
                i,
                2 + j,
            )
            moved.start()
            waiting.append(moved)
            hops[i, j] = moved
    for i in range(number):
        for j in (1, 2, 3):
            hops[i, j].wait_recv()
        total = widen(second[i][:, second_at[i]])
        for j in range(3):
            total = total + widen(landed_two[i][j])
        third[i][...] = total.astype(jnp.bfloat16)
        landed_three[i][seq * 2 + y] = third[i][y]
        for k, wanted in enumerate((1 - y, y, 1 - y)):
            moved = remote(
                third[i].at[wanted],
                landed_three[i].at[seq * 2 + y],
                far_y[k],
                (send, recv),
                i,
                6 + k,
            )
            moved.start()
            waiting.append(moved)
            hops[i, 3 + k] = moved
    for i in range(number):
        for k in range(3):
            hops[i, 3 + k].wait_recv()
        total = widen(landed_three[i][0])
        for k in range(1, 4):
            total = total + widen(landed_three[i][k])
        totals[i][...] = total
    for moved in waiting:
        moved.wait_send()
    for i in range(number):
        for j in order:
            across[i, j].wait_send()
    swap.wait()


def scatter_sums(fulls, groups, before, identity):
    count = lax.axis_size("fsdp")
    number = len(fulls)
    rows = fulls[0].shape[0] // count
    widths = [full.shape[1] for full in fulls]
    ys = count // (LONG * LONG * CORES)
    parts = [full.reshape(ys, LONG, LONG, CORES, rows, full.shape[1]) for full in fulls]

    def room(*lead):
        return [pltpu.VMEM((*lead, rows, width), jnp.bfloat16) for width in widths]

    return pl.pallas_call(
        functools.partial(scatter_kernel, groups),
        out_shape=[jax.ShapeDtypeStruct((rows, width), jnp.float32) for width in widths]
        + [jax.ShapeDtypeStruct(before.shape, before.dtype)],
        in_specs=[ANY] + [VMEM] * number,
        out_specs=[VMEM] * number + [ANY],
        scratch_shapes=room(LONG, ys, LONG)
        + room(LONG - 1, ys, LONG)
        + room(ys, LONG)
        + room(LONG - 1, ys)
        + room(ys)
        + room(2 * ys)
        + [
            pltpu.SemaphoreType.DMA((number, LONG)),
            pltpu.SemaphoreType.DMA((number, LONG)),
            pltpu.SemaphoreType.DMA((number, 9)),
            pltpu.SemaphoreType.DMA((number, 9)),
            pltpu.SemaphoreType.DMA((2,)),
        ],
        compiler_params=pltpu.CompilerParams(
            collective_id=identity, has_side_effects=True, vmem_limit_bytes=48 * 2**20
        ),
        name="scatter_gradients",
    )(before, *parts)


CHUNKS = 4
SAME, CROSS = 32, 16
BLOCK = SAME + CROSS
PLANE = LONG * LONG


def chip_at(sign, step, other_y=0):
    seq, y, x, z, core = coordinates()
    inner = step % PLANE
    dx = inner % LONG
    dz = (dx + inner // LONG) % LONG
    return ((y + other_y) % 2 * LONG + (x + sign * dx + LONG) % LONG) * LONG + (
        z + sign * dz + LONG
    ) % LONG


def remote(source, target, sends, recvs, to):
    return pltpu.make_async_remote_copy(
        src_ref=source,
        dst_ref=target,
        send_sem=sends,
        recv_sem=recvs,
        device_id=to,
        device_id_type=MESH,
    )


class Rows:
    def __init__(self, source, target, sems, self_sems, sign):
        self.source, self.target, self.sems, self.self_sems = source, target, sems, self_sems
        self.sign, self.steps = sign, 2 * PLANE // CHUNKS
        self.depth = self.steps * BLOCK
        self.seq, _, _, _, self.core = coordinates()
        self.partner = (self.seq, lax.axis_index("fsdp") + 1 - 2 * self.core)

    def rows(self, chunk):
        return pl.ds(pl.multiple_of(chunk * self.depth, 16), self.depth)

    def own(self, step):
        rows = pl.ds(pl.multiple_of(step * BLOCK, 16), SAME)
        return pltpu.make_async_copy(
            self.source.at[rows], self.target.at[rows], self.self_sems.at[step // PLANE]
        )

    def send(self, chunk):
        @pl.loop(0, self.steps)
        def _(inner):
            step = chunk * self.steps + inner
            chip = chip_at(self.sign, step)
            row = pl.multiple_of(step * BLOCK, 16)
            same, cross = pl.ds(row, SAME), pl.ds(pl.multiple_of(row + SAME, 16), CROSS)

            @pl.when(step % PLANE == 0)
            def _():
                self.own(step).start()

            sems = (self.sems.at[0, chunk], self.sems.at[1, chunk])

            @pl.when(step % PLANE > 0)
            def _():
                to = (self.seq, chip * CORES + self.core)
                remote(self.source.at[same], self.target.at[same], *sems, to).start()

            to = (self.seq, chip * CORES + 1 - self.core)
            remote(self.source.at[cross], self.target.at[cross], *sems, to).start()

    def whole(self, buffer, chunk, first):
        rows = self.rows(chunk)
        if first:
            rows = pl.ds(pl.multiple_of(chunk * self.depth + SAME, 16), self.depth - SAME)
        part = buffer.at[rows]
        return remote(part, part, self.sems.at[0, chunk], self.sems.at[1, chunk], self.partner)

    def wait(self, chunk):
        @pl.when(chunk % 2 == 0)
        def _():
            self.own(chunk * self.steps).wait()
            self.whole(self.target, chunk, True).wait_recv()

        @pl.when(chunk % 2 == 1)
        def _():
            self.whole(self.target, chunk, False).wait_recv()

    def wait_sends(self):
        for chunk in range(CHUNKS):
            self.whole(self.source, chunk, chunk % 2 == 0).wait_send()


def expert_kernel(
    table,
    normed,
    grad_low,
    own_gate,
    own_up,
    own_down,
    out_ref,
    back_ref,
    d_gate,
    d_up,
    d_down,
    table_both,
    normed_both,
    grad_both,
    grad_twice,
    gated,
    picks,
    x_send,
    g_send,
    x_land,
    g_land,
    out_rows,
    back_land,
    back_sum,
    back_sum_land,
    gate_pre,
    up_pre,
    hidden,
    d_gate_pre,
    d_up_pre,
    w_gate,
    w_up,
    w_down,
    pair_send,
    pair_land,
    pair_send_down,
    pair_land_down,
    seq_send,
    seq_land,
    seq_send_down,
    seq_land_down,
    x_sems,
    g_sems,
    back_sems,
    self_sems,
    out_sems,
    weight_sems,
    sum_sems,
    near_sems,
):
    seq, y, x, z, core = coordinates()
    me = lax.axis_index("fsdp")
    rows_own, width = normed.shape
    partner = (seq, me + 1 - 2 * core)
    other_seq = (1 - seq, me)
    other_y = device(seq, 1 - y, x, z, core)

    barrier = pltpu.get_barrier_semaphore()
    for target in (partner, other_seq, other_y):
        pl.semaphore_signal(barrier, inc=1, device_id=target, device_id_type=MESH)

    @pl.loop(1, PLANE)
    def _(step):
        for side in range(CORES):
            pl.semaphore_signal(
                barrier,
                inc=1,
                device_id=(seq, chip_at(-1, step) * CORES + side),
                device_id_type=MESH,
            )

    pl.semaphore_wait(barrier, CORES * PLANE + 1)

    mine = pl.ds(pl.multiple_of(y * PLANE, PLANE), PLANE)
    theirs = pl.ds(pl.multiple_of((1 - y) * PLANE, PLANE), PLANE)
    near = [
        remote(source, target.at[1], near_sems.at[0, i], near_sems.at[1, i], other_y)
        for i, (source, target) in enumerate(
            ((table.at[theirs], table_both), (normed, normed_both), (grad_low, grad_both))
        )
    ]
    for moved in near:
        moved.start()

    weights = []
    for i, (own, full) in enumerate(((own_gate, w_gate), (own_up, w_up), (own_down, w_down))):
        height = own.shape[0]
        place = full.at[pl.ds(pl.multiple_of(core * height, height), height)]
        kept = pltpu.make_async_copy(own, place, weight_sems.at[2, i])
        sent = remote(own, place, weight_sems.at[0, i], weight_sems.at[1, i], partner)
        kept.start()
        sent.start()
        weights.append((kept, sent))

    x_rows = Rows(x_send.at[:, pl.ds(0, width)], x_land, x_sems, self_sems.at[0], 1)
    g_rows = Rows(g_send, g_land, g_sems, self_sems.at[1], 1)
    back_rows = Rows(x_send, back_land, back_sems, self_sems.at[2], -1)
    steps, depth = x_rows.steps, x_rows.depth

    table_both[0] = table[mine]
    normed_both[0] = normed[...]
    grad_both[0] = grad_low[...]
    place = lax.broadcasted_iota(jnp.int32, (BLOCK, rows_own), 0).astype(jnp.float32)

    def entry(step):
        return table_both[step // PLANE, chip_at(1, step) % PLANE]

    def send_x(chunk):
        @pl.loop(0, steps)
        def _(inner):
            step = chunk * steps + inner
            found = jnp.where(entry(step)[0:1] == place, 1.0, 0.0)
            picks[pl.ds(pl.multiple_of(step * BLOCK, 16), BLOCK), :] = found.astype(jnp.bfloat16)

        rows = x_rows.rows(chunk)
        values = dot_plain(picks[rows, :], normed_both[chunk // 2])
        x_send[rows, :width] = values.astype(jnp.bfloat16)
        x_rows.send(chunk)

    def send_g(chunk):
        @pl.loop(0, steps)
        def _(inner):
            line = entry(chunk * steps + inner)
            weight = jnp.where(line[0:1] == place, line[1:2], 0.0)
            high = weight.astype(jnp.bfloat16)
            rest = (weight - high.astype(jnp.float32)).astype(jnp.bfloat16)
            rows = pl.ds(pl.multiple_of(inner * BLOCK, 16), BLOCK)
            gated[rows, :rows_own] = high
            gated[rows, rows_own:] = rest

        g_send[g_rows.rows(chunk), :] = dot_plain(
            gated[...], grad_twice[pl.ds(pl.multiple_of(chunk // 2 * 2 * rows_own, 16), 2 * rows_own)]
        ).astype(jnp.bfloat16)
        g_rows.send(chunk)

    for chunk in (0, 1):
        send_x(chunk)
    near[0].wait_recv()
    near[1].wait_recv()
    for chunk in (2, 3):
        send_x(chunk)
    near[2].wait_recv()
    for i in range(4):
        grad_twice[pl.ds(i * rows_own, rows_own)] = grad_both[i // 2]

    @pl.loop(0, CHUNKS)
    def _(turn):
        send_g((turn + 2) % CHUNKS)

    for kept, sent in weights:
        kept.wait()
        sent.wait()

    @pl.loop(0, CHUNKS)
    def _(chunk):
        rows = x_rows.rows(chunk)
        x_rows.wait(chunk)
        served = x_land[rows, :]
        gate = dot_plain(served, w_gate[...])
        up = dot_plain(served, w_up[...])
        gate_pre[rows, :] = gate
        up_pre[rows, :] = up
        low = (gate * jax.nn.sigmoid(gate) * up).astype(jnp.bfloat16)
        hidden[rows, :] = low
        out_rows[rows, :] = dot_plain(low, w_down[...]).astype(jnp.bfloat16)

        @pl.loop(0, steps)
        def _(inner):
            step = chunk * steps + inner
            row = pl.multiple_of(step * BLOCK, 16)
            chip = chip_at(-1, step, step // PLANE)
            out_ref[chip, :SAME, :] = out_rows[pl.ds(row, SAME), :]
            remote(
                out_rows.at[pl.ds(pl.multiple_of(row + SAME, 16), CROSS)],
                out_ref.at[chip, pl.ds(SAME, CROSS)],
                out_sems.at[0],
                out_sems.at[1],
                partner,
            ).start()

    x_rows.wait_sends()

    lane = lax.broadcasted_iota(jnp.int32, (depth, SMALL), 1)
    expert = me // CORES

    @pl.loop(0, CHUNKS)
    def _(turn):
        chunk = (turn + 2) % CHUNKS
        rows = g_rows.rows(chunk)
        g_rows.wait(chunk)
        low = g_land[rows, :]
        dots = jnp.sum(
            low.astype(jnp.float32) * out_rows[rows, :].astype(jnp.float32), axis=1, keepdims=True
        )
        high = dots.astype(jnp.bfloat16).astype(jnp.float32)
        x_send[rows, width:] = jnp.where(
            lane == expert, high, jnp.where(lane == expert + 2 * PLANE, dots - high, 0.0)
        ).astype(jnp.bfloat16)
        d_hidden = dot_right(low, w_down[...])
        gate, up = gate_pre[rows, :], up_pre[rows, :]
        sigmoid = jax.nn.sigmoid(gate)
        one = (d_hidden * up * sigmoid * (1.0 + gate * (1.0 - sigmoid))).astype(jnp.bfloat16)
        two = (d_hidden * (gate * sigmoid)).astype(jnp.bfloat16)
        d_gate_pre[rows, :] = one
        d_up_pre[rows, :] = two
        x_send[rows, :width] = (dot_right(one, w_gate[...]) + dot_right(two, w_up[...])).astype(
            jnp.bfloat16
        )
        back_rows.send(chunk)

    tile = 256
    half = own_gate.shape[0]
    half_down = own_down.shape[0]

    def product(side, which, at):
        start = pl.multiple_of(side * half + at * tile, tile)
        return dot_left(x_land[:, pl.ds(start, tile)], (d_gate_pre, d_up_pre)[which][...])

    def product_down(side, at):
        start = pl.multiple_of(side * half_down, half_down)
        columns = pl.ds(pl.multiple_of(at * half, half), half)
        return dot_left(hidden[:, pl.ds(start, half_down)], g_land[:, columns]), columns

    pairs, sums = [], []

    def add_pair(k, mine_sum, sent, landed, seq_sent, seq_landed, own_part):
        moved = remote(sent, landed, sum_sems.at[0, k], sum_sems.at[1, k], partner)
        moved.start()
        own_part()
        moved.wait_recv()
        seq_sent[...] = (mine_sum[...] + landed[...].astype(jnp.float32)).astype(jnp.bfloat16)
        onward = remote(
            seq_sent, seq_landed, sum_sems.at[0, 3 + k], sum_sems.at[1, 3 + k], other_seq
        )
        onward.start()
        pairs.append(moved)
        sums.append(onward)

    @pl.loop(0, width // half)
    def _(at):
        values, columns = product_down(1 - core, at)
        pair_send_down[:, columns] = values.astype(jnp.bfloat16)

    def own_down_part():
        @pl.loop(0, width // half)
        def _(at):
            values, columns = product_down(core, at)
            d_down[:, columns] = values

    add_pair(
        2, d_down, pair_send_down, pair_land_down, seq_send_down, seq_land_down, own_down_part
    )
    for which, mine_sum in enumerate((d_gate, d_up)):

        @pl.loop(0, half // tile)
        def _(at):
            rows = pl.ds(pl.multiple_of(at * tile, tile), tile)
            pair_send[which, rows, :] = product(1 - core, which, at).astype(jnp.bfloat16)

        def own_part(which=which, mine_sum=mine_sum):
            @pl.loop(0, half // tile)
            def _(at):
                mine_sum[pl.ds(pl.multiple_of(at * tile, tile), tile), :] = product(core, which, at)

        add_pair(
            which,
            mine_sum,
            pair_send.at[which],
            pair_land.at[which],
            seq_send.at[which],
            seq_land.at[which],
            own_part,
        )

    back_ref[...] = jnp.zeros_like(back_ref)

    def combine(chunk):
        rows = back_rows.rows(chunk)
        back_rows.wait(chunk)
        back_ref[...] += dot_left(picks[rows, :], back_land[rows, :])

    @pl.loop(2, CHUNKS)
    def _(chunk):
        combine(chunk)

    back_sum[...] = back_ref[...].astype(jnp.bfloat16)
    over = remote(back_sum, back_sum_land, near_sems.at[0, 3], near_sems.at[1, 3], other_y)
    over.start()
    back_ref[...] = jnp.zeros_like(back_ref)

    @pl.loop(0, 2)
    def _(chunk):
        combine(chunk)

    over.wait_recv()
    back_ref[...] += back_sum_land[...].astype(jnp.float32)

    for moved in sums:
        moved.wait_recv()
    for which, mine_sum in enumerate((d_gate, d_up)):
        mine_sum[...] = seq_send[which].astype(jnp.float32) + seq_land[which].astype(jnp.float32)
    d_down[...] = seq_send_down[...].astype(jnp.float32) + seq_land_down[...].astype(jnp.float32)
    outs = out_rows.at[pl.ds(0, 2 * PLANE * CROSS)]
    remote(outs, outs, out_sems.at[0], out_sems.at[1], partner).wait()
    g_rows.wait_sends()
    back_rows.wait_sends()
    for moved in pairs + sums + near + [over]:
        moved.wait_send()


def run_experts(table, normed, grad_low, own_gate, own_up, own_down):
    chips = table.shape[0]
    rows, width = normed.shape
    hidden = own_gate.shape[1]
    slots = chips * BLOCK
    low, high = jnp.bfloat16, jnp.float32
    dma = pltpu.SemaphoreType.DMA
    half, half_down = own_gate.shape[0], own_down.shape[0]
    return pl.pallas_call(
        expert_kernel,
        out_shape=[
            jax.ShapeDtypeStruct((chips, BLOCK, width), low),
            jax.ShapeDtypeStruct((rows, width + SMALL), high),
            jax.ShapeDtypeStruct(own_gate.shape, high),
            jax.ShapeDtypeStruct(own_up.shape, high),
            jax.ShapeDtypeStruct(own_down.shape, high),
        ],
        in_specs=[VMEM] * 6,
        out_specs=[VMEM] * 5,
        scratch_shapes=[
            pltpu.VMEM((2, PLANE, *table.shape[1:]), high),
            pltpu.VMEM((2, rows, width), low),
            pltpu.VMEM((2, rows, width), low),
            pltpu.VMEM((4 * rows, width), low),
            pltpu.VMEM((slots // CHUNKS, 2 * rows), low),
            pltpu.VMEM((slots, rows), low),
            pltpu.VMEM((slots, width + SMALL), low),
            pltpu.VMEM((slots, width), low),
            pltpu.VMEM((slots, width), low),
            pltpu.VMEM((slots, width), low),
            pltpu.VMEM((slots, width), low),
            pltpu.VMEM((slots, width + SMALL), low),
            pltpu.VMEM((rows, width + SMALL), low),
            pltpu.VMEM((rows, width + SMALL), low),
            pltpu.VMEM((slots, hidden), high),
            pltpu.VMEM((slots, hidden), high),
            pltpu.VMEM((slots, hidden), low),
            pltpu.VMEM((slots, hidden), low),
            pltpu.VMEM((slots, hidden), low),
            pltpu.VMEM((CORES * half, hidden), low),
            pltpu.VMEM((CORES * half, hidden), low),
            pltpu.VMEM((CORES * half_down, width), low),
            pltpu.VMEM((2, half, hidden), low),
            pltpu.VMEM((2, half, hidden), low),
            pltpu.VMEM((half_down, width), low),
            pltpu.VMEM((half_down, width), low),
            pltpu.VMEM((2, half, hidden), low),
            pltpu.VMEM((2, half, hidden), low),
            pltpu.VMEM((half_down, width), low),
            pltpu.VMEM((half_down, width), low),
            dma((2, CHUNKS)),
            dma((2, CHUNKS)),
            dma((2, CHUNKS)),
            dma((3, 2)),
            dma((2,)),
            dma((3, 3)),
            dma((2, 6)),
            dma((2, 4)),
        ],
        compiler_params=pltpu.CompilerParams(
            collective_id=2, has_side_effects=True, vmem_limit_bytes=60 * 2**20
        ),
        name="experts",
    )(table, normed, grad_low, own_gate, own_up, own_down)


def from_experts(blocks):
    groups = [
        [chip * CORES + core for chip in range(blocks.shape[0])] for core in range(CORES)
    ]
    return lax.all_to_all(
        blocks, "fsdp", split_axis=0, concat_axis=0, tiled=True, axis_index_groups=groups
    )


def pack_small(router, first, second, shards):
    rows, experts = router.shape
    height = rows // shards
    gains = jnp.concatenate(
        [first.reshape(shards, 1, height), second.reshape(shards, 1, height)], axis=2
    )
    gains = jnp.pad(gains, ((0, 0), (0, height - 1), (0, SMALL - experts - 2 * height)))
    return jnp.concatenate([router, gains.reshape(rows, SMALL - experts)], axis=1)


def on_device(
    tokens,
    positions,
    routes,
    cotangent,
    first_gain,
    w_query,
    w_key,
    w_value,
    w_out,
    second_gain,
    w_router,
    w_gate,
    w_up,
    w_down,
):
    width = tokens.shape[2]
    rows = tokens.shape[1]
    heads_all = w_query.shape[1] // HD
    kv_all = w_key.shape[1] // HD
    group = heads_all // kv_all
    q_width, kv_width = heads_all * HD, kv_all * HD
    scale = HD ** (-0.5)
    slots = lax.axis_size("fsdp")
    experts = slots // CORES
    seq = lax.axis_index("seq")
    places = BLOCK

    x_own = tokens[0]

    chosen = routes[0]
    ids = jnp.arange(experts, dtype=jnp.int32)
    mask = jnp.any(chosen[:, :, None] == ids[None, None, :], axis=1)
    mask_low = mask.astype(jnp.bfloat16)
    earlier = (jnp.arange(rows)[:, None] > jnp.arange(rows)[None, :]).astype(jnp.bfloat16)
    rank = jnp.where(mask, dot_plain(earlier, mask_low).astype(jnp.int32), -1)
    onehot_wide = rank.T[:, None, :] == jnp.arange(places, dtype=jnp.int32)[None, :, None]
    grad_low = cotangent[0]
    grad_output = grad_low.astype(jnp.float32)

    small = pack_small(w_router, first_gain, second_gain, 1)
    full_a, full_b, x_before, pos_before = gather_shards(
        w_query,
        w_key,
        w_value,
        w_out,
        small,
        x_own,
        positions,
    )
    query_full, key_full = full_a[:, :q_width], full_a[:, q_width:]
    value_full = full_b[:, :kv_width]
    out_full = full_b[:, kv_width : kv_width + width]
    small_full = full_b[:, kv_width + width :]
    router_full = small_full[:, :experts]
    height = w_router.shape[0]
    gains = small_full.reshape(slots, height, SMALL)[:, 0, experts : experts + 2 * height]
    gain_first = gains[:, :height].reshape(-1).astype(jnp.float32)
    gain_second = gains[:, height:].reshape(-1).astype(jnp.float32)

    x_both = jnp.concatenate([x_before, x_own], axis=0).astype(jnp.float32)
    pos_both = jnp.concatenate([pos_before[0], positions[0]], axis=0)
    inputs = x_both[rows:]
    inverse = rope_base ** (-(2.0 * jnp.arange(HD // 2, dtype=jnp.float32)) / HD)
    angle = pos_both.astype(jnp.float32)[:, None] * inverse[None, :]
    cosine = jnp.cos(angle)[:, None, :]
    sine_table = jnp.sin(angle)[:, None, :]
    inverse_one = lax.rsqrt(jnp.mean(x_both * x_both, axis=-1, keepdims=True) + epsilon)
    normed_both = (x_both * inverse_one * gain_first).astype(jnp.bfloat16)
    normed_own = normed_both[rows:]
    query_pre = dot_plain(normed_own, query_full).reshape(rows, heads_all, HD)
    key_pre = dot_plain(normed_both, key_full).reshape(2 * rows, kv_all, HD)
    query_rot = (rotate(query_pre, cosine[rows:], sine_table[rows:]) * scale).astype(jnp.bfloat16)
    keyed = rotate(key_pre, cosine, sine_table).astype(jnp.bfloat16)
    valued = dot_plain(normed_both, value_full).astype(jnp.bfloat16).reshape(2 * rows, kv_all, HD)
    grouped = query_rot.reshape(rows, kv_all, group, HD)
    key_at = jnp.arange(2 * rows)[None, :]
    allowed = (key_at - rows <= jnp.arange(rows)[:, None]) & ((key_at >= rows) | (seq == 1))
    scores = jnp.einsum("qkgd,pkd->kgqp", grouped, keyed, preferred_element_type=jnp.float32)
    scores = jnp.where(allowed, scores, masked_score)
    peak = jnp.max(scores, axis=-1, keepdims=True)
    raised = jnp.exp(scores - peak)
    probs = raised / jnp.sum(raised, axis=-1, keepdims=True)
    probs_low = probs.astype(jnp.bfloat16)
    attended = (
        jnp.einsum("kgqp,pkd->qkgd", probs_low, valued, preferred_element_type=jnp.float32)
        .astype(jnp.bfloat16)
        .reshape(rows, q_width)
    )
    middle = inputs + dot_plain(attended, out_full)

    inverse_two = lax.rsqrt(jnp.mean(middle * middle, axis=-1, keepdims=True) + epsilon)
    normed_two = (middle * inverse_two * gain_second).astype(jnp.bfloat16)
    logits = jnp.where(mask, dot_plain(normed_two, router_full), masked_score)
    lifted = jnp.where(mask, jnp.exp(logits - jnp.max(logits, axis=-1, keepdims=True)), 0.0)
    gates = lifted / jnp.sum(lifted, axis=-1, keepdims=True)
    table = jnp.stack([rank.T.astype(jnp.float32), gates.T], axis=1)
    part_out, grad_back, grad_gate, grad_up, grad_down = run_experts(
        table, normed_two, grad_low, w_gate[0], w_up[0], w_down[0]
    )
    grad_routed, dots = grad_back[:, :width], grad_back[:, width:]
    returned = from_experts(part_out).reshape(experts * places, width)

    gates_wide = jnp.where(onehot_wide, gates.T[:, None, :], 0.0)
    mixed = dot_left(gates_wide.astype(jnp.bfloat16).reshape(experts * places, rows), returned)
    layer_out = (middle + mixed).astype(jnp.bfloat16)
    weighted = dots[:, :experts] + dots[:, experts : 2 * experts]
    grad_picked = weighted - gates * jnp.sum(weighted, axis=-1, keepdims=True)
    grad_logits = grad_picked.astype(jnp.bfloat16)
    grad_router = dot_left(normed_two, grad_logits)
    grad_normed_two = dot_right(grad_logits, router_full) + grad_routed

    normed = middle * inverse_two
    scaled = grad_normed_two * gain_second
    grad_middle = grad_output + inverse_two * (
        scaled - normed * jnp.mean(scaled * normed, axis=-1, keepdims=True)
    )
    grad_gain_second = jnp.sum(grad_normed_two * normed, axis=0)
    grad_branch = grad_middle.astype(jnp.bfloat16)
    grad_out_full = dot_left(attended, grad_branch).astype(jnp.bfloat16)
    grad_heads = (
        dot_right(grad_branch, out_full).astype(jnp.bfloat16).reshape(rows, kv_all, group, HD)
    )
    grad_probs = jnp.einsum(
        "qkgd,pkd->kgqp", grad_heads, valued, preferred_element_type=jnp.float32
    )
    grad_scores = (
        probs * (grad_probs - jnp.sum(probs * grad_probs, axis=-1, keepdims=True))
    ).astype(jnp.bfloat16)
    grad_value_in = (
        jnp.einsum("kgqp,qkgd->pkd", probs_low, grad_heads, preferred_element_type=jnp.float32)
        .astype(jnp.bfloat16)
        .reshape(2 * rows, kv_width)
    )
    grad_query_rot = (
        jnp.einsum("kgqp,pkd->qkgd", grad_scores, keyed, preferred_element_type=jnp.float32)
        .astype(jnp.bfloat16)
        .astype(jnp.float32)
        .reshape(rows, heads_all, HD)
    )
    grad_key_rot = (
        jnp.einsum("kgqp,qkgd->pkd", grad_scores, grouped, preferred_element_type=jnp.float32)
        .astype(jnp.bfloat16)
        .astype(jnp.float32)
    )
    grad_query_in = (
        (rotate(grad_query_rot, cosine[rows:], -sine_table[rows:]) * scale)
        .astype(jnp.bfloat16)
        .reshape(rows, q_width)
    )
    grad_key_in = (
        rotate(grad_key_rot, cosine, -sine_table).astype(jnp.bfloat16).reshape(2 * rows, kv_width)
    )
    grad_query_full = dot_left(normed_own, grad_query_in).astype(jnp.bfloat16)
    grad_key_full = dot_left(normed_both, grad_key_in).astype(jnp.bfloat16)
    grad_value_full = dot_left(normed_both, grad_value_in).astype(jnp.bfloat16)
    grad_both = dot_right(grad_key_in, key_full) + dot_right(grad_value_in, value_full)
    grad_before = grad_both[:rows].astype(jnp.bfloat16)
    grad_own = grad_both[rows:] + dot_right(grad_query_in, query_full)
    normed_x = x_both * inverse_one
    grad_gain_first = jnp.sum(grad_own * normed_x[rows:], axis=0) + jnp.sum(
        grad_both[:rows] * normed_x[:rows], axis=0
    )
    small_grad = pack_small(grad_router, grad_gain_first, grad_gain_second, slots)
    small_grad = small_grad.astype(jnp.bfloat16)
    sum_out, sum_key, sum_query, sum_value, sum_small, grad_after = scatter_sums(
        [grad_out_full, grad_key_full, grad_query_full, grad_value_full, small_grad],
        (0, 0, 1, 1, 1),
        grad_before,
        1,
    )
    scaled_one = (grad_own + grad_after.astype(jnp.float32)) * gain_first
    grad_tokens = grad_middle + inverse_one[rows:] * (
        scaled_one
        - normed_x[rows:] * jnp.mean(scaled_one * normed_x[rows:], axis=-1, keepdims=True)
    )
    return (
        layer_out[None],
        grad_tokens[None],
        sum_small[0, experts : experts + height],
        sum_query,
        sum_key,
        sum_value,
        sum_out,
        sum_small[0, experts + height : experts + 2 * height],
        sum_small[:, :experts],
        grad_gate[None],
        grad_up[None],
        grad_down[None],
    )


def solution(mesh):
    rows = P("fsdp", "seq", None)
    matrix, cube = P("fsdp", None), P("fsdp", None, None)
    return jax.shard_map(
        on_device,
        mesh=mesh,
        in_specs=(
            rows,
            P("fsdp", "seq"),
            rows,
            rows,
            P("fsdp"),
            matrix,
            matrix,
            matrix,
            matrix,
            P("fsdp"),
            matrix,
            cube,
            cube,
            cube,
        ),
        out_specs=(
            rows,
            rows,
            P("fsdp"),
            matrix,
            matrix,
            matrix,
            matrix,
            P("fsdp"),
            matrix,
            cube,
            cube,
            cube,
        ),
        check_vma=False,
    )
```
